32 devices in a mesh: seq: 8 (over y, x, core), head: 4 (over z).
Axes of the slice: x: 2, y: 2, z: 4, core: 2. Of those that a mesh axis runs over, the one named last changes fastest.
Arguments:
- inputs: bfloat16 [4096, 4096], P('seq', 'head'), may hold values from -6 to 6
- grad_out: bfloat16 [4096, 4096], P('seq', 'head'), may hold values from -6 to 6
- write_proj: bfloat16 [4096, 128], P('seq'), may hold values from -0.1875 to 0.1875
- read_proj: bfloat16 [4096, 128], P('seq'), may hold values from -0.1875 to 0.1875
- log_decay: float32 [64, 4096], P('head', 'seq'), may hold values from -0.6 to 0
Outputs:
- grad_inputs: bfloat16 [4096, 4096], P('seq', 'head')
- grad_write: float32 [4096, 128], P('seq')
- grad_read: float32 [4096, 128], P('seq')
- grad_decay: float32 [64, 4096], P('head', 'seq')
The draws below stay inside these ranges and needn't reach their ends.
All inputs are finite; a program needn't handle non-finite values.
Results may differ from the reference program's by a relative error of at most 0.03.
Values sent between devices are 32-bit elements; how exact they have to be, the bound alone decides.
No kernel may reach another device: no remote copies, remote signals or barrier semaphores. Data moves between devices by JAX's collectives and lax.ppermute only.
A program may use at most 192 MiB of HBM per device.

```python
import jax
import jax.numpy as jnp
from jax import lax

HEAD_SUBSET = 64
P_SIZE = 64
N = 128
Q = 256
TOK_DEV = 512
TOKEN_COUNT = 4096


def draw_log_decay(key, part):
    key = jax.random.fold_in(key, 11)
    random_subkeys = jax.random.split(key, 7)
    fast_count = HEAD_SUBSET // 2
    perm_order = jax.random.permutation(random_subkeys[0], HEAD_SUBSET)
    is_fast = (perm_order < fast_count)[:, None]
    slow_rate = jnp.exp(jax.random.uniform(random_subkeys[1], (HEAD_SUBSET, 1), jnp.float32, jnp.log(0.05), jnp.log(0.4))) / TOKEN_COUNT
    fast_rate = jnp.exp(jax.random.uniform(random_subkeys[2], (HEAD_SUBSET, 1), jnp.float32, jnp.log(1.0 / 50.0), jnp.log(1.0 / 30.0)))
    baseline_rate = jnp.where(is_fast, fast_rate, slow_rate)
    jitter_level = jax.random.uniform(random_subkeys[3], (HEAD_SUBSET, TOKEN_COUNT), jnp.float32, 0.6, 1.4)
    block_count = TOKEN_COUNT // TOK_DEV
    per_device_factor = jnp.exp(jax.random.uniform(random_subkeys[4], (HEAD_SUBSET, block_count, 1), jnp.float32, jnp.log(0.5), jnp.log(2.0)))
    per_device_factor = jnp.broadcast_to(per_device_factor, (HEAD_SUBSET, block_count, TOK_DEV)).reshape(HEAD_SUBSET, TOKEN_COUNT)
    spike_location = jax.random.randint(random_subkeys[5], (HEAD_SUBSET, 2), 0, TOKEN_COUNT)
    spike_depth = jax.random.uniform(random_subkeys[6], (HEAD_SUBSET, 2), jnp.float32, 0.22, 0.5)
    token_positions = jnp.arange(TOKEN_COUNT)
    spike_events = jnp.sum(jnp.where(token_positions[None, None, :] == spike_location[:, :, None], spike_depth[:, :, None], 0.0), axis=1)
    return -(baseline_rate * jitter_level * per_device_factor) - spike_events


def steps_of(key, extent, cuts, smallest, largest):
    factor_of, own = 1.0, jax.random.fold_in(key, 6)
    for axis_at, parts in cuts:
        draws = jnp.exp(jax.random.uniform(jax.random.fold_in(own, axis_at), (parts,), jnp.float32, smallest / len(cuts), largest / len(cuts)))
        factor_of = factor_of * jnp.repeat(draws, extent[axis_at] // parts).reshape([-1 if axis == axis_at else 1 for axis in range(len(extent))])
    return factor_of


def normal_values(rng, dims, spread, most, pieces=(), dtype=jnp.bfloat16):
    values = jax.random.normal(rng, dims, jnp.float32) * spread
    if len(pieces) > 0:
        values = steps_of(rng, dims, pieces, -0.22, 0.18) * values
    return jnp.clip(values, min=-most, max=most).astype(dtype)


def setup_inputs(seed: int = 0) -> dict:
    key_list = jax.random.split(jax.random.key(seed), 6)
    inputs = normal_values(key_list[0], (TOKEN_COUNT, HEAD_SUBSET * P_SIZE), 1.0, 6.0, ((0, 8), (1, 4)))
    grad_out = normal_values(key_list[1], (TOKEN_COUNT, HEAD_SUBSET * P_SIZE), 1.0, 6.0, ((0, 8), (1, 4)))
    write_proj = normal_values(key_list[2], (TOKEN_COUNT, N), 0.03125, 0.1875, ((0, 8),))
    read_proj = normal_values(key_list[3], (TOKEN_COUNT, N), 0.03125, 0.1875, ((0, 8),))
    log_decay = draw_log_decay(jax.random.fold_in(key_list[5], 71), 0)
    return {"inputs": inputs, "grad_out": grad_out, "write_proj": write_proj, "read_proj": read_proj, "log_decay": log_decay}


def decay_parts(decay_blk):
    running = jnp.cumsum(decay_blk, axis=1)
    totals = running[:, -1]
    length = decay_blk.shape[1]
    causal = jnp.tril(jnp.ones((length, length), jnp.bool_))
    gap_matrix = jnp.where(causal[None], running[:, :, None] - running[:, None, :], -jnp.inf)
    decay_mat = jnp.exp(gap_matrix)
    decay_in = jnp.exp(running).T[:, :, None]
    decay_out = jnp.exp(totals[:, None] - running).T[:, :, None]
    return totals, decay_mat, decay_in, decay_out


def rounded_float(values):
    return lax.optimization_barrier(values.astype(jnp.bfloat16)).astype(jnp.float32)


def block_weights(read_blk, write_blk, decay_mat):
    scores = jnp.dot(read_blk, write_blk.T, preferred_element_type=jnp.float32)
    return rounded_float(scores[None] * decay_mat)


def reference(inputs, grad_out, write_proj, read_proj, log_decay):
    highest = lax.Precision.HIGHEST
    span_count = TOKEN_COUNT // Q
    inputs_c = inputs.reshape(span_count, Q, HEAD_SUBSET, P_SIZE)
    grads_c = grad_out.reshape(span_count, Q, HEAD_SUBSET, P_SIZE)
    write_c = write_proj.reshape(span_count, Q, N)
    read_c = read_proj.reshape(span_count, Q, N)
    decay_c = log_decay.reshape(HEAD_SUBSET, span_count, Q).transpose(1, 0, 2)

    def forward(state_now, blocks):
        inputs_blk, grads_blk, write_blk, read_blk, decay_blk = blocks
        totals, decay_mat, decay_in, decay_out = decay_parts(decay_blk)
        weights = block_weights(read_blk, write_blk, decay_mat)
        inputs_float = inputs_blk.astype(jnp.float32)
        grads_float = grads_blk.astype(jnp.float32)
        read_float = read_blk.astype(jnp.float32)
        write_float = write_blk.astype(jnp.float32)
        out_intra = jnp.einsum('hts,shp->thp', weights, inputs_float)
        grad_pairs = jnp.einsum('thp,shp->hts', grads_float, inputs_float)
        grad_scores = jnp.sum(decay_mat * grad_pairs, axis=0)
        input_weighted = rounded_float(inputs_float * decay_out)
        grad_weighted = rounded_float(grads_float * decay_in)
        state_part = jnp.einsum('qhp,qn->hpn', input_weighted, write_float)
        out_inter = jnp.einsum('tn,hpn->thp', read_float, state_now, precision=highest) * decay_in
        output_dot = jnp.sum(grads_float * (out_intra + out_inter), axis=2)
        read_grad = jnp.dot(grad_scores, write_float, precision=highest) + jnp.einsum('thp,hpn->tn', grad_weighted, state_now, precision=highest)
        write_intra = jnp.dot(grad_scores.T, read_float, precision=highest)
        state_next = jnp.exp(totals)[:, None, None] * state_now + state_part
        return state_next, (output_dot, read_grad, write_intra)

    def backward(grad_now, blocks):
        inputs_blk, grads_blk, write_blk, read_blk, decay_blk = blocks
        totals, decay_mat, decay_in, decay_out = decay_parts(decay_blk)
        weights = block_weights(read_blk, write_blk, decay_mat)
        inputs_float = inputs_blk.astype(jnp.float32)
        grads_float = grads_blk.astype(jnp.float32)
        read_float = read_blk.astype(jnp.float32)
        write_float = write_blk.astype(jnp.float32)
        grad_intra = jnp.einsum('hts,thp->shp', weights, grads_float)
        grad_inter = jnp.einsum('sn,hpn->shp', write_float, grad_now, precision=highest) * decay_out
        grad_full = grad_intra + grad_inter
        input_dot = jnp.sum(inputs_float * grad_full, axis=2)
        input_weighted = rounded_float(inputs_float * decay_out)
        grad_weighted = rounded_float(grads_float * decay_in)
        write_inter = jnp.einsum('shp,hpn->sn', input_weighted, grad_now, precision=highest)
        grad_part = jnp.einsum('qhp,qn->hpn', grad_weighted, read_float)
        grad_next = grad_part + jnp.exp(totals)[:, None, None] * grad_now
        return grad_next, (grad_full.astype(jnp.bfloat16), input_dot, write_inter)

    zero_state = jnp.zeros((HEAD_SUBSET, P_SIZE, N), jnp.float32)
    blocks = (inputs_c, grads_c, write_c, read_c, decay_c)
    final_state, (output_dot, read_grad, write_intra) = lax.scan(forward, zero_state, blocks)
    first_grad, (grad_blocks, input_dot, write_inter) = lax.scan(backward, zero_state, blocks, reverse=True)
    grad_inputs = grad_blocks.reshape(TOKEN_COUNT, HEAD_SUBSET * P_SIZE)
    grad_write = (write_intra + write_inter).reshape(TOKEN_COUNT, N)
    grad_read = read_grad.reshape(TOKEN_COUNT, N)
    change = (output_dot - input_dot).reshape(TOKEN_COUNT, HEAD_SUBSET)
    suffix = jnp.cumsum(change[::-1], axis=0)[::-1]
    grad_decay = (suffix * (P_SIZE * TOKEN_COUNT) ** -0.5).T
    return grad_inputs, grad_write, grad_read, grad_decay
```

```python
import jax
import jax.numpy as jnp
from jax import lax
from jax.experimental import pallas as pl
from jax.experimental.pallas import tpu as pltpu
from jax.sharding import PartitionSpec as P

Q = 256
GROUP = 8
F32 = jnp.float32
BF16 = jnp.bfloat16
VMEM_LIMIT = 48 * 1024 * 1024


def dot(a, b):
    return jnp.dot(a, b, preferred_element_type=F32)


def dot_t(a, b):
    return lax.dot_general(a, b, (((1,), (1,)), ((), ())), preferred_element_type=F32)


def iota(shape, dim):
    return lax.broadcasted_iota(jnp.int32, shape, dim)


def split_two(values):
    high = values.astype(BF16).astype(F32)
    return high, values - high


def split_three(values):
    high, rest = split_two(values)
    mid, low = split_two(rest)
    return high, mid, low


def times_ones(values, ones):
    high, mid, low = split_three(values)
    stacked = jnp.concatenate([high, mid, low, jnp.zeros_like(low)], axis=0).astype(BF16)
    out = dot(stacked, ones)
    return out[0:GROUP] + out[GROUP : 2 * GROUP] + out[2 * GROUP : 3 * GROUP]


def running_of(decay_blk):
    upto = (iota((Q, Q), 0) <= iota((Q, Q), 1)).astype(BF16)
    return times_ones(decay_blk, upto)


def spread_decays(running, head_size):
    lanes = GROUP * head_size
    total = running[:, Q - 1 : Q]
    parts = split_two(jnp.exp(running)) + split_two(jnp.exp(total - running))
    stacked = jnp.concatenate(parts, axis=0).T.astype(BF16)
    row = iota((4 * GROUP, lanes), 0)
    owner = row % GROUP == iota((4 * GROUP, lanes), 1) // head_size
    first = (owner & (row < 2 * GROUP)).astype(F32).astype(BF16)
    second = (owner & (row >= 2 * GROUP)).astype(F32).astype(BF16)
    return dot(stacked, first), dot(stacked, second)


def state_kernel(sel, x_ref, g_ref, w_ref, r_ref, ld_ref, pay_ref, iw_ref, gw_ref, part_ref, tot_ref):
    lanes = x_ref.shape[1]
    width = w_ref.shape[1]
    f_parts, g_parts, ends = [], [], []
    for b in range(2):
        rows = slice(b * Q, (b + 1) * Q)
        running = running_of(ld_ref[:, rows])
        decay_in, decay_out = spread_decays(running, lanes // GROUP)
        iw = (x_ref[rows, :].astype(F32) * decay_out).astype(BF16)
        gw = (g_ref[rows, :].astype(F32) * decay_in).astype(BF16)
        iw_ref[rows, :] = iw
        gw_ref[rows, :] = gw
        f_parts.append(dot(w_ref[rows, :].astype(F32).T.astype(BF16), iw))
        g_parts.append(dot(r_ref[rows, :].astype(F32).T.astype(BF16), gw))
        ends.append(decay_in[Q - 1 : Q, :])
    pay_ref[0:width, :] = ends[1] * f_parts[0] + f_parts[1]
    pay_ref[width : 2 * width, :] = ends[0] * g_parts[1] + g_parts[0]
    pay_ref[2 * width : 2 * width + 8, :] = jnp.broadcast_to(ends[0] * ends[1], (8, lanes))
    part_ref[0:width, :] = f_parts[0]
    part_ref[width : 2 * width, :] = g_parts[1]
    tot_ref[0:8, :] = jnp.broadcast_to(ends[0], (8, lanes))
    tot_ref[8:16, :] = jnp.broadcast_to(ends[1], (8, lanes))


def params():
    return pltpu.CompilerParams(vmem_limit_bytes=VMEM_LIMIT)


def states(which, inputs, grad_out, write_proj, read_proj, log_decay, head_size):
    rows, width = write_proj.shape
    lanes = GROUP * head_size
    wide = pl.BlockSpec((rows, lanes), lambda i, s: (0, s[0]))
    whole = lambda shape: pl.BlockSpec(shape, lambda i, s: (0, 0))
    outs = [
        ((2 * width + 8, lanes), F32),
        ((rows, lanes), BF16),
        ((rows, lanes), BF16),
        ((2 * width, lanes), F32),
        ((16, lanes), F32),
    ]
    return pl.pallas_call(
        state_kernel,
        grid_spec=pltpu.PrefetchScalarGridSpec(
            num_scalar_prefetch=1,
            grid=(1,),
            in_specs=[
                wide,
                wide,
                whole((rows, width)),
                whole((rows, width)),
                pl.BlockSpec((GROUP, rows), lambda i, s: (s[0], 0)),
            ],
            out_specs=[whole(s) for s, _ in outs],
        ),
        out_shape=[jax.ShapeDtypeStruct(s, t) for s, t in outs],
        compiler_params=params(),
        cost_estimate=pl.CostEstimate(flops=4 * rows * lanes * width, bytes_accessed=4 * rows * lanes * 2, transcendentals=0),
        name="states",
    )(which, inputs, grad_out, write_proj, read_proj, log_decay)


def chip_kernel(sel, mine_ref, got_ref, px_ref, py_ref):
    width = (mine_ref.shape[0] - 8) // 2
    lead = sel[0] == 0
    f_rows, b_rows, d_rows = slice(0, width), slice(width, 2 * width), slice(2 * width, 2 * width + 8)
    dec_mine, dec_got = mine_ref[d_rows, :], got_ref[d_rows, :]
    dec_first = jnp.where(lead, dec_mine, dec_got)[0:1]
    dec_second = jnp.where(lead, dec_got, dec_mine)[0:1]
    f_mine, f_got = mine_ref[f_rows, :], got_ref[f_rows, :]
    b_mine, b_got = mine_ref[b_rows, :], got_ref[b_rows, :]
    forward = dec_second * jnp.where(lead, f_mine, f_got) + jnp.where(lead, f_got, f_mine)
    backward = jnp.where(lead, b_mine, b_got) + dec_first * jnp.where(lead, b_got, b_mine)
    both = dec_mine * dec_got
    px_ref[f_rows, :] = jnp.where(sel[1] == 0, forward, backward)
    py_ref[f_rows, :] = jnp.where(sel[2] == 0, forward, backward)
    px_ref[width : width + 8, :] = both
    py_ref[width : width + 8, :] = both


def full(ref_or_shape):
    shape = ref_or_shape.shape
    return pl.BlockSpec(shape, lambda i, s: (0,) * len(shape))


def whole_call(kernel, name, sel, args, outs, flops=0):
    out_shape = [jax.ShapeDtypeStruct(s, t) for s, t in outs]
    moved = sum(a.size * a.dtype.itemsize for a in list(args) + out_shape)
    return pl.pallas_call(
        kernel,
        grid_spec=pltpu.PrefetchScalarGridSpec(
            num_scalar_prefetch=1,
            grid=(1,),
            in_specs=[full(a) for a in args],
            out_specs=[full(o) for o in out_shape],
        ),
        out_shape=out_shape,
        compiler_params=params(),
        cost_estimate=pl.CostEstimate(flops=flops, bytes_accessed=moved, transcendentals=0),
        name=name,
    )(sel, *args)


def carry_kernel(sel, rx_ref, ry_ref, rd_ref, mine_ref, got_ref, own_ref, other_ref):
    width = rx_ref.shape[0] - 8
    head, tail = slice(0, width), slice(width, width + 1)
    lead = sel[0] == 0
    low_x, low_y = sel[1] == 0, sel[2] == 0
    rx, ry, rd = rx_ref[head, :], ry_ref[head, :], rd_ref[head, :]
    dx, dy, dd = rx_ref[tail, :], ry_ref[tail, :], rd_ref[tail, :]
    far = jnp.where(low_x == low_y, rx + dx * (ry + dy * rd), rd + dd * ry)
    near = jnp.where(low_x == low_y, jnp.zeros_like(rx), rx)
    f_in = jnp.where(low_y, near, far)
    b_in = jnp.where(low_y, far, near)
    b_rows = slice(width, 2 * width)
    d_row = slice(2 * width, 2 * width + 1)
    f_next_mine = mine_ref[d_row, :] * f_in + mine_ref[head, :]
    b_next_mine = mine_ref[d_row, :] * b_in + mine_ref[b_rows, :]
    f_next_got = got_ref[d_row, :] * f_in + got_ref[head, :]
    b_next_got = got_ref[d_row, :] * b_in + got_ref[b_rows, :]
    own_ref[head, :] = jnp.where(lead, f_in, f_next_got)
    own_ref[b_rows, :] = jnp.where(lead, b_next_got, b_in)
    other_ref[head, :] = jnp.where(lead, f_next_mine, f_in)
    other_ref[b_rows, :] = jnp.where(lead, b_in, b_next_mine)


def block_states(car_ref, part_ref, tot_ref):
    width = car_ref.shape[0] // 2
    f_car, b_car = car_ref[0:width, :], car_ref[width : 2 * width, :]
    f_next = tot_ref[0:1, :] * f_car + part_ref[0:width, :]
    b_next = tot_ref[8:9, :] * b_car + part_ref[width : 2 * width, :]
    return (f_car, f_next), (b_next, b_car)


def late_kernel(sel, iw_ref, gw_ref, car_ref, part_ref, tot_ref, acc_ref, out_ref):
    rows = iw_ref.shape[0]
    state_in, grad_end = block_states(car_ref, part_ref, tot_ref)
    for b in range(2):
        at, late = slice(b * Q, (b + 1) * Q), slice(rows + b * Q, rows + (b + 1) * Q)
        out_ref[at, :] = acc_ref[at, :] + dot_t(gw_ref[at, :], state_in[b].astype(BF16))
        out_ref[late, :] = acc_ref[late, :] + dot_t(iw_ref[at, :], grad_end[b].astype(BF16))


def cut_kernel(sel, iw_ref, gw_ref, car_ref, part_ref, tot_ref, acc_ref, *rest):
    outs, total = rest[:-1], rest[-1]
    late_kernel(sel, iw_ref, gw_ref, car_ref, part_ref, tot_ref, acc_ref, total)
    rows = iw_ref.shape[0]
    step = rows // len(outs)
    for k, out in enumerate(outs):
        at = pl.multiple_of(jnp.bitwise_xor(sel[3], k) * step, step)
        out[0:step, :] = total[pl.ds(at, step), :]
        out[step : 2 * step, :] = total[pl.ds(rows + at, step), :]


def intra_kernel(x_ref, g_ref, w_ref, r_ref, ld_ref, gint_ref, dot_ref, acc_ref, gs_ref):
    group = pl.program_id(1)
    size = x_ref.shape[1] // GROUP
    half = Q // 2
    running = running_of(ld_ref[...])
    columns = jnp.concatenate([running] * (128 // GROUP), axis=0).T
    scores = dot_t(w_ref[...], r_ref[...])
    keep_top = iota((half, Q), 0) <= iota((half, Q), 1)
    keep_low = iota((half, half), 0) <= iota((half, half), 1)
    lane = iota((Q, 2 * size), 1)

    @pl.when(group == 0)
    def _():
        gs_ref[...] = jnp.zeros_like(gs_ref)

    sums_top, sums_low = [], []
    gs_top = jnp.zeros((half, Q), F32)
    gs_low = jnp.zeros((half, half), F32)
    for pair in range(GROUP // 2):
        at = slice(pair * 2 * size, (pair + 1) * 2 * size)
        x_pair, g_pair = x_ref[:, at], g_ref[:, at]
        top, low = None, None
        for k in range(2):
            h = 2 * pair + k
            mine = (lane < size) if k == 0 else (lane >= size)
            g_own = jnp.where(mine, g_pair, jnp.zeros_like(g_pair))
            row = running[h : h + 1, :]
            col = columns[:, h : h + 1]
            decay_top = jnp.exp(jnp.where(keep_top, row - col[0:half], -jnp.inf))
            decay_low = jnp.exp(jnp.where(keep_low, row[:, half:] - col[half:], -jnp.inf))
            pairs_top = dot_t(x_pair[0:half], g_own)
            pairs_low = dot_t(x_pair[half:], g_own[half:])
            weights_top = scores[0:half] * decay_top
            weights_low = scores[half:, half:] * decay_low
            sums_top.append(jnp.sum(weights_top * pairs_top, axis=0, keepdims=True))
            sums_low.append(jnp.sum(weights_low * pairs_low, axis=0, keepdims=True))
            gs_top = gs_top + decay_top * pairs_top
            gs_low = gs_low + decay_low * pairs_low
            part_top = dot(weights_top.astype(BF16), g_own)
            part_low = dot(weights_low.astype(BF16), g_own[half:])
            top = part_top if top is None else top + part_top
            low = part_low if low is None else low + part_low
        gint_ref[0:half, at] = top
        gint_ref[half:, at] = low
    gs_ref[0:half, :] += gs_top
    gs_ref[half:, half:] += gs_low
    dot_ref[...] = jnp.concatenate(sums_top, axis=0)
    dot_ref[:, half:] += jnp.concatenate(sums_low, axis=0)

    @pl.when(group == pl.num_programs(1) - 1)
    def _():
        grad_scores = gs_ref[...]
        acc_ref[0] = dot(grad_scores.T.astype(BF16), w_ref[...])
        acc_ref[1] = dot(grad_scores.astype(BF16), r_ref[...])


def intra(inputs, grad_out, write_proj, read_proj, log_decay, head_size):
    rows, width = write_proj.shape
    heads = log_decay.shape[0]
    lanes = GROUP * head_size
    spans, groups = rows // Q, heads // GROUP
    wide = pl.BlockSpec((Q, lanes), lambda b, j: (b, j))
    narrow = pl.BlockSpec((Q, width), lambda b, j: (b, 0))
    decays = pl.BlockSpec((GROUP, Q), lambda b, j: (j, b))
    return pl.pallas_call(
        intra_kernel,
        grid=(spans, groups),
        in_specs=[wide, wide, narrow, narrow, decays],
        out_specs=[wide, decays, pl.BlockSpec((2, Q, width), lambda b, j: (0, b, 0))],
        out_shape=[
            jax.ShapeDtypeStruct((rows, heads * head_size), F32),
            jax.ShapeDtypeStruct((heads, rows), F32),
            jax.ShapeDtypeStruct((2, rows, width), F32),
        ],
        scratch_shapes=[pltpu.VMEM((Q, Q), F32)],
        compiler_params=params(),
        cost_estimate=pl.CostEstimate(
            flops=16 * rows * Q * heads * head_size, bytes_accessed=8 * rows * heads * head_size, transcendentals=rows * Q * heads
        ),
        name="intra",
    )(inputs, grad_out, write_proj, read_proj, log_decay)


def grads_kernel(scale, count, sel, x_ref, g_ref, w_ref, r_ref, ld_ref, gint_ref, dot_ref, *rest):
    refs, (gi_ref, gd_ref) = rest[: 4 * count], rest[4 * count :]
    j = pl.program_id(0)
    lanes = x_ref.shape[1]
    width = w_ref.shape[1]
    size = lanes // GROUP

    def body(car_ref, part_ref, tot_ref, pay_ref):
        state_in, grad_end = block_states(car_ref, part_ref, tot_ref)
        last = pay_ref[2 * width : 2 * width + 1, :] * car_ref[0:width, :] + pay_ref[0:width, :]
        after = (state_in[1], last)
        owner = (iota((16, lanes), 0) == iota((16, lanes), 1) // size).astype(F32).astype(BF16)
        onward = (iota((Q, Q), 0) >= iota((Q, Q), 1)).astype(F32).astype(BF16)
        for b in range(2):
            at = slice(b * Q, (b + 1) * Q)
            running = running_of(ld_ref[:, at])
            decay_in, decay_out = spread_decays(running, size)
            g, x = g_ref[at, :].astype(F32), x_ref[at, :].astype(F32)
            out_inter = dot(r_ref[at, :], state_in[b].astype(BF16)) * decay_in
            grad_full = gint_ref[at, :] + dot(w_ref[at, :], grad_end[b].astype(BF16)) * decay_out
            gi_ref[at, :] = grad_full.astype(BF16)
            high, low = split_two(g * out_inter - x * grad_full)
            change = dot_t(owner, high.astype(BF16)) + dot_t(owner, low.astype(BF16))
            change = change[0:GROUP] + dot_ref[:, at]
            cross = jnp.sum(after[b] * grad_end[b], axis=0, keepdims=True)
            cross = jnp.broadcast_to(cross, (Q, lanes))
            c1, c2, c3 = split_three(cross)
            crossing = dot_t(owner, c1.astype(BF16)) + dot_t(owner, c2.astype(BF16)) + dot_t(owner, c3.astype(BF16))
            gd_ref[:, at] = (times_ones(change, onward) + crossing[0:GROUP]) * scale

    if count == 1:
        body(*refs)
    else:
        for k in range(count):
            pl.when(j == sel[4 + k])(lambda k=k: body(*refs[4 * k : 4 * k + 4]))


def grads(sel, inputs, grad_out, write_proj, read_proj, log_decay, gint, dots, per_group, scale, head_size):
    rows, width = write_proj.shape
    heads = log_decay.shape[0]
    lanes = GROUP * head_size
    wide = pl.BlockSpec((rows, lanes), lambda j, s: (0, j))
    decays = pl.BlockSpec((GROUP, rows), lambda j, s: (j, 0))
    flat = [a for group in per_group for a in group]

    def kernel(*refs):
        grads_kernel(scale, len(per_group), *refs)

    return pl.pallas_call(
        kernel,
        grid_spec=pltpu.PrefetchScalarGridSpec(
            num_scalar_prefetch=1,
            grid=(heads // GROUP,),
            in_specs=[wide, wide, full(write_proj), full(read_proj), decays, wide, decays] + [full(a) for a in flat],
            out_specs=[wide, decays],
        ),
        out_shape=[jax.ShapeDtypeStruct((rows, heads * head_size), BF16), jax.ShapeDtypeStruct((heads, rows), F32)],
        compiler_params=params(),
        cost_estimate=pl.CostEstimate(
            flops=8 * rows * width * heads * head_size, bytes_accessed=12 * rows * heads * head_size, transcendentals=0
        ),
        name="grads",
    )(sel, inputs, grad_out, write_proj, read_proj, log_decay, gint, dots, *flat)


def join_kernel(sel, *refs):
    parts, (read_ref, write_ref) = refs[:-2], refs[-2:]
    step = parts[0].shape[0] // 2
    for k, part in enumerate(parts):
        at = pl.multiple_of(jnp.bitwise_xor(sel[3], k) * step, step)
        read_ref[pl.ds(at, step), :] = part[0:step, :]
        write_ref[pl.ds(at, step), :] = part[step : 2 * step, :]


def swap(values, axis, mask):
    count = lax.axis_size(axis)
    return lax.ppermute(values, axis, [(i, i ^ mask) for i in range(count)])


def scan_over(pay, width, reverse):
    count = lax.axis_size("seq")
    place = lax.axis_index("seq")
    ahead = count - 1 - place if reverse else place
    part = pay[width : 2 * width] if reverse else pay[0:width]
    dec = pay[2 * width : 2 * width + 1]

    def shifted(values, hop):
        route = [(i, i - hop) if reverse else (i, i + hop) for i in range(count)]
        return lax.ppermute(values, "seq", [(a, b) for a, b in route if 0 <= b < count])

    hop = 1
    while hop < count:
        got_part, got_dec = shifted(part, hop), shifted(dec, hop)
        use = ahead >= hop
        part = jnp.where(use, part + dec * got_part, part)
        dec = jnp.where(use, dec * got_dec, dec)
        hop *= 2
    return shifted(part, 1)


def local(inputs, grad_out, write_proj, read_proj, log_decay):
    head_count, rows = log_decay.shape
    head_size = inputs.shape[1] // head_count
    width = write_proj.shape[1]
    lanes = GROUP * head_size
    groups = head_count // GROUP
    seq_count, head_parts = lax.axis_size("seq"), lax.axis_size("head")
    scale = (head_size * rows * seq_count) ** (-0.5)
    place = lax.axis_index("seq").astype(jnp.int32)
    mine = place % 2
    fast = seq_count == 8 and groups == 2
    order = [mine, 1 - mine] if fast else [jnp.int32(k) for k in range(groups)]
    sel = jnp.stack(
        [mine, (place // 2) % 2, (place // 4) % 2, lax.axis_index("head").astype(jnp.int32)] + order
    )
    data = (inputs, grad_out, write_proj, read_proj, log_decay)
    if fast:
        other_state = states(order[1][None], *data, head_size)
        got = swap(other_state[0], "seq", 1)
        mine_state = states(order[0][None], *data, head_size)
        per_state = [mine_state, other_state]
        px, py = whole_call(
            chip_kernel, "chip", sel, (mine_state[0], got), [((width + 8, lanes), F32)] * 2
        )
        rx, ry, rd = swap(px, "seq", 2), swap(py, "seq", 4), swap(py, "seq", 6)
    else:
        per_state = [states(k[None], *data, head_size) for k in order]
    gint, dots, early = intra(*data, head_size)
    if fast:
        own, send = whole_call(
            carry_kernel, "carry", sel, (rx, ry, rd, mine_state[0], got), [((2 * width, lanes), F32)] * 2
        )
        carried = [own, swap(send, "seq", 1)]
    else:
        carried = [
            jnp.concatenate([scan_over(s[0], width, False), scan_over(s[0], width, True)]) for s in per_state
        ]
    acc = early.reshape(2 * rows, width)
    late_flops = 8 * rows * lanes * width
    for k in range(groups):
        pay, iw, gw, part, tot = per_state[k]
        args = (iw, gw, carried[k], part, tot, acc)
        if k < groups - 1 or head_parts != 4:
            (acc,) = whole_call(late_kernel, "late", sel, args, [((2 * rows, width), F32)], late_flops)
        else:
            cut = rows // head_parts
            outs = [jax.ShapeDtypeStruct((2 * cut, width), F32)] * head_parts
            pieces = pl.pallas_call(
                cut_kernel,
                grid_spec=pltpu.PrefetchScalarGridSpec(
                    num_scalar_prefetch=1,
                    grid=(1,),
                    in_specs=[full(a) for a in args],
                    out_specs=[full(o) for o in outs],
                    scratch_shapes=[pltpu.VMEM((2 * rows, width), F32)],
                ),
                out_shape=outs,
                compiler_params=params(),
                cost_estimate=pl.CostEstimate(flops=late_flops, bytes_accessed=4 * rows * lanes * 2, transcendentals=0),
                name="late_cut",
            )(sel, *args)
    per_group = [(carried[k], per_state[k][3], per_state[k][4], per_state[k][0]) for k in range(groups)]
    if head_parts == 4:
        got = [swap(pieces[k], "head", k) for k in (1, 2, 3)]
        grad_inputs, grad_decay = grads(sel, *data, gint, dots, per_group, scale, head_size)
        total = pieces[0] + got[0] + got[1] + got[2]
        got = [swap(total, "head", k) for k in (1, 2, 3)]
        grad_read, grad_write = whole_call(
            join_kernel, "join", sel, (total, *got), [((rows, width), F32)] * 2
        )
    else:
        grad_inputs, grad_decay = grads(sel, *data, gint, dots, per_group, scale, head_size)
        summed = lax.psum(acc, "head")
        grad_read, grad_write = summed[:rows], summed[rows:]
    return grad_inputs, grad_write, grad_read, grad_decay


def solution(mesh):
    in_specs = (
        P("seq", "head"),
        P("seq", "head"),
        P("seq", None),
        P("seq", None),
        P("head", "seq"),
    )
    out_specs = (P("seq", "head"), P("seq", None), P("seq", None), P("head", "seq"))
    return jax.shard_map(local, mesh=mesh, in_specs=in_specs, out_specs=out_specs, check_vma=False)
```

```python
import functools

import jax
import jax.numpy as jnp
from jax import lax
from jax.experimental import pallas as pl
from jax.experimental.pallas import tpu as pltpu
from jax.sharding import PartitionSpec as P

Q = 256
GROUP = 8
F32 = jnp.float32
BF16 = jnp.bfloat16
FREE = pl.CostEstimate(flops=1000, bytes_accessed=1000, transcendentals=0)


def dot(a, b):
    return jnp.dot(a, b, preferred_element_type=F32)


def dot_t(a, b):
    return lax.dot_general(a, b, (((1,), (1,)), ((), ())), preferred_element_type=F32)


def iota(shape, dim):
    return lax.broadcasted_iota(jnp.int32, shape, dim)


def split_two(values):
    high = values.astype(BF16).astype(F32)
    return high, values - high


def split_three(values):
    high, rest = split_two(values)
    mid, low = split_two(rest)
    return high, mid, low


def times_ones(values, ones):
    high, mid, low = split_three(values)
    stacked = jnp.concatenate([high, mid, low, jnp.zeros_like(low)], axis=0).astype(BF16)
    out = dot(stacked, ones)
    return out[0:GROUP] + out[GROUP : 2 * GROUP] + out[2 * GROUP : 3 * GROUP]


def running_of(decay_blk):
    upto = (iota((Q, Q), 0) <= iota((Q, Q), 1)).astype(BF16)
    return times_ones(decay_blk, upto)


def spread_decays(running, head_size):
    lanes = GROUP * head_size
    total = running[:, Q - 1 : Q]
    parts = split_two(jnp.exp(running)) + split_two(jnp.exp(total - running))
    stacked = jnp.concatenate(parts, axis=0).T.astype(BF16)
    row = iota((4 * GROUP, lanes), 0)
    owner = row % GROUP == iota((4 * GROUP, lanes), 1) // head_size
    first = (owner & (row < 2 * GROUP)).astype(F32).astype(BF16)
    second = (owner & (row >= 2 * GROUP)).astype(F32).astype(BF16)
    return dot(stacked, first), dot(stacked, second)


def state_kernel(sel, x_hbm, g_hbm, w_hbm, r_hbm, ld_hbm, pay_ref, x_ref, g_ref, w_ref, r_ref, ld_ref, sems):
    rows, lanes = x_ref.shape
    width = w_ref.shape[1]
    here = pl.ds(pl.multiple_of(sel[0] * lanes, lanes), lanes)
    group = pl.ds(pl.multiple_of(sel[0] * GROUP, GROUP), GROUP)
    small = [
        pltpu.make_async_copy(src, dst, sems.at[k])
        for k, (src, dst) in enumerate(((ld_hbm.at[group, :], ld_ref), (w_hbm, w_ref), (r_hbm, r_ref)))
    ]
    large = []
    for b in range(2):
        at = pl.ds(b * Q, Q)
        large.append(pltpu.make_async_copy(x_hbm.at[at, here], x_ref.at[at, :], sems.at[3 + 2 * b]))
        large.append(pltpu.make_async_copy(g_hbm.at[at, here], g_ref.at[at, :], sems.at[4 + 2 * b]))
    for move in small + large:
        move.start()
    small[0].wait()
    decays = [spread_decays(running_of(ld_ref[:, b * Q : (b + 1) * Q]), lanes // GROUP) for b in range(2)]
    small[1].wait()
    small[2].wait()
    f_parts, g_parts, ends = [], [], []
    for b in range(2):
        at = slice(b * Q, (b + 1) * Q)
        decay_in, decay_out = decays[b]
        large[2 * b].wait()
        iw = (x_ref[at, :].astype(F32) * decay_out).astype(BF16)
        f_parts.append(dot(w_ref[at, :].astype(F32).T.astype(BF16), iw))
        large[2 * b + 1].wait()
        gw = (g_ref[at, :].astype(F32) * decay_in).astype(BF16)
        g_parts.append(dot(r_ref[at, :].astype(F32).T.astype(BF16), gw))
        ends.append(decay_in[Q - 1 : Q, :])
    pay_ref[0:width, :] = ends[1] * f_parts[0] + f_parts[1]
    pay_ref[width : 2 * width, :] = ends[0] * g_parts[1] + g_parts[0]
    pay_ref[2 * width : 2 * width + 8, :] = jnp.broadcast_to(ends[0] * ends[1], (8, lanes))


def params(limit=32):
    return pltpu.CompilerParams(vmem_limit_bytes=limit * 1024 * 1024)


def shape_of(shape, dtype=F32):
    return jax.ShapeDtypeStruct(shape, dtype)


def stored(shape, dtype=F32):
    return pltpu.HBM(shape, dtype)


def far_off(values):
    return pltpu.with_memory_space_constraint(values, pltpu.HBM)


def states(which, inputs, grad_out, write_proj, read_proj, log_decay, head_size):
    rows, width = write_proj.shape
    lanes = GROUP * head_size
    outs = [shape_of((2 * width + 8, lanes))]
    return pl.pallas_call(
        state_kernel,
        grid_spec=pltpu.PrefetchScalarGridSpec(
            num_scalar_prefetch=1,
            grid=(1,),
            in_specs=[pl.BlockSpec(memory_space=pltpu.HBM)] * 5,
            out_specs=[full(o) for o in outs],
            scratch_shapes=[
                pltpu.VMEM((rows, lanes), BF16),
                pltpu.VMEM((rows, lanes), BF16),
                pltpu.VMEM((rows, width), BF16),
                pltpu.VMEM((rows, width), BF16),
                pltpu.VMEM((GROUP, rows), F32),
                pltpu.SemaphoreType.DMA((7,)),
            ],
        ),
        out_shape=outs,
        compiler_params=params(),
        cost_estimate=FREE,
        name="states",
    )(which, *map(far_off, (inputs, grad_out, write_proj, read_proj, log_decay)))[0]


def chip_kernel(sel, mine_ref, got_ref, px_ref, py_ref):
    width = (mine_ref.shape[0] - 8) // 2
    lead = sel[2] == 0
    f_rows, b_rows, d_rows = slice(0, width), slice(width, 2 * width), slice(2 * width, 2 * width + 8)
    dec_mine, dec_got = mine_ref[d_rows, :], got_ref[d_rows, :]
    dec_first = jnp.where(lead, dec_mine, dec_got)[0:1]
    dec_second = jnp.where(lead, dec_got, dec_mine)[0:1]
    f_mine, f_got = mine_ref[f_rows, :], got_ref[f_rows, :]
    b_mine, b_got = mine_ref[b_rows, :], got_ref[b_rows, :]
    forward = dec_second * jnp.where(lead, f_mine, f_got) + jnp.where(lead, f_got, f_mine)
    backward = jnp.where(lead, b_mine, b_got) + dec_first * jnp.where(lead, b_got, b_mine)
    both = dec_mine * dec_got
    px_ref[f_rows, :] = jnp.where(sel[3] == 0, forward, backward)
    py_ref[f_rows, :] = jnp.where(sel[4] == 0, forward, backward)
    px_ref[width : width + 8, :] = both
    py_ref[width : width + 8, :] = both


def full(ref_or_shape):
    shape = ref_or_shape.shape
    return pl.BlockSpec(shape, lambda i, s: (0,) * len(shape))


ANYWHERE = pl.BlockSpec(memory_space=pl.ANY)


def call(kernel, name, sel, args, outs, in_specs=None, scratch=(), out_specs=None, after=()):
    skip, count = len(args), len(after)

    def body(s, *refs):
        kernel(s, *refs[:skip], *refs[skip + count :])

    return pl.pallas_call(
        body,
        grid_spec=pltpu.PrefetchScalarGridSpec(
            num_scalar_prefetch=1,
            grid=(1,),
            in_specs=(in_specs or [full(a) for a in args]) + [ANYWHERE] * count,
            out_specs=out_specs or [full(o) for o in outs],
            scratch_shapes=list(scratch),
        ),
        out_shape=list(outs),
        compiler_params=params(),
        cost_estimate=FREE,
        name=name,
    )(sel, *args, *after)


def carry_kernel(way, sel, *refs):
    *got_refs, mine_ref, got_ref, mine_dec, got_dec, own_ref, send_ref = refs
    width = mine_ref.shape[0]
    head, tail = slice(0, width), slice(width, width + 1)
    same = sel[3] == sel[4]
    rx = got_refs[0][head, :]
    if len(got_refs) == 1:
        entering = jnp.where(same, jnp.zeros_like(rx), rx)
    else:
        ry, rd = got_refs[1][head, :], got_refs[2][head, :]
        dx, dy, dd = (ref[tail, :] for ref in got_refs)
        entering = jnp.where(same, rx + dx * (ry + dy * rd), rd + dd * ry)
    first = sel[way] == sel[2]
    own_ref[...] = jnp.where(first, entering, got_dec[0:1, :] * entering + got_ref[...])
    send_ref[...] = jnp.where(first, mine_dec[0:1, :] * entering + mine_ref[...], entering)


def carry(way, sel, arrived, mine, got, name, after=()):
    width, lanes = arrived[0].shape[0] - 8, arrived[0].shape[1]
    part = pl.BlockSpec((width, lanes), lambda i, s: (s[way], 0))
    dec = pl.BlockSpec((8, lanes), lambda i, s: (2 * width // 8, 0))
    return call(
        functools.partial(carry_kernel, way),
        name,
        sel,
        [*arrived, mine, got, mine, got],
        [shape_of((width, lanes))] * 2,
        in_specs=[full(a) for a in arrived] + [part, part, dec, dec],
        after=after,
    )


def late_kernel(way, sel, wg_ref, car_ref, part_ref, tot_ref, acc_ref, out_ref):
    car = car_ref[...]
    onward = tot_ref[0:1, :] * car + part_ref[...]
    forward = sel[way] == 0
    for b in range(2):
        at = slice(b * Q, (b + 1) * Q)
        held = jnp.where(forward, onward if b else car, car if b else onward).astype(BF16)
        out_ref[at, :] = acc_ref[0, at, :] + dot_t(wg_ref[0, at, :], held)


def cut_kernel(way, sel, wg_ref, car_ref, part_ref, tot_ref, acc_ref, keep_ref, send_ref, total):
    late_kernel(way, sel, wg_ref, car_ref, part_ref, tot_ref, acc_ref, total)
    step = keep_ref.shape[0]
    odd = sel[5] % 2
    keep_ref[...] = total[pl.ds(pl.multiple_of(odd * step, step), step), :]
    send_ref[...] = total[pl.ds(pl.multiple_of((1 - odd) * step, step), step), :]


def late(way, sel, k, local_parts, carried, acc, cut, name):
    wg, part, tot = local_parts
    rows = wg.shape[1]
    width, lanes = carried.shape
    both = acc.shape[0] == 2
    outs = [shape_of((rows // 2, width))] * 2 if cut else [shape_of((rows, width))]
    return call(
        functools.partial(cut_kernel if cut else late_kernel, way),
        name,
        sel,
        [wg, carried, part, tot, acc],
        outs,
        in_specs=[
            pl.BlockSpec((1, rows, lanes), lambda i, s: (s[way], 0, s[6 + k])),
            full(carried),
            pl.BlockSpec((width, lanes), lambda i, s: (s[way], s[6 + k])),
            pl.BlockSpec((8, lanes), lambda i, s: (s[way], s[6 + k])),
            pl.BlockSpec((1, rows, width), lambda i, s: (s[way] if both else 0, 0, 0)),
        ],
        scratch=[pltpu.VMEM((rows, width), F32)] if cut else [],
    )


def decay_blocks(running):
    half = Q // 2
    columns = jnp.concatenate([running] * (128 // GROUP), axis=0).T
    keep_top = iota((half, Q), 0) <= iota((half, Q), 1)
    keep_low = iota((half, half), 0) <= iota((half, half), 1)

    def of(h):
        row, col = running[h : h + 1, :], columns[:, h : h + 1]
        top = jnp.exp(jnp.where(keep_top, row - col[0:half], -jnp.inf))
        low = jnp.exp(jnp.where(keep_low, row[:, half:] - col[half:], -jnp.inf))
        return top, low

    return of


def pair_products(x_pair, g_pair):
    half = Q // 2
    lane = iota(x_pair.shape, 1)
    none = jnp.zeros_like(x_pair)
    left = lane < x_pair.shape[1] // 2
    first, second = jnp.where(left, x_pair, none), jnp.where(left, none, x_pair)
    top = dot_t(jnp.concatenate([first[0:half], second[0:half]], axis=0), g_pair)
    low = dot_t(jnp.concatenate([first[half:], second[half:]], axis=0), g_pair[half:])
    return (top[0:half], low[0:half]), (top[half:], low[half:])


def scores_kernel(x_ref, g_ref, w_ref, r_ref, ld_ref, *rest):
    acc_ref, wg_ref, part_ref, tot_ref, gs_ref = rest[-5:]
    group = pl.program_id(1)
    size = x_ref.shape[1] // GROUP
    half = Q // 2
    running = running_of(ld_ref[...])
    decay_in, decay_out = spread_decays(running, size)
    iw = (x_ref[...].astype(F32) * decay_out).astype(BF16)
    gw = (g_ref[...].astype(F32) * decay_in).astype(BF16)
    wg_ref[0] = gw
    wg_ref[1] = iw
    tot_ref[...] = jnp.broadcast_to(decay_in[Q - 1 : Q, :], tot_ref.shape)

    @pl.when(pl.program_id(0) == 0)
    def _():
        part_ref[...] = dot(w_ref[...].astype(F32).T.astype(BF16), iw)

    @pl.when(pl.program_id(0) == 1)
    def _():
        part_ref[...] = dot(r_ref[...].astype(F32).T.astype(BF16), gw)

    decays = decay_blocks(running)
    gs_top = jnp.zeros((half, Q), F32)
    gs_low = jnp.zeros((half, half), F32)
    for pair in range(GROUP // 2):
        at = slice(pair * 2 * size, (pair + 1) * 2 * size)
        for k, (pairs_top, pairs_low) in enumerate(pair_products(x_ref[:, at], g_ref[:, at])):
            decay_top, decay_low = decays(2 * pair + k)
            gs_top = gs_top + decay_top * pairs_top
            gs_low = gs_low + decay_low * pairs_low

    @pl.when(group == 0)
    def _():
        gs_ref[0:half, :] = gs_top
        gs_ref[half:, 0:half] = jnp.zeros_like(gs_low)
        gs_ref[half:, half:] = gs_low

    @pl.when(group > 0)
    def _():
        gs_ref[0:half, :] += gs_top
        gs_ref[half:, half:] += gs_low

    @pl.when(group == pl.num_programs(1) - 1)
    def _():
        grad_scores = gs_ref[...]
        acc_ref[0] = dot(grad_scores.T.astype(BF16), w_ref[...])
        acc_ref[1] = dot(grad_scores.astype(BF16), r_ref[...])


def scores(inputs, grad_out, write_proj, read_proj, log_decay, head_size, after):
    rows, width = write_proj.shape
    heads = log_decay.shape[0]
    lanes = GROUP * head_size
    wide = pl.BlockSpec((Q, lanes), lambda b, j: (b, j))
    narrow = pl.BlockSpec((Q, width), lambda b, j: (b, 0))
    return pl.pallas_call(
        scores_kernel,
        grid=(rows // Q, heads // GROUP),
        in_specs=[wide, wide, narrow, narrow, pl.BlockSpec((GROUP, Q), lambda b, j: (j, b))] + [ANYWHERE] * len(after),
        out_specs=[
            pl.BlockSpec((2, Q, width), lambda b, j: (0, b, 0)),
            pl.BlockSpec((2, Q, lanes), lambda b, j: (0, b, j)),
            pl.BlockSpec((width, lanes), lambda b, j: (b, j)),
            pl.BlockSpec((8, lanes), lambda b, j: (b, j)),
        ],
        out_shape=[
            shape_of((2, rows, width)),
            stored((2, rows, heads * head_size), BF16),
            stored((2 * width, heads * head_size)),
            stored((16, heads * head_size)),
        ],
        scratch_shapes=[pltpu.VMEM((Q, Q), F32)],
        compiler_params=params(),
        cost_estimate=FREE,
        name="scores",
    )(inputs, grad_out, write_proj, read_proj, log_decay, *after)


def grads_kernel(scale, sel, x_ref, g_ref, gw_ref, w_ref, r_ref, ld_ref, part_ref, tot_ref, near_ref, far_ref, pay_ref, *rest):
    gi_ref, gd_ref = rest[-2:]
    lanes = x_ref.shape[1]
    width = w_ref.shape[1]
    size = lanes // GROUP
    half = Q // 2
    near_forward = sel[0] == 0
    f_car = jnp.where(near_forward, near_ref[...], far_ref[...])
    b_car = jnp.where(near_forward, far_ref[...], near_ref[...])
    f_next = tot_ref[0:1, :] * f_car + part_ref[0:width, :]
    b_next = tot_ref[8:9, :] * b_car + part_ref[width : 2 * width, :]
    state_in, grad_end = (f_car, f_next), (b_next, b_car)
    last = pay_ref[2 * width : 2 * width + 1, :] * f_car + pay_ref[0:width, :]
    after = (f_next, last)
    owner = iota((16, lanes), 0) == iota((16, lanes), 1) // size
    ones = owner.astype(F32).astype(BF16)
    onward = (iota((Q, Q), 0) >= iota((Q, Q), 1)).astype(F32).astype(BF16)
    left = iota((Q, 2 * size), 1) < size
    for b in range(2):
        at = slice(b * Q, (b + 1) * Q)
        running = running_of(ld_ref[:, at])
        decays = decay_blocks(running)
        decay_out = spread_decays(running, size)[1]
        products = dot_t(w_ref[at, :], r_ref[at, :])
        sums_top, sums_low, changes = [], [], None
        for pair in range(GROUP // 2):
            here = slice(pair * 2 * size, (pair + 1) * 2 * size)
            x_pair, g_pair = x_ref[at, here], g_ref[at, here]
            none = jnp.zeros_like(g_pair)
            top = low = None
            for k, (pairs_top, pairs_low) in enumerate(pair_products(x_pair, g_pair)):
                decay_top, decay_low = decays(2 * pair + k)
                weights_top = products[0:half] * decay_top
                weights_low = products[half:, half:] * decay_low
                sums_top.append(jnp.sum(weights_top * pairs_top, axis=0, keepdims=True))
                sums_low.append(jnp.sum(weights_low * pairs_low, axis=0, keepdims=True))
                g_own = jnp.where(left, g_pair, none) if k == 0 else jnp.where(left, none, g_pair)
                part_top = dot(weights_top.astype(BF16), g_own)
                part_low = dot(weights_low.astype(BF16), g_own[half:])
                top = part_top if top is None else top + part_top
                low = part_low if low is None else low + part_low
            out_inter = dot(r_ref[at, :], state_in[b][:, here].astype(BF16))
            grad_inter = dot(w_ref[at, :], grad_end[b][:, here].astype(BF16)) * decay_out[:, here]
            grad_full = jnp.concatenate([top, low], axis=0) + grad_inter
            gi_ref[at, here] = grad_full.astype(BF16)
            high, low = split_two(gw_ref[0, at, here].astype(F32) * out_inter - x_pair.astype(F32) * grad_full)
            change = dot_t(ones[:, here], high.astype(BF16)) + dot_t(ones[:, here], low.astype(BF16))
            changes = change if changes is None else changes + change
        early, late_half = jnp.concatenate(sums_top, axis=0), jnp.concatenate(sums_low, axis=0)
        within = changes[0:GROUP] + early + jnp.concatenate([jnp.zeros_like(late_half), late_half], axis=1)
        cross = jnp.sum(after[b] * grad_end[b], axis=0, keepdims=True)
        crossing = jnp.sum(jnp.where(owner[0:GROUP], cross, 0.0), axis=1, keepdims=True)
        gd_ref[:, at] = (times_ones(within, onward) + crossing) * scale


def grads(sel, k, data, local_parts, carried, scale, head_size, held=(), after=()):
    inputs, grad_out, write_proj, read_proj, log_decay = data
    wg, part, tot = local_parts
    rows, width = write_proj.shape
    heads = log_decay.shape[0]
    lanes = GROUP * head_size
    wide = pl.BlockSpec((rows, lanes), lambda i, s: (0, s[6 + k]))
    decays = pl.BlockSpec((GROUP, rows), lambda i, s: (s[6 + k], 0))
    args = [inputs, grad_out, wg, write_proj, read_proj, log_decay, part, tot, *carried]
    return pl.pallas_call(
        functools.partial(grads_kernel, scale),
        grid_spec=pltpu.PrefetchScalarGridSpec(
            num_scalar_prefetch=1,
            grid=(1,),
            in_specs=[
                wide,
                wide,
                pl.BlockSpec((1, rows, lanes), lambda i, s: (0, 0, s[6 + k])),
                full(write_proj),
                full(read_proj),
                decays,
                pl.BlockSpec((2 * width, lanes), lambda i, s: (0, s[6 + k])),
                pl.BlockSpec((16, lanes), lambda i, s: (0, s[6 + k])),
            ]
            + [full(a) for a in carried]
            + [ANYWHERE] * (len(held) + len(after)),
            out_specs=[wide, decays],
        ),
        out_shape=[stored((rows, heads * head_size), BF16), stored((heads, rows))],
        input_output_aliases={1 + len(args): 0, 2 + len(args): 1} if held else {},
        compiler_params=params(),
        cost_estimate=FREE,
        name="grads",
    )(sel, *args, *held, *after)


def join_kernel(sel, near_own, near_other, far_own, far_other, read_ref, write_ref, sems):
    step = near_own.shape[0]
    odd = sel[5] % 2

    def copies(near_ref, far_ref):
        moves = []
        for k, (part, out) in enumerate(
            ((near_own, near_ref), (near_other, near_ref), (far_own, far_ref), (far_other, far_ref))
        ):
            at = pl.multiple_of((odd if k % 2 == 0 else 1 - odd) * step, step)
            moves.append(pltpu.make_async_copy(part, out.at[pl.ds(at, step), :], sems.at[k]))
        for move in moves:
            move.start()
        for move in moves:
            move.wait()

    pl.when(sel[0] == 0)(lambda: copies(read_ref, write_ref))
    pl.when(sel[0] != 0)(lambda: copies(write_ref, read_ref))


def swap(values, axis, mask):
    count = lax.axis_size(axis)
    return lax.ppermute(values, axis, [(i, i ^ mask) for i in range(count)])


def scan_over(pay, width, reverse):
    count = lax.axis_size("seq")
    place = lax.axis_index("seq")
    ahead = count - 1 - place if reverse else place
    part = pay[width : 2 * width] if reverse else pay[0:width]
    dec = pay[2 * width : 2 * width + 1]

    def shifted(values, hop):
        route = [(i, i - hop) if reverse else (i, i + hop) for i in range(count)]
        return lax.ppermute(values, "seq", [(a, b) for a, b in route if 0 <= b < count])

    hop = 1
    while hop < count:
        got_part, got_dec = shifted(part, hop), shifted(dec, hop)
        use = ahead >= hop
        part = jnp.where(use, part + dec * got_part, part)
        dec = jnp.where(use, dec * got_dec, dec)
        hop *= 2
    return shifted(part, 1)


def tied(value, *others):
    return lax.optimization_barrier((value, *others))[0]


def local(inputs, grad_out, write_proj, read_proj, log_decay):
    head_count, rows = log_decay.shape
    head_size = inputs.shape[1] // head_count
    width = write_proj.shape[1]
    lanes = GROUP * head_size
    groups = head_count // GROUP
    seq_count, head_parts = lax.axis_size("seq"), lax.axis_size("head")
    scale = (head_size * rows * seq_count) ** (-0.5)
    place = lax.axis_index("seq").astype(jnp.int32)
    core, x, y = place % 2, (place // 2) % 2, (place // 4) % 2
    fast = seq_count == 8 and groups == 2 and head_parts == 4
    order = [core, 1 - core] if fast else [jnp.int32(k) for k in range(groups)]
    ways = [y, 1 - y] if fast else [jnp.int32(0), jnp.int32(1)]
    sel = jnp.stack([*ways, core, x, y, lax.axis_index("head").astype(jnp.int32), *order])
    data = (inputs, grad_out, write_proj, read_proj, log_decay)

    if fast:
        other = states(order[1][None], *data, head_size)
        got = swap(other, "seq", 1)
        mine = states(order[0][None], *data, head_size)
        px, py = call(chip_kernel, "chip", sel, (mine, got), [shape_of((width + 8, lanes))] * 2)
        rx, ry, rd = swap(px, "seq", 2), swap(py, "seq", 4), swap(py, "seq", 6)
        early, *parts = scores(*data, head_size, (px, py))
        near_own, send = carry(0, sel, [rx], mine, got, "carry_near", (parts[2],))
        near_got = swap(send, "seq", 1)
        (acc,) = late(0, sel, 0, parts, near_own, early, False, "late_near_mine")
        near_parts = late(0, sel, 1, parts, near_got, acc[None], True, "late_near_other")
        near_half = near_parts[0] + swap(near_parts[1], "head", 1)
        near_cross = swap(near_half, "head", 2)
        far_own, send = carry(1, sel, [rx, ry, rd], mine, got, "carry_far", (near_half,))
        far_got = swap(send, "seq", 1)
        (acc,) = late(1, sel, 0, parts, far_own, early, False, "late_far_mine")
        far_parts = late(1, sel, 1, parts, far_got, acc[None], True, "late_far_other")
        far_arrived = swap(far_parts[1], "head", 1)
        near_sum = near_half + near_cross
        near_rest = swap(near_sum, "head", 1)
        held = grads(sel, 0, data, parts, (near_own, far_own, mine), scale, head_size, (), (far_parts[1],))
        far_half = far_parts[0] + tied(far_arrived, *held)
        far_cross = swap(far_half, "head", 2)
        grad_inputs, grad_decay = grads(
            sel, 1, data, parts, (near_got, far_got, other), scale, head_size, held, (far_half,)
        )
        far_sum = far_half + tied(far_cross, grad_decay)
        far_rest = swap(far_sum, "head", 1)
        grad_read, grad_write = call(
            join_kernel,
            "join",
            sel,
            (near_sum, near_rest, far_sum, far_rest),
            [shape_of((rows, width))] * 2,
            in_specs=[ANYWHERE] * 4,
            out_specs=[ANYWHERE] * 2,
            scratch=[pltpu.SemaphoreType.DMA((4,))],
        )
        return grad_inputs, grad_write, grad_read, grad_decay

    pays = [states(k[None], *data, head_size) for k in order]
    early, *parts = scores(*data, head_size, ())
    carried = [[scan_over(pay, width, bool(way)) for pay in pays] for way in (0, 1)]
    totals = []
    for way in (0, 1):
        acc = early
        for k in range(groups):
            acc = late(way, sel, k, parts, carried[way][k], acc, False, "late")[0][None]
        totals.append(acc[0])
    held = ()
    for k in range(groups):
        held = grads(sel, k, data, parts, (carried[0][k], carried[1][k], pays[k]), scale, head_size, tuple(held))
    grad_inputs, grad_decay = held
    grad_read, grad_write = lax.psum(tuple(totals), "head")
    return grad_inputs, grad_write, grad_read, grad_decay


def solution(mesh):
    in_specs = (
        P("seq", "head"),
        P("seq", "head"),
        P("seq", None),
        P("seq", None),
        P("head", "seq"),
    )
    out_specs = (P("seq", "head"), P("seq", None), P("seq", None), P("head", "seq"))
    return jax.shard_map(local, mesh=mesh, in_specs=in_specs, out_specs=out_specs, check_vma=False)
```

```python
import functools

import jax
import jax.numpy as jnp
from jax import lax
from jax.experimental import pallas as pl
from jax.experimental.pallas import tpu as pltpu
from jax.sharding import PartitionSpec as P

Q = 256
GROUP = 8
F32 = jnp.float32
BF16 = jnp.bfloat16
ANYWHERE = pl.BlockSpec(memory_space=pl.ANY)
FREE = pl.CostEstimate(flops=1000, bytes_accessed=1000, transcendentals=0)


def dot(a, b):
    return jnp.dot(a, b, preferred_element_type=F32)


def dot_t(a, b):
    return lax.dot_general(a, b, (((1,), (1,)), ((), ())), preferred_element_type=F32)


def iota(shape, dim):
    return lax.broadcasted_iota(jnp.int32, shape, dim)


def split_two(values):
    high = values.astype(BF16).astype(F32)
    return high, values - high


def split_three(values):
    high, rest = split_two(values)
    mid, low = split_two(rest)
    return high, mid, low


def times_ones(values, ones):
    high, mid, low = split_three(values)
    stacked = jnp.concatenate([high, mid, low, jnp.zeros_like(low)], axis=0).astype(BF16)
    out = dot(stacked, ones)
    return out[0:GROUP] + out[GROUP : 2 * GROUP] + out[2 * GROUP : 3 * GROUP]


def running_of(decay_blk):
    upto = (iota((Q, Q), 0) <= iota((Q, Q), 1)).astype(BF16)
    return times_ones(decay_blk, upto)


def spread_decays(running, head_size):
    lanes = GROUP * head_size
    total = running[:, Q - 1 : Q]
    parts = split_two(jnp.exp(running)) + split_two(jnp.exp(total - running))
    stacked = jnp.concatenate(parts, axis=0).T.astype(BF16)
    row = iota((4 * GROUP, lanes), 0)
    owner = row % GROUP == iota((4 * GROUP, lanes), 1) // head_size
    first = (owner & (row < 2 * GROUP)).astype(F32).astype(BF16)
    second = (owner & (row >= 2 * GROUP)).astype(F32).astype(BF16)
    return dot(stacked, first), dot(stacked, second)


def state_kernel(sel, x_hbm, g_hbm, w_hbm, r_hbm, ld_hbm, *rest):
    outs, (x_ref, g_ref, w_ref, r_ref, ld_ref, pay_ref, wg_ref, part_ref, tot_ref, sems) = rest[:4], rest[4:]
    rows, lanes = x_ref.shape
    width = w_ref.shape[1]
    here = pl.ds(pl.multiple_of(sel[0] * lanes, lanes), lanes)
    group = pl.ds(pl.multiple_of(sel[0] * GROUP, GROUP), GROUP)
    small = [
        pltpu.make_async_copy(src, dst, sems.at[k])
        for k, (src, dst) in enumerate(((ld_hbm.at[group, :], ld_ref), (w_hbm, w_ref), (r_hbm, r_ref)))
    ]
    large = []
    for b in range(2):
        at = pl.ds(b * Q, Q)
        large.append(pltpu.make_async_copy(x_hbm.at[at, here], x_ref.at[at, :], sems.at[3 + 2 * b]))
        large.append(pltpu.make_async_copy(g_hbm.at[at, here], g_ref.at[at, :], sems.at[4 + 2 * b]))
    for move in small + large:
        move.start()
    leaving = []

    def leave(src, dst):
        leaving.append(pltpu.make_async_copy(src, dst, sems.at[7 + len(leaving)]))
        leaving[-1].start()

    pay_out, wg_out, part_out, tot_out = outs
    small[0].wait()
    decays = [spread_decays(running_of(ld_ref[:, b * Q : (b + 1) * Q]), lanes // GROUP) for b in range(2)]
    ends = [decay_in[Q - 1 : Q, :] for decay_in, _ in decays]
    tot_ref[0:8, :] = jnp.broadcast_to(ends[0], (8, lanes))
    tot_ref[8:16, :] = jnp.broadcast_to(ends[1], (8, lanes))
    leave(tot_ref, tot_out)
    small[1].wait()
    small[2].wait()
    f_parts, g_parts = [], []
    for b in range(2):
        at = slice(b * Q, (b + 1) * Q)
        decay_in, decay_out = decays[b]
        large[2 * b].wait()
        iw = (x_ref[at, :].astype(F32) * decay_out).astype(BF16)
        wg_ref[1, at, :] = iw
        leave(wg_ref.at[1, pl.ds(b * Q, Q), :], wg_out.at[1, pl.ds(b * Q, Q), :])
        f_parts.append(dot(w_ref[at, :].astype(F32).T.astype(BF16), iw))
        large[2 * b + 1].wait()
        gw = (g_ref[at, :].astype(F32) * decay_in).astype(BF16)
        wg_ref[0, at, :] = gw
        leave(wg_ref.at[0, pl.ds(b * Q, Q), :], wg_out.at[0, pl.ds(b * Q, Q), :])
        g_parts.append(dot(r_ref[at, :].astype(F32).T.astype(BF16), gw))
    pay_ref[0:width, :] = ends[1] * f_parts[0] + f_parts[1]
    pay_ref[width : 2 * width, :] = ends[0] * g_parts[1] + g_parts[0]
    pay_ref[2 * width : 2 * width + 8, :] = jnp.broadcast_to(ends[0] * ends[1], (8, lanes))
    leave(pay_ref, pay_out)
    part_ref[0:width, :] = f_parts[0]
    part_ref[width : 2 * width, :] = g_parts[1]
    leave(part_ref, part_out)
    for move in leaving:
        move.wait()


def params(limit=32):
    return pltpu.CompilerParams(vmem_limit_bytes=limit * 1024 * 1024)


def shape_of(shape, dtype=F32):
    return jax.ShapeDtypeStruct(shape, dtype)


def stored(shape, dtype=F32):
    return pltpu.HBM(shape, dtype)


def far_off(values):
    return pltpu.with_memory_space_constraint(values, pltpu.HBM)


def states(which, inputs, grad_out, write_proj, read_proj, log_decay, head_size):
    rows, width = write_proj.shape
    lanes = GROUP * head_size
    shapes = [((2 * width + 8, lanes), F32), ((2, rows, lanes), BF16), ((2 * width, lanes), F32), ((16, lanes), F32)]
    return pl.pallas_call(
        state_kernel,
        grid_spec=pltpu.PrefetchScalarGridSpec(
            num_scalar_prefetch=1,
            grid=(1,),
            in_specs=[pl.BlockSpec(memory_space=pltpu.HBM)] * 5,
            out_specs=[ANYWHERE] * 4,
            scratch_shapes=[
                pltpu.VMEM((rows, lanes), BF16),
                pltpu.VMEM((rows, lanes), BF16),
                pltpu.VMEM((rows, width), BF16),
                pltpu.VMEM((rows, width), BF16),
                pltpu.VMEM((GROUP, rows), F32),
                *[pltpu.VMEM(*a) for a in shapes],
                pltpu.SemaphoreType.DMA((14,)),
            ],
        ),
        out_shape=[shape_of(*shapes[0]), *[stored(*a) for a in shapes[1:]]],
        compiler_params=params(),
        cost_estimate=FREE,
        name="states",
    )(which, *map(far_off, (inputs, grad_out, write_proj, read_proj, log_decay)))


def chip_kernel(sel, mine_ref, got_ref, first_ref, second_ref):
    width = (mine_ref.shape[0] - 8) // 2
    lead = sel[2] == 0
    f_rows, b_rows, d_rows = slice(0, width), slice(width, 2 * width), slice(2 * width, 2 * width + 8)
    dec_mine, dec_got = mine_ref[d_rows, :], got_ref[d_rows, :]
    dec_first = jnp.where(lead, dec_mine, dec_got)[0:1]
    dec_second = jnp.where(lead, dec_got, dec_mine)[0:1]
    f_mine, f_got = mine_ref[f_rows, :], got_ref[f_rows, :]
    b_mine, b_got = mine_ref[b_rows, :], got_ref[b_rows, :]
    forward = dec_second * jnp.where(lead, f_mine, f_got) + jnp.where(lead, f_got, f_mine)
    backward = jnp.where(lead, b_mine, b_got) + dec_first * jnp.where(lead, b_got, b_mine)
    low = sel[4] == 0
    first_ref[f_rows, :] = jnp.where(low, forward, backward)
    first_ref[width : width + 8, :] = dec_mine * dec_got
    second_ref[...] = jnp.where(low, backward, forward)


def full(ref_or_shape):
    shape = ref_or_shape.shape
    return pl.BlockSpec(shape, lambda i, s: (0,) * len(shape))


def call(kernel, name, sel, args, outs, in_specs=None, scratch=(), out_specs=None, after=()):
    skip, count = len(args), len(after)

    def body(s, *refs):
        kernel(s, *refs[:skip], *refs[skip + count :])

    return pl.pallas_call(
        body,
        grid_spec=pltpu.PrefetchScalarGridSpec(
            num_scalar_prefetch=1,
            grid=(1,),
            in_specs=(in_specs or [full(a) for a in args]) + [ANYWHERE] * count,
            out_specs=out_specs or [full(o) for o in outs],
            scratch_shapes=list(scratch),
        ),
        out_shape=list(outs),
        compiler_params=params(),
        cost_estimate=FREE,
        name=name,
    )(sel, *args, *after)


def leave_states(way, sel, entering, mine_ref, got_ref, mine_dec, got_dec, own_ref, send_ref):
    first = sel[way] == sel[2]
    own_ref[...] = jnp.where(first, entering, got_dec[0:1, :] * entering + got_ref[...])
    send_ref[...] = jnp.where(first, mine_dec[0:1, :] * entering + mine_ref[...], entering)


def near_kernel(sel, rx_ref, px_ref, *refs):
    width = rx_ref.shape[0] - 8
    head, tail = slice(0, width), slice(width, width + 1)
    same = sel[3] == sel[4]
    rx, px = rx_ref[head, :], px_ref[head, :]
    leave_states(0, sel, jnp.where(same, jnp.zeros_like(rx), rx), *refs[:-1])
    refs[-1][...] = jnp.where(same, rx_ref[tail, :] * px + rx, px_ref[tail, :] * rx + px)


def far_kernel(sel, rx_ref, sx_ref, ry_ref, *refs):
    width = sx_ref.shape[0]
    ry = ry_ref[...]
    leave_states(1, sel, jnp.where(sel[3] == sel[4], sx_ref[...] + rx_ref[width : width + 1, :] * ry, ry), *refs)


def carry(way, sel, arrived, mine, got, after=()):
    width, lanes = mine.shape[0] // 2 - 4, mine.shape[1]
    part = pl.BlockSpec((width, lanes), lambda i, s: (s[way], 0))
    dec = pl.BlockSpec((8, lanes), lambda i, s: (2 * width // 8, 0))
    return call(
        (near_kernel, far_kernel)[way],
        ("carry_near", "carry_far")[way],
        sel,
        [*arrived, mine, got, mine, got],
        [shape_of((width, lanes))] * (3 - way),
        in_specs=[full(a) for a in arrived] + [part, part, dec, dec],
        after=after,
    )


def late_kernel(way, sel, wg_ref, car_ref, part_ref, tot_ref, acc_ref, out_ref):
    car = car_ref[...]
    onward = tot_ref[0:1, :] * car + part_ref[...]
    forward = sel[way] == 0
    for b in range(2):
        at = slice(b * Q, (b + 1) * Q)
        held = jnp.where(forward, onward if b else car, car if b else onward).astype(BF16)
        out_ref[at, :] = acc_ref[0, at, :] + dot_t(wg_ref[0, at, :], held)


def cut_kernel(way, sel, wg_ref, car_ref, part_ref, tot_ref, acc_ref, keep_ref, send_ref, total):
    late_kernel(way, sel, wg_ref, car_ref, part_ref, tot_ref, acc_ref, total)
    step = keep_ref.shape[0]
    odd = sel[5] % 2
    keep_ref[...] = total[pl.ds(pl.multiple_of(odd * step, step), step), :]
    send_ref[...] = total[pl.ds(pl.multiple_of((1 - odd) * step, step), step), :]


def late(way, sel, state, carried, acc, cut, name):
    _, wg, part, tot = state
    rows = wg.shape[1]
    width, lanes = carried.shape
    both = acc.shape[0] == 2
    outs = [shape_of((rows // 2, width))] * 2 if cut else [shape_of((rows, width))]
    return call(
        functools.partial(cut_kernel if cut else late_kernel, way),
        name,
        sel,
        [wg, carried, part, tot, acc],
        outs,
        in_specs=[
            pl.BlockSpec((1, rows, lanes), lambda i, s: (s[way], 0, 0)),
            full(carried),
            pl.BlockSpec((width, lanes), lambda i, s: (s[way], 0)),
            pl.BlockSpec((8, lanes), lambda i, s: (s[way], 0)),
            pl.BlockSpec((1, rows, width), lambda i, s: (s[way] if both else 0, 0, 0)),
        ],
        scratch=[pltpu.VMEM((rows, width), F32)] if cut else [],
    )


def decay_blocks(running):
    half = Q // 2
    columns = jnp.concatenate([running] * (128 // GROUP), axis=0).T
    keep_top = iota((half, Q), 0) <= iota((half, Q), 1)
    keep_low = iota((half, half), 0) <= iota((half, half), 1)

    def of(h):
        row, col = running[h : h + 1, :], columns[:, h : h + 1]
        top = jnp.exp(jnp.where(keep_top, row - col[0:half], -jnp.inf))
        low = jnp.exp(jnp.where(keep_low, row[:, half:] - col[half:], -jnp.inf))
        return top, low

    return of


def pair_products(x_pair, g_pair):
    half = Q // 2
    lane = iota(x_pair.shape, 1)
    none = jnp.zeros_like(x_pair)
    left = lane < x_pair.shape[1] // 2
    first, second = jnp.where(left, x_pair, none), jnp.where(left, none, x_pair)
    top = dot_t(jnp.concatenate([first[0:half], second[0:half]], axis=0), g_pair)
    low = dot_t(jnp.concatenate([first[half:], second[half:]], axis=0), g_pair[half:])
    return (top[0:half], low[0:half]), (top[half:], low[half:])


def scores_kernel(x_ref, g_ref, w_ref, r_ref, ld_ref, *rest):
    acc_ref, gs_ref = rest[-2:]
    group = pl.program_id(1)
    size = x_ref.shape[1] // GROUP
    half = Q // 2
    running = running_of(ld_ref[...])
    decays = decay_blocks(running)
    gs_top = jnp.zeros((half, Q), F32)
    gs_low = jnp.zeros((half, half), F32)
    for pair in range(GROUP // 2):
        at = slice(pair * 2 * size, (pair + 1) * 2 * size)
        for k, (pairs_top, pairs_low) in enumerate(pair_products(x_ref[:, at], g_ref[:, at])):
            decay_top, decay_low = decays(2 * pair + k)
            gs_top = gs_top + decay_top * pairs_top
            gs_low = gs_low + decay_low * pairs_low

    @pl.when(group == 0)
    def _():
        gs_ref[0:half, :] = gs_top
        gs_ref[half:, 0:half] = jnp.zeros_like(gs_low)
        gs_ref[half:, half:] = gs_low

    @pl.when(group > 0)
    def _():
        gs_ref[0:half, :] += gs_top
        gs_ref[half:, half:] += gs_low

    @pl.when(group == pl.num_programs(1) - 1)
    def _():
        grad_scores = gs_ref[...]
        acc_ref[0] = dot(grad_scores.T.astype(BF16), w_ref[...])
        acc_ref[1] = dot(grad_scores.astype(BF16), r_ref[...])


def scores(inputs, grad_out, write_proj, read_proj, log_decay, head_size, after):
    rows, width = write_proj.shape
    heads = log_decay.shape[0]
    lanes = GROUP * head_size
    wide = pl.BlockSpec((Q, lanes), lambda b, j: (b, j))
    narrow = pl.BlockSpec((Q, width), lambda b, j: (b, 0))
    return pl.pallas_call(
        scores_kernel,
        grid=(rows // Q, heads // GROUP),
        in_specs=[wide, wide, narrow, narrow, pl.BlockSpec((GROUP, Q), lambda b, j: (j, b))] + [ANYWHERE] * len(after),
        out_specs=pl.BlockSpec((2, Q, width), lambda b, j: (0, b, 0)),
        out_shape=shape_of((2, rows, width)),
        scratch_shapes=[pltpu.VMEM((Q, Q), F32)],
        compiler_params=params(),
        cost_estimate=FREE,
        name="scores",
    )(inputs, grad_out, write_proj, read_proj, log_decay, *after)


def grads_kernel(scale, sel, x_ref, g_ref, gw_ref, w_ref, r_ref, ld_ref, part_ref, tot_ref, near_ref, far_ref, pay_ref, *rest):
    gi_ref, gd_ref = rest[-2:]
    lanes = x_ref.shape[1]
    width = w_ref.shape[1]
    size = lanes // GROUP
    half = Q // 2
    near_forward = sel[0] == 0
    f_car = jnp.where(near_forward, near_ref[...], far_ref[...])
    b_car = jnp.where(near_forward, far_ref[...], near_ref[...])
    f_next = tot_ref[0:1, :] * f_car + part_ref[0:width, :]
    b_next = tot_ref[8:9, :] * b_car + part_ref[width : 2 * width, :]
    state_in, grad_end = (f_car, f_next), (b_next, b_car)
    last = pay_ref[2 * width : 2 * width + 1, :] * f_car + pay_ref[0:width, :]
    after = (f_next, last)
    owner = iota((16, lanes), 0) == iota((16, lanes), 1) // size
    ones = owner.astype(F32).astype(BF16)
    onward = (iota((Q, Q), 0) >= iota((Q, Q), 1)).astype(F32).astype(BF16)
    left = iota((Q, 2 * size), 1) < size
    for b in range(2):
        at = slice(b * Q, (b + 1) * Q)
        running = running_of(ld_ref[:, at])
        decays = decay_blocks(running)
        decay_out = spread_decays(running, size)[1]
        products = dot_t(w_ref[at, :], r_ref[at, :])
        sums_top, sums_low, changes = [], [], None
        for pair in range(GROUP // 2):
            here = slice(pair * 2 * size, (pair + 1) * 2 * size)
            x_pair, g_pair = x_ref[at, here], g_ref[at, here]
            none = jnp.zeros_like(g_pair)
            top = low = None
            for k, (pairs_top, pairs_low) in enumerate(pair_products(x_pair, g_pair)):
                decay_top, decay_low = decays(2 * pair + k)
                weights_top = products[0:half] * decay_top
                weights_low = products[half:, half:] * decay_low
                sums_top.append(jnp.sum(weights_top * pairs_top, axis=0, keepdims=True))
                sums_low.append(jnp.sum(weights_low * pairs_low, axis=0, keepdims=True))
                g_own = jnp.where(left, g_pair, none) if k == 0 else jnp.where(left, none, g_pair)
                part_top = dot(weights_top.astype(BF16), g_own)
                part_low = dot(weights_low.astype(BF16), g_own[half:])
                top = part_top if top is None else top + part_top
                low = part_low if low is None else low + part_low
            out_inter = dot(r_ref[at, :], state_in[b][:, here].astype(BF16))
            grad_inter = dot(w_ref[at, :], grad_end[b][:, here].astype(BF16)) * decay_out[:, here]
            grad_full = jnp.concatenate([top, low], axis=0) + grad_inter
            gi_ref[at, here] = grad_full.astype(BF16)
            high, low = split_two(gw_ref[0, at, here].astype(F32) * out_inter - x_pair.astype(F32) * grad_full)
            change = dot_t(ones[:, here], high.astype(BF16)) + dot_t(ones[:, here], low.astype(BF16))
            changes = change if changes is None else changes + change
        early, late_half = jnp.concatenate(sums_top, axis=0), jnp.concatenate(sums_low, axis=0)
        within = changes[0:GROUP] + early + jnp.concatenate([jnp.zeros_like(late_half), late_half], axis=1)
        cross = jnp.sum(after[b] * grad_end[b], axis=0, keepdims=True)
        crossing = jnp.sum(jnp.where(owner[0:GROUP], cross, 0.0), axis=1, keepdims=True)
        gd_ref[:, at] = (times_ones(within, onward) + crossing) * scale


def grads(sel, k, data, state, carried, scale, head_size, held=(), after=()):
    inputs, grad_out, write_proj, read_proj, log_decay = data
    pay, wg, part, tot = state
    rows, width = write_proj.shape
    heads = log_decay.shape[0]
    lanes = GROUP * head_size
    wide = pl.BlockSpec((rows, lanes), lambda i, s: (0, s[6 + k]))
    decays = pl.BlockSpec((GROUP, rows), lambda i, s: (s[6 + k], 0))
    args = [inputs, grad_out, wg, write_proj, read_proj, log_decay, part, tot, *carried, pay]
    return pl.pallas_call(
        functools.partial(grads_kernel, scale),
        grid_spec=pltpu.PrefetchScalarGridSpec(
            num_scalar_prefetch=1,
            grid=(1,),
            in_specs=[
                wide,
                wide,
                pl.BlockSpec((1, rows, lanes), lambda i, s: (0, 0, 0)),
                full(write_proj),
                full(read_proj),
                decays,
            ]
            + [full(a) for a in (part, tot, *carried, pay)]
            + [ANYWHERE] * (len(held) + len(after)),
            out_specs=[wide, decays],
        ),
        out_shape=[stored((rows, heads * head_size), BF16), stored((heads, rows))],
        input_output_aliases={1 + len(args): 0, 2 + len(args): 1} if held else {},
        compiler_params=params(),
        cost_estimate=FREE,
        name="grads",
    )(sel, *args, *held, *after)


def join_kernel(sel, near_own, near_other, far_own, far_other, read_ref, write_ref, sems):
    step = near_own.shape[0]
    odd = sel[5] % 2

    def copies(near_ref, far_ref):
        moves = []
        for k, (part, out) in enumerate(
            ((near_own, near_ref), (near_other, near_ref), (far_own, far_ref), (far_other, far_ref))
        ):
            at = pl.multiple_of((odd if k % 2 == 0 else 1 - odd) * step, step)
            moves.append(pltpu.make_async_copy(part, out.at[pl.ds(at, step), :], sems.at[k]))
        for move in moves:
            move.start()
        for move in moves:
            move.wait()

    pl.when(sel[0] == 0)(lambda: copies(read_ref, write_ref))
    pl.when(sel[0] != 0)(lambda: copies(write_ref, read_ref))


def swap(values, axis, mask):
    count = lax.axis_size(axis)
    return lax.ppermute(values, axis, [(i, i ^ mask) for i in range(count)])


def scan_over(pay, width, reverse):
    count = lax.axis_size("seq")
    place = lax.axis_index("seq")
    ahead = count - 1 - place if reverse else place
    part = pay[width : 2 * width] if reverse else pay[0:width]
    dec = pay[2 * width : 2 * width + 1]

    def shifted(values, hop):
        route = [(i, i - hop) if reverse else (i, i + hop) for i in range(count)]
        return lax.ppermute(values, "seq", [(a, b) for a, b in route if 0 <= b < count])

    hop = 1
    while hop < count:
        got_part, got_dec = shifted(part, hop), shifted(dec, hop)
        use = ahead >= hop
        part = jnp.where(use, part + dec * got_part, part)
        dec = jnp.where(use, dec * got_dec, dec)
        hop *= 2
    return shifted(part, 1)


def tied(value, *others):
    return lax.optimization_barrier((value, *others))[0]


def local(inputs, grad_out, write_proj, read_proj, log_decay):
    head_count, rows = log_decay.shape
    head_size = inputs.shape[1] // head_count
    width = write_proj.shape[1]
    lanes = GROUP * head_size
    groups = head_count // GROUP
    seq_count, head_parts = lax.axis_size("seq"), lax.axis_size("head")
    scale = (head_size * rows * seq_count) ** (-0.5)
    place = lax.axis_index("seq").astype(jnp.int32)
    core, x, y = place % 2, (place // 2) % 2, (place // 4) % 2
    fast = seq_count == 8 and groups == 2 and head_parts == 4
    order = [core, 1 - core] if fast else [jnp.int32(k) for k in range(groups)]
    ways = [y, 1 - y] if fast else [jnp.int32(0), jnp.int32(1)]
    sel = jnp.stack([*ways, core, x, y, lax.axis_index("head").astype(jnp.int32), *order])
    data = (inputs, grad_out, write_proj, read_proj, log_decay)

    if fast:
        other = states(order[1][None], *data, head_size)
        got = swap(other[0], "seq", 1)
        mine = states(order[0][None], *data, head_size)
        outs = [shape_of((width + 8, lanes)), shape_of((width, lanes))]
        px, qx = call(chip_kernel, "chip", sel, (mine[0], got), outs)
        rx, sx = swap(px, "seq", 2), swap(qx, "seq", 2)
        early = scores(*data, head_size, (px,))
        near_own, send, pair = carry(0, sel, [rx, px], mine[0], got, (early,))
        ry = swap(pair, "seq", 4)
        near_got = swap(send, "seq", 1)
        (acc,) = late(0, sel, mine, near_own, early, False, "late_near_mine")
        near_parts = late(0, sel, other, near_got, acc[None], True, "late_near_other")
        near_half = near_parts[0] + swap(near_parts[1], "head", 1)
        near_cross = swap(near_half, "head", 2)
        far_own, send = carry(1, sel, [rx, sx, ry], mine[0], got, (near_half,))
        far_got = swap(send, "seq", 1)
        (acc,) = late(1, sel, mine, far_own, early, False, "late_far_mine")
        far_parts = late(1, sel, other, far_got, acc[None], True, "late_far_other")
        far_arrived = swap(far_parts[1], "head", 1)
        near_sum = near_half + near_cross
        near_rest = swap(near_sum, "head", 1)
        held = grads(sel, 0, data, mine, (near_own, far_own), scale, head_size, (), (far_parts[1],))
        far_half = far_parts[0] + tied(far_arrived, *held)
        far_cross = swap(far_half, "head", 2)
        grad_inputs, grad_decay = grads(
            sel, 1, data, other, (near_got, far_got), scale, head_size, held, (far_half,)
        )
        far_sum = far_half + tied(far_cross, grad_decay)
        far_rest = swap(far_sum, "head", 1)
        grad_read, grad_write = call(
            join_kernel,
            "join",
            sel,
            (near_sum, near_rest, far_sum, far_rest),
            [shape_of((rows, width))] * 2,
            in_specs=[ANYWHERE] * 4,
            out_specs=[ANYWHERE] * 2,
            scratch=[pltpu.SemaphoreType.DMA((4,))],
        )
        return grad_inputs, grad_write, grad_read, grad_decay

    local_states = [states(k[None], *data, head_size) for k in order]
    early = scores(*data, head_size, ())
    carried = [[scan_over(state[0], width, bool(way)) for state in local_states] for way in (0, 1)]
    totals = []
    for way in (0, 1):
        acc = early
        for k, state in enumerate(local_states):
            acc = late(way, sel, state, carried[way][k], acc, False, "late")[0][None]
        totals.append(acc[0])
    held = ()
    for k, state in enumerate(local_states):
        held = grads(sel, k, data, state, (carried[0][k], carried[1][k]), scale, head_size, tuple(held))
    grad_inputs, grad_decay = held
    grad_read, grad_write = lax.psum(tuple(totals), "head")
    return grad_inputs, grad_write, grad_read, grad_decay


def solution(mesh):
    in_specs = (
        P("seq", "head"),
        P("seq", "head"),
        P("seq", None),
        P("seq", None),
        P("head", "seq"),
    )
    out_specs = (P("seq", "head"), P("seq", None), P("seq", None), P("head", "seq"))
    return jax.shard_map(local, mesh=mesh, in_specs=in_specs, out_specs=out_specs, check_vma=False)
```

```python
import functools

import jax
import jax.numpy as jnp
from jax import lax
from jax.experimental import pallas as pl
from jax.experimental.pallas import tpu as pltpu
from jax.sharding import PartitionSpec as P

Q = 256
GROUP = 8
F32 = jnp.float32
BF16 = jnp.bfloat16
ANYWHERE = pl.BlockSpec(memory_space=pl.ANY)
FREE = pl.CostEstimate(flops=1000, bytes_accessed=1000, transcendentals=0)


def dot(a, b):
    return jnp.dot(a, b, preferred_element_type=F32)


def dot_t(a, b):
    return lax.dot_general(a, b, (((1,), (1,)), ((), ())), preferred_element_type=F32)


def iota(shape, dim):
    return lax.broadcasted_iota(jnp.int32, shape, dim)


def split_two(values):
    high = values.astype(BF16).astype(F32)
    return high, values - high


def split_three(values):
    high, rest = split_two(values)
    mid, low = split_two(rest)
    return high, mid, low


def times_ones(values, ones):
    high, mid, low = split_three(values)
    stacked = jnp.concatenate([high, mid, low, jnp.zeros_like(low)], axis=0).astype(BF16)
    out = dot(stacked, ones)
    return out[0:GROUP] + out[GROUP : 2 * GROUP] + out[2 * GROUP : 3 * GROUP]


def running_of(decay_blk):
    upto = (iota((Q, Q), 0) <= iota((Q, Q), 1)).astype(BF16)
    return times_ones(decay_blk, upto)


def spread_decays(running, head_size):
    lanes = GROUP * head_size
    total = running[:, Q - 1 : Q]
    parts = split_two(jnp.exp(running)) + split_two(jnp.exp(total - running))
    stacked = jnp.concatenate(parts, axis=0).T.astype(BF16)
    row = iota((4 * GROUP, lanes), 0)
    owner = row % GROUP == iota((4 * GROUP, lanes), 1) // head_size
    first = (owner & (row < 2 * GROUP)).astype(F32).astype(BF16)
    second = (owner & (row >= 2 * GROUP)).astype(F32).astype(BF16)
    return dot(stacked, first), dot(stacked, second)


def state_kernel(sel, x_hbm, g_hbm, w_hbm, r_hbm, ld_hbm, *rest):
    outs, (x_ref, g_ref, w_ref, r_ref, ld_ref, pay_ref, wg_ref, part_ref, tot_ref, sems) = rest[:4], rest[4:]
    state_body(sel, (x_hbm, g_hbm, w_hbm, r_hbm, ld_hbm), (x_ref, g_ref, w_ref, r_ref, ld_ref), outs, pay_ref, wg_ref, part_ref, tot_ref, sems)


def loaded_kernel(sel, *refs):
    state_body(sel, None, refs[:5], refs[5:9], *refs[9:])


def state_body(sel, sources, refs, outs, pay_ref, wg_ref, part_ref, tot_ref, sems):
    x_ref, g_ref, w_ref, r_ref, ld_ref = refs
    rows, lanes = x_ref.shape
    width = w_ref.shape[1]
    here = pl.ds(pl.multiple_of(sel[0] * lanes, lanes), lanes)
    group = pl.ds(pl.multiple_of(sel[0] * GROUP, GROUP), GROUP)
    moves = []
    if sources:
        x_hbm, g_hbm, w_hbm, r_hbm, ld_hbm = sources
        pairs = [(ld_hbm.at[group, :], ld_ref), (w_hbm, w_ref), (r_hbm, r_ref)]
        for b in range(2):
            at = pl.ds(b * Q, Q)
            pairs.append((x_hbm.at[at, here], x_ref.at[at, :]))
            pairs.append((g_hbm.at[at, here], g_ref.at[at, :]))
        moves = [pltpu.make_async_copy(src, dst, sems.at[k]) for k, (src, dst) in enumerate(pairs)]
    for move in moves:
        move.start()
    leaving = []

    def leave(src, dst):
        leaving.append(pltpu.make_async_copy(src, dst, sems.at[7 + len(leaving)]))
        leaving[-1].start()

    pay_out, wg_out, part_out, tot_out = outs
    for move in moves[:1]:
        move.wait()
    decays = [spread_decays(running_of(ld_ref[:, b * Q : (b + 1) * Q]), lanes // GROUP) for b in range(2)]
    ends = [decay_in[Q - 1 : Q, :] for decay_in, _ in decays]
    tot_ref[0:8, :] = jnp.broadcast_to(ends[0], (8, lanes))
    tot_ref[8:16, :] = jnp.broadcast_to(ends[1], (8, lanes))
    leave(tot_ref, tot_out)
    for move in moves[1:3]:
        move.wait()
    f_parts, g_parts = [], []
    for b in range(2):
        at = slice(b * Q, (b + 1) * Q)
        decay_in, decay_out = decays[b]
        for move in moves[3 + 2 * b : 4 + 2 * b]:
            move.wait()
        iw = (x_ref[at, :].astype(F32) * decay_out).astype(BF16)
        wg_ref[1, at, :] = iw
        leave(wg_ref.at[1, pl.ds(b * Q, Q), :], wg_out.at[1, pl.ds(b * Q, Q), :])
        f_parts.append(dot(w_ref[at, :].astype(F32).T.astype(BF16), iw))
        for move in moves[4 + 2 * b : 5 + 2 * b]:
            move.wait()
        gw = (g_ref[at, :].astype(F32) * decay_in).astype(BF16)
        wg_ref[0, at, :] = gw
        leave(wg_ref.at[0, pl.ds(b * Q, Q), :], wg_out.at[0, pl.ds(b * Q, Q), :])
        g_parts.append(dot(r_ref[at, :].astype(F32).T.astype(BF16), gw))
    pay_ref[0:width, :] = ends[1] * f_parts[0] + f_parts[1]
    pay_ref[width : 2 * width, :] = ends[0] * g_parts[1] + g_parts[0]
    pay_ref[2 * width : 2 * width + 8, :] = jnp.broadcast_to(ends[0] * ends[1], (8, lanes))
    leave(pay_ref, pay_out)
    part_ref[0:width, :] = f_parts[0]
    part_ref[width : 2 * width, :] = g_parts[1]
    leave(part_ref, part_out)
    for move in leaving:
        move.wait()


def params(limit=32):
    return pltpu.CompilerParams(vmem_limit_bytes=limit * 1024 * 1024)


def shape_of(shape, dtype=F32):
    return jax.ShapeDtypeStruct(shape, dtype)


def stored(shape, dtype=F32):
    return pltpu.HBM(shape, dtype)


def far_off(values):
    return pltpu.with_memory_space_constraint(values, pltpu.HBM)


def states(which, inputs, grad_out, write_proj, read_proj, log_decay, head_size, loaded):
    rows, width = write_proj.shape
    lanes = GROUP * head_size
    shapes = [((2 * width + 8, lanes), F32), ((2, rows, lanes), BF16), ((2 * width, lanes), F32), ((16, lanes), F32)]
    args = (inputs, grad_out, write_proj, read_proj, log_decay)
    buffers = [((rows, lanes), BF16)] * 2 + [((rows, width), BF16)] * 2 + [((GROUP, rows), F32)]
    wide = pl.BlockSpec((rows, lanes), lambda i, s: (0, s[0]))
    return pl.pallas_call(
        loaded_kernel if loaded else state_kernel,
        grid_spec=pltpu.PrefetchScalarGridSpec(
            num_scalar_prefetch=1,
            grid=(1,),
            in_specs=[wide, wide, full(write_proj), full(read_proj), pl.BlockSpec((GROUP, rows), lambda i, s: (s[0], 0))]
            if loaded
            else [pl.BlockSpec(memory_space=pltpu.HBM)] * 5,
            out_specs=[ANYWHERE] * 4,
            scratch_shapes=[
                *[pltpu.VMEM(*a) for a in ([] if loaded else buffers) + shapes],
                pltpu.SemaphoreType.DMA((14,)),
            ],
        ),
        out_shape=[shape_of(*shapes[0]), *[stored(*a) for a in shapes[1:]]],
        compiler_params=params(),
        cost_estimate=FREE,
        name="states",
    )(which, *(args if loaded else map(far_off, args)))


def chip_kernel(sel, mine_ref, got_ref, first_ref, second_ref):
    width = (mine_ref.shape[0] - 8) // 2
    lead = sel[2] == 0
    f_rows, b_rows, d_rows = slice(0, width), slice(width, 2 * width), slice(2 * width, 2 * width + 8)
    dec_mine, dec_got = mine_ref[d_rows, :], got_ref[d_rows, :]
    dec_first = jnp.where(lead, dec_mine, dec_got)[0:1]
    dec_second = jnp.where(lead, dec_got, dec_mine)[0:1]
    f_mine, f_got = mine_ref[f_rows, :], got_ref[f_rows, :]
    b_mine, b_got = mine_ref[b_rows, :], got_ref[b_rows, :]
    forward = dec_second * jnp.where(lead, f_mine, f_got) + jnp.where(lead, f_got, f_mine)
    backward = jnp.where(lead, b_mine, b_got) + dec_first * jnp.where(lead, b_got, b_mine)
    low = sel[4] == 0
    first_ref[f_rows, :] = jnp.where(low, forward, backward)
    first_ref[width : width + 8, :] = dec_mine * dec_got
    second_ref[...] = jnp.where(low, backward, forward)


def full(ref_or_shape):
    shape = ref_or_shape.shape
    return pl.BlockSpec(shape, lambda i, s: (0,) * len(shape))


def call(kernel, name, sel, args, outs, in_specs=None, scratch=(), out_specs=None, after=()):
    skip, count = len(args), len(after)

    def body(s, *refs):
        kernel(s, *refs[:skip], *refs[skip + count :])

    return pl.pallas_call(
        body,
        grid_spec=pltpu.PrefetchScalarGridSpec(
            num_scalar_prefetch=1,
            grid=(1,),
            in_specs=(in_specs or [full(a) for a in args]) + [ANYWHERE] * count,
            out_specs=out_specs or [full(o) for o in outs],
            scratch_shapes=list(scratch),
        ),
        out_shape=list(outs),
        compiler_params=params(),
        cost_estimate=FREE,
        name=name,
    )(sel, *args, *after)


def leave_states(way, sel, entering, mine_ref, got_ref, mine_dec, got_dec, own_ref, send_ref):
    first = sel[way] == sel[2]
    own_ref[...] = jnp.where(first, entering, got_dec[0:1, :] * entering + got_ref[...])
    send_ref[...] = jnp.where(first, mine_dec[0:1, :] * entering + mine_ref[...], entering)


def near_kernel(sel, rx_ref, px_ref, *refs):
    width = rx_ref.shape[0] - 8
    head, tail = slice(0, width), slice(width, width + 1)
    same = sel[3] == sel[4]
    rx, px = rx_ref[head, :], px_ref[head, :]
    leave_states(0, sel, jnp.where(same, jnp.zeros_like(rx), rx), *refs[:-1])
    refs[-1][...] = jnp.where(same, rx_ref[tail, :] * px + rx, px_ref[tail, :] * rx + px)


def far_kernel(sel, rx_ref, sx_ref, ry_ref, *refs):
    width = sx_ref.shape[0]
    ry = ry_ref[...]
    leave_states(1, sel, jnp.where(sel[3] == sel[4], sx_ref[...] + rx_ref[width : width + 1, :] * ry, ry), *refs)


def carry(way, sel, arrived, mine, got, after=()):
    width, lanes = mine.shape[0] // 2 - 4, mine.shape[1]
    part = pl.BlockSpec((width, lanes), lambda i, s: (s[way], 0))
    dec = pl.BlockSpec((8, lanes), lambda i, s: (2 * width // 8, 0))
    return call(
        (near_kernel, far_kernel)[way],
        ("carry_near", "carry_far")[way],
        sel,
        [*arrived, mine, got, mine, got],
        [shape_of((width, lanes))] * (3 - way),
        in_specs=[full(a) for a in arrived] + [part, part, dec, dec],
        after=after,
    )


def late_kernel(way, sel, wg_ref, car_ref, part_ref, tot_ref, acc_ref, out_ref):
    car = car_ref[...]
    onward = tot_ref[0:1, :] * car + part_ref[...]
    forward = sel[way] == 0
    for b in range(2):
        at = slice(b * Q, (b + 1) * Q)
        held = jnp.where(forward, onward if b else car, car if b else onward).astype(BF16)
        out_ref[at, :] = acc_ref[0, at, :] + dot_t(wg_ref[0, at, :], held)


def cut_kernel(way, sel, wg_ref, car_ref, part_ref, tot_ref, acc_ref, keep_ref, send_ref, total):
    late_kernel(way, sel, wg_ref, car_ref, part_ref, tot_ref, acc_ref, total)
    step = keep_ref.shape[0]
    odd = sel[5] % 2
    keep_ref[...] = total[pl.ds(pl.multiple_of(odd * step, step), step), :]
    send_ref[...] = total[pl.ds(pl.multiple_of((1 - odd) * step, step), step), :]


def late(way, sel, state, carried, acc, cut, name):
    _, wg, part, tot = state
    rows = wg.shape[1]
    width, lanes = carried.shape
    both = acc.shape[0] == 2
    outs = [shape_of((rows // 2, width))] * 2 if cut else [shape_of((rows, width))]
    return call(
        functools.partial(cut_kernel if cut else late_kernel, way),
        name,
        sel,
        [wg, carried, part, tot, acc],
        outs,
        in_specs=[
            pl.BlockSpec((1, rows, lanes), lambda i, s: (s[way], 0, 0)),
            full(carried),
            pl.BlockSpec((width, lanes), lambda i, s: (s[way], 0)),
            pl.BlockSpec((8, lanes), lambda i, s: (s[way], 0)),
            pl.BlockSpec((1, rows, width), lambda i, s: (s[way] if both else 0, 0, 0)),
        ],
        scratch=[pltpu.VMEM((rows, width), F32)] if cut else [],
    )


def decay_blocks(running):
    half = Q // 2
    columns = jnp.concatenate([running] * (128 // GROUP), axis=0).T
    keep_top = iota((half, Q), 0) <= iota((half, Q), 1)
    keep_low = iota((half, half), 0) <= iota((half, half), 1)

    def of(h):
        row, col = running[h : h + 1, :], columns[:, h : h + 1]
        top = jnp.exp(jnp.where(keep_top, row - col[0:half], -jnp.inf))
        low = jnp.exp(jnp.where(keep_low, row[:, half:] - col[half:], -jnp.inf))
        return top, low

    return of


def pair_products(x_pair, g_pair):
    half = Q // 2
    lane = iota(x_pair.shape, 1)
    none = jnp.zeros_like(x_pair)
    left = lane < x_pair.shape[1] // 2
    first, second = jnp.where(left, x_pair, none), jnp.where(left, none, x_pair)
    top = dot_t(jnp.concatenate([first[0:half], second[0:half]], axis=0), g_pair)
    low = dot_t(jnp.concatenate([first[half:], second[half:]], axis=0), g_pair[half:])
    return (top[0:half], low[0:half]), (top[half:], low[half:])


def scores_kernel(x_ref, g_ref, w_ref, r_ref, ld_ref, *rest):
    acc_ref, gint_ref, dot_ref, gs_ref = rest[-4:]
    group = pl.program_id(1)
    size = x_ref.shape[1] // GROUP
    half = Q // 2
    decays = decay_blocks(running_of(ld_ref[...]))
    products = dot_t(w_ref[...], r_ref[...])
    left = iota((Q, 2 * size), 1) < size
    gs_top = jnp.zeros((half, Q), F32)
    gs_low = jnp.zeros((half, half), F32)
    sums_top, sums_low = [], []
    for pair in range(GROUP // 2):
        at = slice(pair * 2 * size, (pair + 1) * 2 * size)
        g_pair = g_ref[:, at]
        none = jnp.zeros_like(g_pair)
        top = low = None
        for k, (pairs_top, pairs_low) in enumerate(pair_products(x_ref[:, at], g_pair)):
            decay_top, decay_low = decays(2 * pair + k)
            scaled_top, scaled_low = decay_top * pairs_top, decay_low * pairs_low
            gs_top = gs_top + scaled_top
            gs_low = gs_low + scaled_low
            sums_top.append(jnp.sum(products[0:half] * scaled_top, axis=0, keepdims=True))
            sums_low.append(jnp.sum(products[half:, half:] * scaled_low, axis=0, keepdims=True))
            g_own = jnp.where(left, g_pair, none) if k == 0 else jnp.where(left, none, g_pair)
            part_top = dot((products[0:half] * decay_top).astype(BF16), g_own)
            part_low = dot((products[half:, half:] * decay_low).astype(BF16), g_own[half:])
            top = part_top if top is None else top + part_top
            low = part_low if low is None else low + part_low
        gint_ref[0:half, at] = top
        gint_ref[half:, at] = low
    late_half = jnp.concatenate(sums_low, axis=0)
    dot_ref[...] = jnp.concatenate(sums_top, axis=0) + jnp.concatenate([jnp.zeros_like(late_half), late_half], axis=1)

    @pl.when(group == 0)
    def _():
        gs_ref[0:half, :] = gs_top
        gs_ref[half:, 0:half] = jnp.zeros_like(gs_low)
        gs_ref[half:, half:] = gs_low

    @pl.when(group > 0)
    def _():
        gs_ref[0:half, :] += gs_top
        gs_ref[half:, half:] += gs_low

    @pl.when(group == pl.num_programs(1) - 1)
    def _():
        grad_scores = gs_ref[...]
        acc_ref[0] = dot(grad_scores.T.astype(BF16), w_ref[...])
        acc_ref[1] = dot(grad_scores.astype(BF16), r_ref[...])


def scores(inputs, grad_out, write_proj, read_proj, log_decay, head_size, after):
    rows, width = write_proj.shape
    heads = log_decay.shape[0]
    lanes = GROUP * head_size
    wide = pl.BlockSpec((Q, lanes), lambda b, j: (b, j))
    narrow = pl.BlockSpec((Q, width), lambda b, j: (b, 0))
    return pl.pallas_call(
        scores_kernel,
        grid=(rows // Q, heads // GROUP),
        in_specs=[wide, wide, narrow, narrow, pl.BlockSpec((GROUP, Q), lambda b, j: (j, b))] + [ANYWHERE] * len(after),
        out_specs=[
            pl.BlockSpec((2, Q, width), lambda b, j: (0, b, 0)),
            wide,
            pl.BlockSpec((GROUP, Q), lambda b, j: (j, b)),
        ],
        out_shape=[shape_of((2, rows, width)), stored((rows, heads * head_size)), stored((heads, rows))],
        scratch_shapes=[pltpu.VMEM((Q, Q), F32)],
        compiler_params=params(),
        cost_estimate=FREE,
        name="scores",
    )(inputs, grad_out, write_proj, read_proj, log_decay, *after)


def grads_kernel(
    scale, sel, x_ref, gw_ref, w_ref, r_ref, ld_ref, gint_ref, dot_ref, part_ref, tot_ref, near_ref, far_ref, pay_ref, *rest
):
    gi_ref, gd_ref = rest[-2:]
    lanes = x_ref.shape[1]
    width = w_ref.shape[1]
    size = lanes // GROUP
    near_forward = sel[0] == 0
    f_car = jnp.where(near_forward, near_ref[...], far_ref[...])
    b_car = jnp.where(near_forward, far_ref[...], near_ref[...])
    f_next = tot_ref[0:1, :] * f_car + part_ref[0:width, :]
    b_next = tot_ref[8:9, :] * b_car + part_ref[width : 2 * width, :]
    state_in, grad_end = (f_car, f_next), (b_next, b_car)
    last = pay_ref[2 * width : 2 * width + 1, :] * f_car + pay_ref[0:width, :]
    after = (f_next, last)
    owner = iota((16, lanes), 0) == iota((16, lanes), 1) // size
    ones = owner.astype(F32).astype(BF16)
    onward = (iota((Q, Q), 0) >= iota((Q, Q), 1)).astype(F32).astype(BF16)
    for b in range(2):
        at = slice(b * Q, (b + 1) * Q)
        decay_out = spread_decays(running_of(ld_ref[:, at]), size)[1]
        out_inter = dot(r_ref[at, :], state_in[b].astype(BF16))
        grad_full = gint_ref[at, :] + dot(w_ref[at, :], grad_end[b].astype(BF16)) * decay_out
        gi_ref[at, :] = grad_full.astype(BF16)
        high, low = split_two(gw_ref[0, at, :].astype(F32) * out_inter - x_ref[at, :].astype(F32) * grad_full)
        change = dot_t(ones, high.astype(BF16)) + dot_t(ones, low.astype(BF16))
        cross = jnp.sum(after[b] * grad_end[b], axis=0, keepdims=True)
        crossing = jnp.sum(jnp.where(owner[0:GROUP], cross, 0.0), axis=1, keepdims=True)
        gd_ref[:, at] = (times_ones(change[0:GROUP] + dot_ref[:, at], onward) + crossing) * scale


def grads(sel, k, data, gint, dots, state, carried, scale, head_size, held=(), after=()):
    inputs, _, write_proj, read_proj, log_decay = data
    pay, wg, part, tot = state
    rows, width = write_proj.shape
    heads = log_decay.shape[0]
    lanes = GROUP * head_size
    wide = pl.BlockSpec((rows, lanes), lambda i, s: (0, s[6 + k]))
    decays = pl.BlockSpec((GROUP, rows), lambda i, s: (s[6 + k], 0))
    args = [inputs, wg, write_proj, read_proj, log_decay, gint, dots, part, tot, *carried, pay]
    return pl.pallas_call(
        functools.partial(grads_kernel, scale),
        grid_spec=pltpu.PrefetchScalarGridSpec(
            num_scalar_prefetch=1,
            grid=(1,),
            in_specs=[
                wide,
                pl.BlockSpec((1, rows, lanes), lambda i, s: (0, 0, 0)),
                full(write_proj),
                full(read_proj),
                decays,
                wide,
                decays,
            ]
            + [full(a) for a in (part, tot, *carried, pay)]
            + [ANYWHERE] * (len(held) + len(after)),
            out_specs=[wide, decays],
        ),
        out_shape=[stored((rows, heads * head_size), BF16), stored((heads, rows))],
        input_output_aliases={1 + len(args): 0, 2 + len(args): 1} if held else {},
        compiler_params=params(),
        cost_estimate=FREE,
        name="grads",
    )(sel, *args, *held, *after)


def join_kernel(places, sel, *refs):
    count = len(places)
    parts, (read_ref, write_ref, sems) = refs[:count], refs[-3:]
    step = parts[0].shape[0]
    odd = sel[5] % 2

    def copies(*outs):
        moves = []
        for k, (part, (way, back)) in enumerate(zip(parts, places)):
            at = pl.multiple_of((1 - odd if back else odd) * step, step)
            moves.append(pltpu.make_async_copy(part, outs[way].at[pl.ds(at, step), :], sems.at[k]))
        for move in moves:
            move.start()
        for move in moves:
            move.wait()

    pl.when(sel[0] == 0)(lambda: copies(read_ref, write_ref))
    pl.when(sel[0] != 0)(lambda: copies(write_ref, read_ref))


def join(sel, parts, places, shape, held=()):
    count = len(parts)
    return pl.pallas_call(
        functools.partial(join_kernel, places),
        grid_spec=pltpu.PrefetchScalarGridSpec(
            num_scalar_prefetch=1,
            grid=(1,),
            in_specs=[ANYWHERE] * (count + len(held)),
            out_specs=[ANYWHERE] * 2,
            scratch_shapes=[pltpu.SemaphoreType.DMA((count,))],
        ),
        out_shape=[stored(shape)] * 2,
        input_output_aliases={1 + count: 0, 2 + count: 1} if held else {},
        compiler_params=params(),
        cost_estimate=FREE,
        name="join",
    )(sel, *parts, *held)


def swap(values, axis, mask):
    count = lax.axis_size(axis)
    return lax.ppermute(values, axis, [(i, i ^ mask) for i in range(count)])


def scan_over(pay, width, reverse):
    count = lax.axis_size("seq")
    place = lax.axis_index("seq")
    ahead = count - 1 - place if reverse else place
    part = pay[width : 2 * width] if reverse else pay[0:width]
    dec = pay[2 * width : 2 * width + 1]

    def shifted(values, hop):
        route = [(i, i - hop) if reverse else (i, i + hop) for i in range(count)]
        return lax.ppermute(values, "seq", [(a, b) for a, b in route if 0 <= b < count])

    hop = 1
    while hop < count:
        got_part, got_dec = shifted(part, hop), shifted(dec, hop)
        use = ahead >= hop
        part = jnp.where(use, part + dec * got_part, part)
        dec = jnp.where(use, dec * got_dec, dec)
        hop *= 2
    return shifted(part, 1)


def tied(value, *others):
    return lax.optimization_barrier((value, *others))[0]


def local(inputs, grad_out, write_proj, read_proj, log_decay):
    head_count, rows = log_decay.shape
    head_size = inputs.shape[1] // head_count
    width = write_proj.shape[1]
    lanes = GROUP * head_size
    groups = head_count // GROUP
    seq_count, head_parts = lax.axis_size("seq"), lax.axis_size("head")
    scale = (head_size * rows * seq_count) ** (-0.5)
    place = lax.axis_index("seq").astype(jnp.int32)
    core, x, y = place % 2, (place // 2) % 2, (place // 4) % 2
    fast = seq_count == 8 and groups == 2 and head_parts == 4
    order = [core, 1 - core] if fast else [jnp.int32(k) for k in range(groups)]
    ways = [y, 1 - y] if fast else [jnp.int32(0), jnp.int32(1)]
    sel = jnp.stack([*ways, core, x, y, lax.axis_index("head").astype(jnp.int32), *order])
    data = (inputs, grad_out, write_proj, read_proj, log_decay)

    if fast:
        other = states(order[1][None], *data, head_size, False)
        got = swap(other[0], "seq", 1)
        mine = states(order[0][None], *data, head_size, True)
        outs = [shape_of((width + 8, lanes)), shape_of((width, lanes))]
        px, qx = call(chip_kernel, "chip", sel, (mine[0], got), outs)
        rx, sx = swap(px, "seq", 2), swap(qx, "seq", 2)
        early, gint, dots = scores(*data, head_size, (px,))
        near_own, send, pair = carry(0, sel, [rx, px], mine[0], got, (dots,))
        ry = swap(pair, "seq", 4)
        near_got = swap(send, "seq", 1)
        (acc,) = late(0, sel, mine, near_own, early, False, "late_near_mine")
        near_parts = late(0, sel, other, near_got, acc[None], True, "late_near_other")
        near_half = near_parts[0] + swap(near_parts[1], "head", 1)
        near_cross = swap(near_half, "head", 2)
        far_own, send = carry(1, sel, [rx, sx, ry], mine[0], got, (near_half,))
        far_got = swap(send, "seq", 1)
        (acc,) = late(1, sel, mine, far_own, early, False, "late_far_mine")
        far_parts = late(1, sel, other, far_got, acc[None], True, "late_far_other")
        far_arrived = swap(far_parts[1], "head", 1)
        near_sum = near_half + near_cross
        near_rest = swap(near_sum, "head", 1)
        held = grads(sel, 0, data, gint, dots, mine, (near_own, far_own), scale, head_size, (), (far_parts[1],))
        far_half = far_parts[0] + tied(far_arrived, *held)
        far_cross = swap(far_half, "head", 2)
        grad_inputs, grad_decay = grads(
            sel, 1, data, gint, dots, other, (near_got, far_got), scale, head_size, held, (far_half,)
        )
        far_sum = far_half + tied(far_cross, grad_decay)
        far_rest = swap(far_sum, "head", 1)
        held = join(sel, (near_sum, near_rest, far_sum), ((0, 0), (0, 1), (1, 0)), (rows, width))
        grad_read, grad_write = join(sel, (tied(far_rest, *held),), ((1, 1),), (rows, width), held)
        return grad_inputs, grad_write, grad_read, grad_decay

    local_states = [states(k[None], *data, head_size, False) for k in order]
    early, gint, dots = scores(*data, head_size, ())
    carried = [[scan_over(state[0], width, bool(way)) for state in local_states] for way in (0, 1)]
    totals = []
    for way in (0, 1):
        acc = early
        for k, state in enumerate(local_states):
            acc = late(way, sel, state, carried[way][k], acc, False, "late")[0][None]
        totals.append(acc[0])
    held = ()
    for k, state in enumerate(local_states):
        held = grads(sel, k, data, gint, dots, state, (carried[0][k], carried[1][k]), scale, head_size, tuple(held))
    grad_inputs, grad_decay = held
    grad_read, grad_write = lax.psum(tuple(totals), "head")
    return grad_inputs, grad_write, grad_read, grad_decay


def solution(mesh):
    in_specs = (
        P("seq", "head"),
        P("seq", "head"),
        P("seq", None),
        P("seq", None),
        P("head", "seq"),
    )
    out_specs = (P("seq", "head"), P("seq", None), P("seq", None), P("head", "seq"))
    return jax.shard_map(local, mesh=mesh, in_specs=in_specs, out_specs=out_specs, check_vma=False)
```

```python
import functools

import jax
import jax.numpy as jnp
from jax import lax
from jax.experimental import pallas as pl
from jax.experimental.pallas import tpu as pltpu
from jax.sharding import PartitionSpec as P

Q = 256
GROUP = 8
F32 = jnp.float32
BF16 = jnp.bfloat16
ANYWHERE = pl.BlockSpec(memory_space=pl.ANY)
FREE = pl.CostEstimate(flops=1000, bytes_accessed=1000, transcendentals=0)


def dot(a, b):
    return jnp.dot(a, b, preferred_element_type=F32)


def dot_t(a, b):
    return lax.dot_general(a, b, (((1,), (1,)), ((), ())), preferred_element_type=F32)


def iota(shape, dim):
    return lax.broadcasted_iota(jnp.int32, shape, dim)


def split_two(values):
    high = values.astype(BF16).astype(F32)
    return high, values - high


def split_three(values):
    high, rest = split_two(values)
    mid, low = split_two(rest)
    return high, mid, low


def times_ones(values, ones):
    high, mid, low = split_three(values)
    stacked = jnp.concatenate([high, mid, low, jnp.zeros_like(low)], axis=0).astype(BF16)
    out = dot(stacked, ones)
    return out[0:GROUP] + out[GROUP : 2 * GROUP] + out[2 * GROUP : 3 * GROUP]


def running_of(decay_blk):
    upto = (iota((Q, Q), 0) <= iota((Q, Q), 1)).astype(BF16)
    return times_ones(decay_blk, upto)


def spread_decays(running, head_size):
    lanes = GROUP * head_size
    total = running[:, Q - 1 : Q]
    parts = split_two(jnp.exp(running)) + split_two(jnp.exp(total - running))
    stacked = jnp.concatenate(parts, axis=0).T.astype(BF16)
    row = iota((4 * GROUP, lanes), 0)
    owner = row % GROUP == iota((4 * GROUP, lanes), 1) // head_size
    first = (owner & (row < 2 * GROUP)).astype(F32).astype(BF16)
    second = (owner & (row >= 2 * GROUP)).astype(F32).astype(BF16)
    return dot(stacked, first), dot(stacked, second)


def state_kernel(sel, x_hbm, g_hbm, w_hbm, r_hbm, ld_hbm, *rest):
    outs, (x_ref, g_ref, w_ref, r_ref, ld_ref, pay_ref, wg_ref, part_ref, tot_ref, sems) = rest[:4], rest[4:]
    state_body(sel, (x_hbm, g_hbm, w_hbm, r_hbm, ld_hbm), (x_ref, g_ref, w_ref, r_ref, ld_ref), outs, pay_ref, wg_ref, part_ref, tot_ref, sems)


def loaded_kernel(sel, *refs):
    state_body(sel, None, refs[:5], refs[5:9], *refs[9:])


def state_body(sel, sources, refs, outs, pay_ref, wg_ref, part_ref, tot_ref, sems):
    x_ref, g_ref, w_ref, r_ref, ld_ref = refs
    rows, lanes = x_ref.shape
    width = w_ref.shape[1]
    here = pl.ds(pl.multiple_of(sel[0] * lanes, lanes), lanes)
    group = pl.ds(pl.multiple_of(sel[0] * GROUP, GROUP), GROUP)
    moves = []
    if sources:
        x_hbm, g_hbm, w_hbm, r_hbm, ld_hbm = sources
        pairs = [(ld_hbm.at[group, :], ld_ref), (w_hbm, w_ref), (r_hbm, r_ref)]
        for b in range(2):
            at = pl.ds(b * Q, Q)
            pairs.append((x_hbm.at[at, here], x_ref.at[at, :]))
            pairs.append((g_hbm.at[at, here], g_ref.at[at, :]))
        moves = [pltpu.make_async_copy(src, dst, sems.at[k]) for k, (src, dst) in enumerate(pairs)]
    for move in moves:
        move.start()
    leaving = []

    def leave(src, dst):
        leaving.append(pltpu.make_async_copy(src, dst, sems.at[7 + len(leaving)]))
        leaving[-1].start()

    pay_out, wg_out, part_out, tot_out = outs
    for move in moves[:1]:
        move.wait()
    decays = [spread_decays(running_of(ld_ref[:, b * Q : (b + 1) * Q]), lanes // GROUP) for b in range(2)]
    ends = [decay_in[Q - 1 : Q, :] for decay_in, _ in decays]
    tot_ref[0:8, :] = jnp.broadcast_to(ends[0], (8, lanes))
    tot_ref[8:16, :] = jnp.broadcast_to(ends[1], (8, lanes))
    leave(tot_ref, tot_out)
    for move in moves[1:3]:
        move.wait()
    f_parts, g_parts = [], []
    for b in range(2):
        at = slice(b * Q, (b + 1) * Q)
        decay_in, decay_out = decays[b]
        for move in moves[3 + 2 * b : 4 + 2 * b]:
            move.wait()
        iw = (x_ref[at, :].astype(F32) * decay_out).astype(BF16)
        wg_ref[1, at, :] = iw
        leave(wg_ref.at[1, pl.ds(b * Q, Q), :], wg_out.at[1, pl.ds(b * Q, Q), :])
        f_parts.append(dot(w_ref[at, :].astype(F32).T.astype(BF16), iw))
        for move in moves[4 + 2 * b : 5 + 2 * b]:
            move.wait()
        gw = (g_ref[at, :].astype(F32) * decay_in).astype(BF16)
        wg_ref[0, at, :] = gw
        leave(wg_ref.at[0, pl.ds(b * Q, Q), :], wg_out.at[0, pl.ds(b * Q, Q), :])
        g_parts.append(dot(r_ref[at, :].astype(F32).T.astype(BF16), gw))
    pay_ref[0:width, :] = ends[1] * f_parts[0] + f_parts[1]
    pay_ref[width : 2 * width, :] = ends[0] * g_parts[1] + g_parts[0]
    pay_ref[2 * width : 2 * width + 8, :] = jnp.broadcast_to(ends[0] * ends[1], (8, lanes))
    leave(pay_ref, pay_out)
    part_ref[0:width, :] = f_parts[0]
    part_ref[width : 2 * width, :] = g_parts[1]
    leave(part_ref, part_out)
    for move in leaving:
        move.wait()


def params(limit=32):
    return pltpu.CompilerParams(vmem_limit_bytes=limit * 1024 * 1024)


def shape_of(shape, dtype=F32):
    return jax.ShapeDtypeStruct(shape, dtype)


def stored(shape, dtype=F32):
    return pltpu.HBM(shape, dtype)


def far_off(values):
    return pltpu.with_memory_space_constraint(values, pltpu.HBM)


def states(which, inputs, grad_out, write_proj, read_proj, log_decay, head_size, loaded):
    rows, width = write_proj.shape
    lanes = GROUP * head_size
    shapes = [((2 * width + 8, lanes), F32), ((2, rows, lanes), BF16), ((2 * width, lanes), F32), ((16, lanes), F32)]
    args = (inputs, grad_out, write_proj, read_proj, log_decay)
    buffers = [((rows, lanes), BF16)] * 2 + [((rows, width), BF16)] * 2 + [((GROUP, rows), F32)]
    wide = pl.BlockSpec((rows, lanes), lambda i, s: (0, s[0]))
    return pl.pallas_call(
        loaded_kernel if loaded else state_kernel,
        grid_spec=pltpu.PrefetchScalarGridSpec(
            num_scalar_prefetch=1,
            grid=(1,),
            in_specs=[wide, wide, full(write_proj), full(read_proj), pl.BlockSpec((GROUP, rows), lambda i, s: (s[0], 0))]
            if loaded
            else [pl.BlockSpec(memory_space=pltpu.HBM)] * 5,
            out_specs=[ANYWHERE] * 4,
            scratch_shapes=[
                *[pltpu.VMEM(*a) for a in ([] if loaded else buffers) + shapes],
                pltpu.SemaphoreType.DMA((14,)),
            ],
        ),
        out_shape=[shape_of(*shapes[0]), *[stored(*a) for a in shapes[1:]]],
        compiler_params=params(),
        cost_estimate=FREE,
        name="states",
    )(which, *(args if loaded else map(far_off, args)))


def chip_kernel(sel, mine_ref, got_ref, first_ref, second_ref):
    width = (mine_ref.shape[0] - 8) // 2
    lead = sel[2] == 0
    f_rows, b_rows, d_rows = slice(0, width), slice(width, 2 * width), slice(2 * width, 2 * width + 8)
    dec_mine, dec_got = mine_ref[d_rows, :], got_ref[d_rows, :]
    dec_first = jnp.where(lead, dec_mine, dec_got)[0:1]
    dec_second = jnp.where(lead, dec_got, dec_mine)[0:1]
    f_mine, f_got = mine_ref[f_rows, :], got_ref[f_rows, :]
    b_mine, b_got = mine_ref[b_rows, :], got_ref[b_rows, :]
    forward = dec_second * jnp.where(lead, f_mine, f_got) + jnp.where(lead, f_got, f_mine)
    backward = jnp.where(lead, b_mine, b_got) + dec_first * jnp.where(lead, b_got, b_mine)
    low = sel[4] == 0
    first_ref[f_rows, :] = jnp.where(low, forward, backward)
    first_ref[width : width + 8, :] = dec_mine * dec_got
    second_ref[...] = jnp.where(low, backward, forward)


def full(ref_or_shape):
    shape = ref_or_shape.shape
    return pl.BlockSpec(shape, lambda i, s: (0,) * len(shape))


def call(kernel, name, sel, args, outs, in_specs=None, scratch=(), out_specs=None, after=()):
    skip, count = len(args), len(after)

    def body(s, *refs):
        kernel(s, *refs[:skip], *refs[skip + count :])

    return pl.pallas_call(
        body,
        grid_spec=pltpu.PrefetchScalarGridSpec(
            num_scalar_prefetch=1,
            grid=(1,),
            in_specs=(in_specs or [full(a) for a in args]) + [ANYWHERE] * count,
            out_specs=out_specs or [full(o) for o in outs],
            scratch_shapes=list(scratch),
        ),
        out_shape=list(outs),
        compiler_params=params(),
        cost_estimate=FREE,
        name=name,
    )(sel, *args, *after)


def leave_states(way, sel, entering, mine_ref, got_ref, mine_dec, got_dec, own_ref, send_ref):
    first = sel[way] == sel[2]
    own_ref[...] = jnp.where(first, entering, got_dec[0:1, :] * entering + got_ref[...])
    send_ref[...] = jnp.where(first, mine_dec[0:1, :] * entering + mine_ref[...], entering)


def near_kernel(sel, rx_ref, px_ref, *refs):
    width = rx_ref.shape[0] - 8
    head, tail = slice(0, width), slice(width, width + 1)
    same = sel[3] == sel[4]
    rx, px = rx_ref[head, :], px_ref[head, :]
    leave_states(0, sel, jnp.where(same, jnp.zeros_like(rx), rx), *refs[:-1])
    refs[-1][...] = jnp.where(same, rx_ref[tail, :] * px + rx, px_ref[tail, :] * rx + px)


def far_kernel(sel, rx_ref, sx_ref, ry_ref, *refs):
    width = sx_ref.shape[0]
    ry = ry_ref[...]
    leave_states(1, sel, jnp.where(sel[3] == sel[4], sx_ref[...] + rx_ref[width : width + 1, :] * ry, ry), *refs)


def carry(way, sel, arrived, mine, got, after=()):
    width, lanes = mine.shape[0] // 2 - 4, mine.shape[1]
    part = pl.BlockSpec((width, lanes), lambda i, s: (s[way], 0))
    dec = pl.BlockSpec((8, lanes), lambda i, s: (2 * width // 8, 0))
    return call(
        (near_kernel, far_kernel)[way],
        ("carry_near", "carry_far")[way],
        sel,
        [*arrived, mine, got, mine, got],
        [shape_of((width, lanes))] * (3 - way),
        in_specs=[full(a) for a in arrived] + [part, part, dec, dec],
        after=after,
    )


def late_kernel(way, sel, wg_ref, car_ref, part_ref, tot_ref, acc_ref, out_ref):
    car = car_ref[...]
    onward = tot_ref[0:1, :] * car + part_ref[...]
    forward = sel[way] == 0
    for b in range(2):
        at = slice(b * Q, (b + 1) * Q)
        held = jnp.where(forward, onward if b else car, car if b else onward).astype(BF16)
        out_ref[at, :] = acc_ref[0, at, :] + dot_t(wg_ref[0, at, :], held)


def cut_kernel(way, sel, wg_ref, car_ref, part_ref, tot_ref, acc_ref, keep_ref, send_ref, total):
    late_kernel(way, sel, wg_ref, car_ref, part_ref, tot_ref, acc_ref, total)
    step = keep_ref.shape[0]
    odd = sel[5] % 2
    keep_ref[...] = total[pl.ds(pl.multiple_of(odd * step, step), step), :]
    send_ref[...] = total[pl.ds(pl.multiple_of((1 - odd) * step, step), step), :]


def late(way, sel, state, carried, acc, cut, name):
    _, wg, part, tot = state
    rows = wg.shape[1]
    width, lanes = carried.shape
    both = acc.shape[0] == 2
    outs = [shape_of((rows // 2, width))] * 2 if cut else [shape_of((rows, width))]
    return call(
        functools.partial(cut_kernel if cut else late_kernel, way),
        name,
        sel,
        [wg, carried, part, tot, acc],
        outs,
        in_specs=[
            pl.BlockSpec((1, rows, lanes), lambda i, s: (s[way], 0, 0)),
            full(carried),
            pl.BlockSpec((width, lanes), lambda i, s: (s[way], 0)),
            pl.BlockSpec((8, lanes), lambda i, s: (s[way], 0)),
            pl.BlockSpec((1, rows, width), lambda i, s: (s[way] if both else 0, 0, 0)),
        ],
        scratch=[pltpu.VMEM((rows, width), F32)] if cut else [],
    )


def decay_blocks(running):
    half = Q // 2
    columns = jnp.concatenate([running] * (128 // GROUP), axis=0).T
    keep_top = iota((half, Q), 0) <= iota((half, Q), 1)
    keep_low = iota((half, half), 0) <= iota((half, half), 1)

    def of(h):
        row, col = running[h : h + 1, :], columns[:, h : h + 1]
        top = jnp.exp(jnp.where(keep_top, row - col[0:half], -jnp.inf))
        low = jnp.exp(jnp.where(keep_low, row[:, half:] - col[half:], -jnp.inf))
        return top, low

    return of


def pair_products(x_pair, g_pair):
    half = Q // 2
    lane = iota(x_pair.shape, 1)
    none = jnp.zeros_like(x_pair)
    left = lane < x_pair.shape[1] // 2
    first, second = jnp.where(left, x_pair, none), jnp.where(left, none, x_pair)
    top = dot_t(jnp.concatenate([first[0:half], second[0:half]], axis=0), g_pair)
    low = dot_t(jnp.concatenate([first[half:], second[half:]], axis=0), g_pair[half:])
    return (top[0:half], low[0:half]), (top[half:], low[half:])


def scores_kernel(x_ref, g_ref, w_ref, r_ref, ld_ref, *rest):
    acc_ref, gint_ref, dot_ref, gs_ref = rest[-4:]
    group = pl.program_id(1)
    size = x_ref.shape[1] // GROUP
    half = Q // 2
    decays = decay_blocks(running_of(ld_ref[...]))
    products = dot_t(w_ref[...], r_ref[...])
    left = iota((Q, 2 * size), 1) < size
    gs_top = jnp.zeros((half, Q), F32)
    gs_low = jnp.zeros((half, half), F32)
    sums_top, sums_low = [], []
    for pair in range(GROUP // 2):
        at = slice(pair * 2 * size, (pair + 1) * 2 * size)
        g_pair = g_ref[:, at]
        none = jnp.zeros_like(g_pair)
        top = low = None
        for k, (pairs_top, pairs_low) in enumerate(pair_products(x_ref[:, at], g_pair)):
            decay_top, decay_low = decays(2 * pair + k)
            scaled_top, scaled_low = decay_top * pairs_top, decay_low * pairs_low
            gs_top = gs_top + scaled_top
            gs_low = gs_low + scaled_low
            sums_top.append(jnp.sum(products[0:half] * scaled_top, axis=0, keepdims=True))
            sums_low.append(jnp.sum(products[half:, half:] * scaled_low, axis=0, keepdims=True))
            g_own = jnp.where(left, g_pair, none) if k == 0 else jnp.where(left, none, g_pair)
            part_top = dot((products[0:half] * decay_top).astype(BF16), g_own)
            part_low = dot((products[half:, half:] * decay_low).astype(BF16), g_own[half:])
            top = part_top if top is None else top + part_top
            low = part_low if low is None else low + part_low
        gint_ref[0:half, at] = top
        gint_ref[half:, at] = low
    late_half = jnp.concatenate(sums_low, axis=0)
    dot_ref[...] = jnp.concatenate(sums_top, axis=0) + jnp.concatenate([jnp.zeros_like(late_half), late_half], axis=1)

    @pl.when(group == 0)
    def _():
        gs_ref[0:half, :] = gs_top
        gs_ref[half:, 0:half] = jnp.zeros_like(gs_low)
        gs_ref[half:, half:] = gs_low

    @pl.when(group > 0)
    def _():
        gs_ref[0:half, :] += gs_top
        gs_ref[half:, half:] += gs_low

    @pl.when(group == pl.num_programs(1) - 1)
    def _():
        grad_scores = gs_ref[...]
        acc_ref[0] = dot(grad_scores.T.astype(BF16), w_ref[...])
        acc_ref[1] = dot(grad_scores.astype(BF16), r_ref[...])


def scores(inputs, grad_out, write_proj, read_proj, log_decay, head_size, after):
    rows, width = write_proj.shape
    heads = log_decay.shape[0]
    lanes = GROUP * head_size
    wide = pl.BlockSpec((Q, lanes), lambda b, j: (b, j))
    narrow = pl.BlockSpec((Q, width), lambda b, j: (b, 0))
    return pl.pallas_call(
        scores_kernel,
        grid=(rows // Q, heads // GROUP),
        in_specs=[wide, wide, narrow, narrow, pl.BlockSpec((GROUP, Q), lambda b, j: (j, b))] + [ANYWHERE] * len(after),
        out_specs=[
            pl.BlockSpec((2, Q, width), lambda b, j: (0, b, 0)),
            wide,
            pl.BlockSpec((GROUP, Q), lambda b, j: (j, b)),
        ],
        out_shape=[shape_of((2, rows, width)), stored((rows, heads * head_size)), stored((heads, rows))],
        scratch_shapes=[pltpu.VMEM((Q, Q), F32)],
        compiler_params=params(),
        cost_estimate=FREE,
        name="scores",
    )(inputs, grad_out, write_proj, read_proj, log_decay, *after)


def grads_kernel(
    scale, sel, x_ref, gw_ref, w_ref, r_ref, ld_ref, gint_ref, dot_ref, part_ref, tot_ref, near_ref, far_ref, pay_ref, *rest
):
    gi_ref, gd_ref = rest[-2:]
    lanes = x_ref.shape[1]
    width = w_ref.shape[1]
    size = lanes // GROUP
    near_forward = sel[0] == 0
    f_car = jnp.where(near_forward, near_ref[...], far_ref[...])
    b_car = jnp.where(near_forward, far_ref[...], near_ref[...])
    f_next = tot_ref[0:1, :] * f_car + part_ref[0:width, :]
    b_next = tot_ref[8:9, :] * b_car + part_ref[width : 2 * width, :]
    state_in, grad_end = (f_car, f_next), (b_next, b_car)
    last = pay_ref[2 * width : 2 * width + 1, :] * f_car + pay_ref[0:width, :]
    after = (f_next, last)
    owner = iota((16, lanes), 0) == iota((16, lanes), 1) // size
    ones = owner.astype(F32).astype(BF16)
    onward = (iota((Q, Q), 0) >= iota((Q, Q), 1)).astype(F32).astype(BF16)
    for b in range(2):
        at = slice(b * Q, (b + 1) * Q)
        decay_out = spread_decays(running_of(ld_ref[:, at]), size)[1]
        out_inter = dot(r_ref[at, :], state_in[b].astype(BF16))
        grad_full = gint_ref[at, :] + dot(w_ref[at, :], grad_end[b].astype(BF16)) * decay_out
        gi_ref[at, :] = grad_full.astype(BF16)
        high, low = split_two(gw_ref[0, at, :].astype(F32) * out_inter - x_ref[at, :].astype(F32) * grad_full)
        change = dot_t(ones, high.astype(BF16)) + dot_t(ones, low.astype(BF16))
        cross = jnp.sum(after[b] * grad_end[b], axis=0, keepdims=True)
        crossing = jnp.sum(jnp.where(owner[0:GROUP], cross, 0.0), axis=1, keepdims=True)
        gd_ref[:, at] = (times_ones(change[0:GROUP] + dot_ref[:, at], onward) + crossing) * scale


def grads(sel, k, data, gint, dots, state, carried, scale, head_size, held=(), after=()):
    inputs, _, write_proj, read_proj, log_decay = data
    pay, wg, part, tot = state
    rows, width = write_proj.shape
    heads = log_decay.shape[0]
    lanes = GROUP * head_size
    wide = pl.BlockSpec((rows, lanes), lambda i, s: (0, s[6 + k]))
    decays = pl.BlockSpec((GROUP, rows), lambda i, s: (s[6 + k], 0))
    args = [inputs, wg, write_proj, read_proj, log_decay, gint, dots, part, tot, *carried, pay]
    return pl.pallas_call(
        functools.partial(grads_kernel, scale),
        grid_spec=pltpu.PrefetchScalarGridSpec(
            num_scalar_prefetch=1,
            grid=(1,),
            in_specs=[
                wide,
                pl.BlockSpec((1, rows, lanes), lambda i, s: (0, 0, 0)),
                full(write_proj),
                full(read_proj),
                decays,
                wide,
                decays,
            ]
            + [full(a) for a in (part, tot, *carried, pay)]
            + [ANYWHERE] * (len(held) + len(after)),
            out_specs=[wide, decays],
        ),
        out_shape=[stored((rows, heads * head_size), BF16), stored((heads, rows))],
        input_output_aliases={1 + len(args): 0, 2 + len(args): 1} if held else {},
        compiler_params=params(),
        cost_estimate=FREE,
        name="grads",
    )(sel, *args, *held, *after)


def join_kernel(places, sel, *refs):
    count = len(places)
    parts, (read_ref, write_ref, sems) = refs[:count], refs[-3:]
    step = parts[0].shape[0]
    odd = sel[5] % 2

    def copies(*outs):
        moves = []
        for k, (part, (way, back)) in enumerate(zip(parts, places)):
            at = pl.multiple_of((1 - odd if back else odd) * step, step)
            moves.append(pltpu.make_async_copy(part, outs[way].at[pl.ds(at, step), :], sems.at[k]))
        for move in moves:
            move.start()
        for move in moves:
            move.wait()

    pl.when(sel[0] == 0)(lambda: copies(read_ref, write_ref))
    pl.when(sel[0] != 0)(lambda: copies(write_ref, read_ref))


def join(sel, parts, places, shape, held=()):
    count = len(parts)
    return pl.pallas_call(
        functools.partial(join_kernel, places),
        grid_spec=pltpu.PrefetchScalarGridSpec(
            num_scalar_prefetch=1,
            grid=(1,),
            in_specs=[ANYWHERE] * (count + len(held)),
            out_specs=[ANYWHERE] * 2,
            scratch_shapes=[pltpu.SemaphoreType.DMA((count,))],
        ),
        out_shape=[stored(shape)] * 2,
        input_output_aliases={1 + count: 0, 2 + count: 1} if held else {},
        compiler_params=params(),
        cost_estimate=FREE,
        name="join",
    )(sel, *parts, *held)


def swap(values, axis, mask):
    count = lax.axis_size(axis)
    return lax.ppermute(values, axis, [(i, i ^ mask) for i in range(count)])


def scan_over(pay, width, reverse):
    count = lax.axis_size("seq")
    place = lax.axis_index("seq")
    ahead = count - 1 - place if reverse else place
    part = pay[width : 2 * width] if reverse else pay[0:width]
    dec = pay[2 * width : 2 * width + 1]

    def shifted(values, hop):
        route = [(i, i - hop) if reverse else (i, i + hop) for i in range(count)]
        return lax.ppermute(values, "seq", [(a, b) for a, b in route if 0 <= b < count])

    hop = 1
    while hop < count:
        got_part, got_dec = shifted(part, hop), shifted(dec, hop)
        use = ahead >= hop
        part = jnp.where(use, part + dec * got_part, part)
        dec = jnp.where(use, dec * got_dec, dec)
        hop *= 2
    return shifted(part, 1)


def tied(value, *others):
    return lax.optimization_barrier((value, *others))[0]


def local(inputs, grad_out, write_proj, read_proj, log_decay):
    head_count, rows = log_decay.shape
    head_size = inputs.shape[1] // head_count
    width = write_proj.shape[1]
    lanes = GROUP * head_size
    groups = head_count // GROUP
    seq_count, head_parts = lax.axis_size("seq"), lax.axis_size("head")
    scale = (head_size * rows * seq_count) ** (-0.5)
    place = lax.axis_index("seq").astype(jnp.int32)
    core, x, y = place % 2, (place // 2) % 2, (place // 4) % 2
    fast = seq_count == 8 and groups == 2 and head_parts == 4
    order = [core, 1 - core] if fast else [jnp.int32(k) for k in range(groups)]
    ways = [y, 1 - y] if fast else [jnp.int32(0), jnp.int32(1)]
    sel = jnp.stack([*ways, core, x, y, lax.axis_index("head").astype(jnp.int32), *order])
    data = (inputs, grad_out, write_proj, read_proj, log_decay)

    if fast:
        other = states(order[1][None], *data, head_size, False)
        got = swap(other[0], "seq", 1)
        mine = states(order[0][None], *data, head_size, True)
        outs = [shape_of((width + 8, lanes)), shape_of((width, lanes))]
        px, qx = call(chip_kernel, "chip", sel, (mine[0], got), outs)
        rx, sx = swap(px, "seq", 2), swap(qx, "seq", 2)
        early, gint, dots = scores(*data, head_size, (px,))
        near_own, send, pair = carry(0, sel, [rx, px], mine[0], got, (far_off(gint),))
        ry = swap(pair, "seq", 4)
        near_got = swap(send, "seq", 1)
        (acc,) = late(0, sel, mine, near_own, early, False, "late_near_mine")
        near_parts = late(0, sel, other, near_got, acc[None], True, "late_near_other")
        near_half = near_parts[0] + swap(near_parts[1], "head", 1)
        near_cross = swap(near_half, "head", 2)
        far_own, send = carry(1, sel, [rx, sx, ry], mine[0], got, (near_half,))
        far_got = swap(send, "seq", 1)
        (acc,) = late(1, sel, mine, far_own, early, False, "late_far_mine")
        far_parts = late(1, sel, other, far_got, acc[None], True, "late_far_other")
        far_arrived = swap(far_parts[1], "head", 1)
        near_sum = near_half + near_cross
        near_rest = swap(near_sum, "head", 1)
        held = grads(sel, 0, data, gint, dots, mine, (near_own, far_own), scale, head_size, (), (far_parts[1],))
        far_half = far_parts[0] + tied(far_arrived, *held)
        far_cross = swap(far_half, "head", 2)
        grad_inputs, grad_decay = grads(
            sel, 1, data, gint, dots, other, (near_got, far_got), scale, head_size, held, (far_half,)
        )
        far_sum = far_half + tied(far_cross, grad_decay)
        far_rest = swap(far_sum, "head", 1)
        held = join(sel, (near_sum, near_rest, far_sum), ((0, 0), (0, 1), (1, 0)), (rows, width))
        grad_read, grad_write = join(sel, (tied(far_rest, *held),), ((1, 1),), (rows, width), held)
        return grad_inputs, grad_write, grad_read, grad_decay

    local_states = [states(k[None], *data, head_size, False) for k in order]
    early, gint, dots = scores(*data, head_size, ())
    carried = [[scan_over(state[0], width, bool(way)) for state in local_states] for way in (0, 1)]
    totals = []
    for way in (0, 1):
        acc = early
        for k, state in enumerate(local_states):
            acc = late(way, sel, state, carried[way][k], acc, False, "late")[0][None]
        totals.append(acc[0])
    held = ()
    for k, state in enumerate(local_states):
        held = grads(sel, k, data, gint, dots, state, (carried[0][k], carried[1][k]), scale, head_size, tuple(held))
    grad_inputs, grad_decay = held
    grad_read, grad_write = lax.psum(tuple(totals), "head")
    return grad_inputs, grad_write, grad_read, grad_decay


def solution(mesh):
    in_specs = (
        P("seq", "head"),
        P("seq", "head"),
        P("seq", None),
        P("seq", None),
        P("head", "seq"),
    )
    out_specs = (P("seq", "head"), P("seq", None), P("seq", None), P("head", "seq"))
    return jax.shard_map(local, mesh=mesh, in_specs=in_specs, out_specs=out_specs, check_vma=False)
```

```python
import functools

import jax
import jax.numpy as jnp
from jax import lax
from jax.experimental import pallas as pl
from jax.experimental.pallas import tpu as pltpu
from jax.sharding import PartitionSpec as P

Q = 256
GROUP = 8
F32 = jnp.float32
BF16 = jnp.bfloat16
ANYWHERE = pl.BlockSpec(memory_space=pl.ANY)
FREE = pl.CostEstimate(flops=1000, bytes_accessed=1000, transcendentals=0)


def dot(a, b):
    return jnp.dot(a, b, preferred_element_type=F32)


def dot_t(a, b):
    return lax.dot_general(a, b, (((1,), (1,)), ((), ())), preferred_element_type=F32)


def iota(shape, dim):
    return lax.broadcasted_iota(jnp.int32, shape, dim)


def split_two(values):
    high = values.astype(BF16).astype(F32)
    return high, values - high


def split_three(values):
    high, rest = split_two(values)
    mid, low = split_two(rest)
    return high, mid, low


def times_ones(values, ones):
    high, mid, low = split_three(values)
    stacked = jnp.concatenate([high, mid, low, jnp.zeros_like(low)], axis=0).astype(BF16)
    out = dot(stacked, ones)
    return out[0:GROUP] + out[GROUP : 2 * GROUP] + out[2 * GROUP : 3 * GROUP]


def running_of(decay_blk):
    upto = (iota((Q, Q), 0) <= iota((Q, Q), 1)).astype(BF16)
    return times_ones(decay_blk, upto)


def spread_both(ld_ref, head_size):
    lanes = GROUP * head_size
    upto = (iota((Q, Q), 0) <= iota((Q, Q), 1)).astype(BF16)
    pieces = [split_three(ld_ref[:, b * Q : (b + 1) * Q]) for b in range(2)]
    summed = dot(jnp.concatenate([*pieces[0], *pieces[1], *([jnp.zeros((GROUP, Q), F32)] * 2)], axis=0).astype(BF16), upto)
    stacked = []
    for b in range(2):
        first, second, third = (summed[(3 * b + k) * GROUP : (3 * b + k + 1) * GROUP] for k in range(3))
        running = first + second + third
        stacked += split_two(jnp.exp(running)) + split_two(jnp.exp(running[:, Q - 1 : Q] - running))
    stacked = jnp.concatenate(stacked, axis=0).T.astype(BF16)
    row = iota((8 * GROUP, lanes), 0)
    owner = row % GROUP == iota((8 * GROUP, lanes), 1) // head_size
    masks = [(owner & (row // (2 * GROUP) == k)).astype(F32).astype(BF16) for k in range(4)]
    return [(dot(stacked, masks[2 * b]), dot(stacked, masks[2 * b + 1])) for b in range(2)]


def state_kernel(sel, x_hbm, g_hbm, w_hbm, r_hbm, ld_hbm, *rest):
    outs, (x_ref, g_ref, w_ref, r_ref, ld_ref, pay_ref, wg_ref, part_ref, tot_ref, sems) = rest[:4], rest[4:]
    state_body(sel, (x_hbm, g_hbm, w_hbm, r_hbm, ld_hbm), (x_ref, g_ref, w_ref, r_ref, ld_ref), outs, pay_ref, wg_ref, part_ref, tot_ref, sems)


def loaded_kernel(sel, *refs):
    state_body(sel, None, refs[:5], refs[5:9], *refs[9:])


def state_body(sel, sources, refs, outs, pay_ref, wg_ref, part_ref, tot_ref, sems):
    x_ref, g_ref, w_ref, r_ref, ld_ref = refs
    rows, lanes = x_ref.shape
    width = w_ref.shape[1]
    here = pl.ds(pl.multiple_of(sel[0] * lanes, lanes), lanes)
    group = pl.ds(pl.multiple_of(sel[0] * GROUP, GROUP), GROUP)
    moves = []
    if sources:
        x_hbm, g_hbm, w_hbm, r_hbm, ld_hbm = sources
        pairs = [(ld_hbm.at[group, :], ld_ref), (w_hbm, w_ref), (r_hbm, r_ref)]
        for src, dst in ((x_hbm, x_ref), (g_hbm, g_ref)):
            for b in range(2):
                at = pl.ds(b * Q, Q)
                pairs.append((src.at[at, here], dst.at[at, :]))
        moves = [pltpu.make_async_copy(src, dst, sems.at[k]) for k, (src, dst) in enumerate(pairs)]
    for move in moves:
        move.start()
    leaving = []

    def leave(src, dst):
        leaving.append(pltpu.make_async_copy(src, dst, sems.at[7 + len(leaving)]))
        leaving[-1].start()

    pay_out, wg_out, part_out, tot_out = outs
    for move in moves[:1]:
        move.wait()
    decays = spread_both(ld_ref, lanes // GROUP)
    ends = [decay_in[Q - 1 : Q, :] for decay_in, _ in decays]
    tot_ref[0:8, :] = jnp.broadcast_to(ends[0], (8, lanes))
    tot_ref[8:16, :] = jnp.broadcast_to(ends[1], (8, lanes))
    leave(tot_ref, tot_out)
    for move in moves[1:3]:
        move.wait()
    turned = [[ref[b * Q : (b + 1) * Q, :].astype(F32).T.astype(BF16) for b in range(2)] for ref in (w_ref, r_ref)]
    for way, src in ((1, x_ref), (0, g_ref)):
        parts = []
        for b in range(2):
            at = slice(b * Q, (b + 1) * Q)
            for move in moves[5 - 2 * way + b : 6 - 2 * way + b]:
                move.wait()
            scaled = (src[at, :].astype(F32) * decays[b][way]).astype(BF16)
            wg_ref[way, at, :] = scaled
            leave(wg_ref.at[way, pl.ds(b * Q, Q), :], wg_out.at[way, pl.ds(b * Q, Q), :])
            parts.append(dot(turned[1 - way][b], scaled))
        rows_of = pl.ds((1 - way) * width, width)
        if way:
            pay_ref[rows_of, :] = ends[1] * parts[0] + parts[1]
            leave(pay_ref.at[rows_of, :], pay_out.at[rows_of, :])
        else:
            pay_ref[rows_of, :] = ends[0] * parts[1] + parts[0]
            pay_ref[2 * width : 2 * width + 8, :] = jnp.broadcast_to(ends[0] * ends[1], (8, lanes))
            last = pl.ds(width, width + 8)
            leave(pay_ref.at[last, :], pay_out.at[last, :])
        part_ref[rows_of, :] = parts[1 - way]
        leave(part_ref.at[rows_of, :], part_out.at[rows_of, :])
    for move in leaving:
        move.wait()


def params(limit=32):
    return pltpu.CompilerParams(vmem_limit_bytes=limit * 1024 * 1024)


def shape_of(shape, dtype=F32):
    return jax.ShapeDtypeStruct(shape, dtype)


def stored(shape, dtype=F32):
    return pltpu.HBM(shape, dtype)


def far_off(values):
    return pltpu.with_memory_space_constraint(values, pltpu.HBM)


def states(which, inputs, grad_out, write_proj, read_proj, log_decay, head_size, loaded):
    rows, width = write_proj.shape
    lanes = GROUP * head_size
    shapes = [((2 * width + 8, lanes), F32), ((2, rows, lanes), BF16), ((2 * width, lanes), F32), ((16, lanes), F32)]
    args = (inputs, grad_out, write_proj, read_proj, log_decay)
    buffers = [((rows, lanes), BF16)] * 2 + [((rows, width), BF16)] * 2 + [((GROUP, rows), F32)]
    wide = pl.BlockSpec((rows, lanes), lambda i, s: (0, s[0]))
    return pl.pallas_call(
        loaded_kernel if loaded else state_kernel,
        grid_spec=pltpu.PrefetchScalarGridSpec(
            num_scalar_prefetch=1,
            grid=(1,),
            in_specs=[wide, wide, full(write_proj), full(read_proj), pl.BlockSpec((GROUP, rows), lambda i, s: (s[0], 0))]
            if loaded
            else [pl.BlockSpec(memory_space=pltpu.HBM)] * 5,
            out_specs=[ANYWHERE] * 4,
            scratch_shapes=[
                *[pltpu.VMEM(*a) for a in ([] if loaded else buffers) + shapes],
                pltpu.SemaphoreType.DMA((16,)),
            ],
        ),
        out_shape=[shape_of(*shapes[0]), *[stored(*a) for a in shapes[1:]]],
        compiler_params=params(),
        cost_estimate=FREE,
        name="states",
    )(which, *(args if loaded else map(far_off, args)))


def chip_kernel(sel, mine_ref, got_ref, first_ref, second_ref):
    width = (mine_ref.shape[0] - 8) // 2
    lead = sel[2] == 0
    f_rows, b_rows, d_rows = slice(0, width), slice(width, 2 * width), slice(2 * width, 2 * width + 8)
    dec_mine, dec_got = mine_ref[d_rows, :], got_ref[d_rows, :]
    dec_first = jnp.where(lead, dec_mine, dec_got)[0:1]
    dec_second = jnp.where(lead, dec_got, dec_mine)[0:1]
    f_mine, f_got = mine_ref[f_rows, :], got_ref[f_rows, :]
    b_mine, b_got = mine_ref[b_rows, :], got_ref[b_rows, :]
    forward = dec_second * jnp.where(lead, f_mine, f_got) + jnp.where(lead, f_got, f_mine)
    backward = jnp.where(lead, b_mine, b_got) + dec_first * jnp.where(lead, b_got, b_mine)
    low = sel[4] == 0
    first_ref[f_rows, :] = jnp.where(low, forward, backward)
    first_ref[width : width + 8, :] = dec_mine * dec_got
    second_ref[...] = jnp.where(low, backward, forward)


def full(ref_or_shape):
    shape = ref_or_shape.shape
    return pl.BlockSpec(shape, lambda i, s: (0,) * len(shape))


def call(kernel, name, sel, args, outs, in_specs=None, scratch=(), out_specs=None, after=()):
    skip, count = len(args), len(after)

    def body(s, *refs):
        kernel(s, *refs[:skip], *refs[skip + count :])

    return pl.pallas_call(
        body,
        grid_spec=pltpu.PrefetchScalarGridSpec(
            num_scalar_prefetch=1,
            grid=(1,),
            in_specs=(in_specs or [full(a) for a in args]) + [ANYWHERE] * count,
            out_specs=out_specs or [full(o) for o in outs],
            scratch_shapes=list(scratch),
        ),
        out_shape=list(outs),
        compiler_params=params(),
        cost_estimate=FREE,
        name=name,
    )(sel, *args, *after)


def leave_states(way, sel, entering, mine_ref, got_ref, mine_dec, got_dec, own_ref, send_ref):
    first = sel[way] == sel[2]
    own_ref[...] = jnp.where(first, entering, got_dec[0:1, :] * entering + got_ref[...])
    send_ref[...] = jnp.where(first, mine_dec[0:1, :] * entering + mine_ref[...], entering)


def near_kernel(sel, rx_ref, px_ref, *refs):
    width = rx_ref.shape[0] - 8
    head, tail = slice(0, width), slice(width, width + 1)
    same = sel[3] == sel[4]
    rx, px = rx_ref[head, :], px_ref[head, :]
    leave_states(0, sel, jnp.where(same, jnp.zeros_like(rx), rx), *refs[:-1])
    refs[-1][...] = jnp.where(same, rx_ref[tail, :] * px + rx, px_ref[tail, :] * rx + px)


def far_kernel(sel, rx_ref, sx_ref, ry_ref, *refs):
    width = sx_ref.shape[0]
    ry = ry_ref[...]
    leave_states(1, sel, jnp.where(sel[3] == sel[4], sx_ref[...] + rx_ref[width : width + 1, :] * ry, ry), *refs)


def carry(way, sel, arrived, mine, got, after=()):
    width, lanes = mine.shape[0] // 2 - 4, mine.shape[1]
    part = pl.BlockSpec((width, lanes), lambda i, s: (s[way], 0))
    dec = pl.BlockSpec((8, lanes), lambda i, s: (2 * width // 8, 0))
    return call(
        (near_kernel, far_kernel)[way],
        ("carry_near", "carry_far")[way],
        sel,
        [*arrived, mine, got, mine, got],
        [shape_of((width, lanes))] * (3 - way),
        in_specs=[full(a) for a in arrived] + [part, part, dec, dec],
        after=after,
    )


def late_kernel(way, sel, wg_ref, car_ref, part_ref, tot_ref, acc_ref, out_ref):
    car = car_ref[...]
    onward = tot_ref[0:1, :] * car + part_ref[...]
    forward = sel[way] == 0
    for b in range(2):
        at = slice(b * Q, (b + 1) * Q)
        held = jnp.where(forward, onward if b else car, car if b else onward).astype(BF16)
        out_ref[at, :] = acc_ref[0, at, :] + dot_t(wg_ref[0, at, :], held)


def cut_kernel(way, sel, wg_ref, car_ref, part_ref, tot_ref, acc_ref, keep_ref, send_ref, total):
    late_kernel(way, sel, wg_ref, car_ref, part_ref, tot_ref, acc_ref, total)
    step = keep_ref.shape[0]
    odd = sel[5] % 2
    keep_ref[...] = total[pl.ds(pl.multiple_of(odd * step, step), step), :]
    send_ref[...] = total[pl.ds(pl.multiple_of((1 - odd) * step, step), step), :]


def late(way, sel, state, carried, acc, cut, name):
    _, wg, part, tot = state
    rows = wg.shape[1]
    width, lanes = carried.shape
    both = acc.shape[0] == 2
    outs = [shape_of((rows // 2, width))] * 2 if cut else [shape_of((rows, width))]
    return call(
        functools.partial(cut_kernel if cut else late_kernel, way),
        name,
        sel,
        [wg, carried, part, tot, acc],
        outs,
        in_specs=[
            pl.BlockSpec((1, rows, lanes), lambda i, s: (s[way], 0, 0)),
            full(carried),
            pl.BlockSpec((width, lanes), lambda i, s: (s[way], 0)),
            pl.BlockSpec((8, lanes), lambda i, s: (s[way], 0)),
            pl.BlockSpec((1, rows, width), lambda i, s: (s[way] if both else 0, 0, 0)),
        ],
        scratch=[pltpu.VMEM((rows, width), F32)] if cut else [],
    )


def decay_blocks(running):
    half = Q // 2
    columns = jnp.concatenate([running] * (128 // GROUP), axis=0).T
    keep_top = iota((half, Q), 0) <= iota((half, Q), 1)
    keep_low = iota((half, half), 0) <= iota((half, half), 1)

    def of(h):
        row, col = running[h : h + 1, :], columns[:, h : h + 1]
        top = jnp.exp(jnp.where(keep_top, row - col[0:half], -jnp.inf))
        low = jnp.exp(jnp.where(keep_low, row[:, half:] - col[half:], -jnp.inf))
        return top, low

    return of


def pair_products(x_pair, g_pair):
    half = Q // 2
    lane = iota(x_pair.shape, 1)
    none = jnp.zeros_like(x_pair)
    left = lane < x_pair.shape[1] // 2
    first, second = jnp.where(left, x_pair, none), jnp.where(left, none, x_pair)
    top = dot_t(jnp.concatenate([first[0:half], second[0:half]], axis=0), g_pair)
    low = dot_t(jnp.concatenate([first[half:], second[half:]], axis=0), g_pair[half:])
    return (top[0:half], low[0:half]), (top[half:], low[half:])


def scores_kernel(x_ref, g_ref, w_ref, r_ref, ld_ref, *rest):
    acc_ref, gint_ref, dot_ref, gs_ref = rest[-4:]
    group = pl.program_id(1)
    size = x_ref.shape[1] // GROUP
    half = Q // 2
    decays = decay_blocks(running_of(ld_ref[...]))
    products = dot_t(w_ref[...], r_ref[...])
    left = iota((Q, 2 * size), 1) < size
    gs_top = jnp.zeros((half, Q), F32)
    gs_low = jnp.zeros((half, half), F32)
    sums_top, sums_low = [], []
    for pair in range(GROUP // 2):
        at = slice(pair * 2 * size, (pair + 1) * 2 * size)
        g_pair = g_ref[:, at]
        none = jnp.zeros_like(g_pair)
        top = low = None
        for k, (pairs_top, pairs_low) in enumerate(pair_products(x_ref[:, at], g_pair)):
            decay_top, decay_low = decays(2 * pair + k)
            scaled_top, scaled_low = decay_top * pairs_top, decay_low * pairs_low
            gs_top = gs_top + scaled_top
            gs_low = gs_low + scaled_low
            sums_top.append(jnp.sum(products[0:half] * scaled_top, axis=0, keepdims=True))
            sums_low.append(jnp.sum(products[half:, half:] * scaled_low, axis=0, keepdims=True))
            g_own = jnp.where(left, g_pair, none) if k == 0 else jnp.where(left, none, g_pair)
            part_top = dot((products[0:half] * decay_top).astype(BF16), g_own)
            part_low = dot((products[half:, half:] * decay_low).astype(BF16), g_own[half:])
            top = part_top if top is None else top + part_top
            low = part_low if low is None else low + part_low
        gint_ref[0:half, at] = top
        gint_ref[half:, at] = low
    late_half = jnp.concatenate(sums_low, axis=0)
    dot_ref[...] = jnp.concatenate(sums_top, axis=0) + jnp.concatenate([jnp.zeros_like(late_half), late_half], axis=1)

    @pl.when(group == 0)
    def _():
        gs_ref[0:half, :] = gs_top
        gs_ref[half:, 0:half] = jnp.zeros_like(gs_low)
        gs_ref[half:, half:] = gs_low

    @pl.when(group > 0)
    def _():
        gs_ref[0:half, :] += gs_top
        gs_ref[half:, half:] += gs_low

    @pl.when(group == pl.num_programs(1) - 1)
    def _():
        grad_scores = gs_ref[...]
        acc_ref[0] = dot(grad_scores.T.astype(BF16), w_ref[...])
        acc_ref[1] = dot(grad_scores.astype(BF16), r_ref[...])


def scores(inputs, grad_out, write_proj, read_proj, log_decay, head_size, after):
    rows, width = write_proj.shape
    heads = log_decay.shape[0]
    lanes = GROUP * head_size
    wide = pl.BlockSpec((Q, lanes), lambda b, j: (b, j))
    narrow = pl.BlockSpec((Q, width), lambda b, j: (b, 0))
    return pl.pallas_call(
        scores_kernel,
        grid=(rows // Q, heads // GROUP),
        in_specs=[wide, wide, narrow, narrow, pl.BlockSpec((GROUP, Q), lambda b, j: (j, b))] + [ANYWHERE] * len(after),
        out_specs=[
            pl.BlockSpec((2, Q, width), lambda b, j: (0, b, 0)),
            wide,
            pl.BlockSpec((GROUP, Q), lambda b, j: (j, b)),
        ],
        out_shape=[shape_of((2, rows, width)), stored((rows, heads * head_size)), stored((heads, rows))],
        scratch_shapes=[pltpu.VMEM((Q, Q), F32)],
        compiler_params=params(),
        cost_estimate=FREE,
        name="scores",
    )(inputs, grad_out, write_proj, read_proj, log_decay, *after)


def grads_kernel(
    scale, sel, x_ref, gw_ref, w_ref, r_ref, ld_ref, gint_ref, dot_ref, part_ref, tot_ref, near_ref, far_ref, pay_ref, *rest
):
    gi_ref, gd_ref = rest[-2:]
    lanes = x_ref.shape[1]
    width = w_ref.shape[1]
    size = lanes // GROUP
    near_forward = sel[0] == 0
    f_car = jnp.where(near_forward, near_ref[...], far_ref[...])
    b_car = jnp.where(near_forward, far_ref[...], near_ref[...])
    f_next = tot_ref[0:1, :] * f_car + part_ref[0:width, :]
    b_next = tot_ref[8:9, :] * b_car + part_ref[width : 2 * width, :]
    state_in, grad_end = (f_car, f_next), (b_next, b_car)
    last = pay_ref[2 * width : 2 * width + 1, :] * f_car + pay_ref[0:width, :]
    after = (f_next, last)
    owner = iota((16, lanes), 0) == iota((16, lanes), 1) // size
    ones = owner.astype(F32).astype(BF16)
    onward = (iota((Q, Q), 0) >= iota((Q, Q), 1)).astype(F32).astype(BF16)
    decays = spread_both(ld_ref, size)
    for b in range(2):
        at = slice(b * Q, (b + 1) * Q)
        decay_out = decays[b][1]
        out_inter = dot(r_ref[at, :], state_in[b].astype(BF16))
        grad_full = gint_ref[at, :] + dot(w_ref[at, :], grad_end[b].astype(BF16)) * decay_out
        gi_ref[at, :] = grad_full.astype(BF16)
        high, low = split_two(gw_ref[0, at, :].astype(F32) * out_inter - x_ref[at, :].astype(F32) * grad_full)
        change = dot_t(ones, high.astype(BF16)) + dot_t(ones, low.astype(BF16))
        cross = jnp.sum(after[b] * grad_end[b], axis=0, keepdims=True)
        crossing = jnp.sum(jnp.where(owner[0:GROUP], cross, 0.0), axis=1, keepdims=True)
        gd_ref[:, at] = (times_ones(change[0:GROUP] + dot_ref[:, at], onward) + crossing) * scale


def grads(sel, k, data, gint, dots, state, carried, scale, head_size, held=(), after=()):
    inputs, _, write_proj, read_proj, log_decay = data
    pay, wg, part, tot = state
    rows, width = write_proj.shape
    heads = log_decay.shape[0]
    lanes = GROUP * head_size
    wide = pl.BlockSpec((rows, lanes), lambda i, s: (0, s[6 + k]))
    decays = pl.BlockSpec((GROUP, rows), lambda i, s: (s[6 + k], 0))
    args = [inputs, wg, write_proj, read_proj, log_decay, gint, dots, part, tot, *carried, pay]
    return pl.pallas_call(
        functools.partial(grads_kernel, scale),
        grid_spec=pltpu.PrefetchScalarGridSpec(
            num_scalar_prefetch=1,
            grid=(1,),
            in_specs=[
                wide,
                pl.BlockSpec((1, rows, lanes), lambda i, s: (0, 0, 0)),
                full(write_proj),
                full(read_proj),
                decays,
                wide,
                decays,
            ]
            + [full(a) for a in (part, tot, *carried, pay)]
            + [ANYWHERE] * (len(held) + len(after)),
            out_specs=[wide, decays],
        ),
        out_shape=[stored((rows, heads * head_size), BF16), stored((heads, rows))],
        input_output_aliases={1 + len(args): 0, 2 + len(args): 1} if held else {},
        compiler_params=params(),
        cost_estimate=FREE,
        name="grads",
    )(sel, *args, *held, *after)


def join_kernel(places, sel, *refs):
    count = len(places)
    parts, (read_ref, write_ref, sems) = refs[:count], refs[-3:]
    step = parts[0].shape[0]
    odd = sel[5] % 2

    def copies(*outs):
        moves = []
        for k, (part, (way, back)) in enumerate(zip(parts, places)):
            at = pl.multiple_of((1 - odd if back else odd) * step, step)
            moves.append(pltpu.make_async_copy(part, outs[way].at[pl.ds(at, step), :], sems.at[k]))
        for move in moves:
            move.start()
        for move in moves:
            move.wait()

    pl.when(sel[0] == 0)(lambda: copies(read_ref, write_ref))
    pl.when(sel[0] != 0)(lambda: copies(write_ref, read_ref))


def join(sel, parts, places, shape, held=()):
    count = len(parts)
    return pl.pallas_call(
        functools.partial(join_kernel, places),
        grid_spec=pltpu.PrefetchScalarGridSpec(
            num_scalar_prefetch=1,
            grid=(1,),
            in_specs=[ANYWHERE] * (count + len(held)),
            out_specs=[ANYWHERE] * 2,
            scratch_shapes=[pltpu.SemaphoreType.DMA((count,))],
        ),
        out_shape=[stored(shape)] * 2,
        input_output_aliases={1 + count: 0, 2 + count: 1} if held else {},
        compiler_params=params(),
        cost_estimate=FREE,
        name="join",
    )(sel, *parts, *held)


def swap(values, axis, mask):
    count = lax.axis_size(axis)
    return lax.ppermute(values, axis, [(i, i ^ mask) for i in range(count)])


def scan_over(pay, width, reverse):
    count = lax.axis_size("seq")
    place = lax.axis_index("seq")
    ahead = count - 1 - place if reverse else place
    part = pay[width : 2 * width] if reverse else pay[0:width]
    dec = pay[2 * width : 2 * width + 1]

    def shifted(values, hop):
        route = [(i, i - hop) if reverse else (i, i + hop) for i in range(count)]
        return lax.ppermute(values, "seq", [(a, b) for a, b in route if 0 <= b < count])

    hop = 1
    while hop < count:
        got_part, got_dec = shifted(part, hop), shifted(dec, hop)
        use = ahead >= hop
        part = jnp.where(use, part + dec * got_part, part)
        dec = jnp.where(use, dec * got_dec, dec)
        hop *= 2
    return shifted(part, 1)


def tied(value, *others):
    return lax.optimization_barrier((value, *others))[0]


def local(inputs, grad_out, write_proj, read_proj, log_decay):
    head_count, rows = log_decay.shape
    head_size = inputs.shape[1] // head_count
    width = write_proj.shape[1]
    lanes = GROUP * head_size
    groups = head_count // GROUP
    seq_count, head_parts = lax.axis_size("seq"), lax.axis_size("head")
    scale = (head_size * rows * seq_count) ** (-0.5)
    place = lax.axis_index("seq").astype(jnp.int32)
    core, x, y = place % 2, (place // 2) % 2, (place // 4) % 2
    fast = seq_count == 8 and groups == 2 and head_parts == 4
    order = [core, 1 - core] if fast else [jnp.int32(k) for k in range(groups)]
    ways = [y, 1 - y] if fast else [jnp.int32(0), jnp.int32(1)]
    sel = jnp.stack([*ways, core, x, y, lax.axis_index("head").astype(jnp.int32), *order])
    data = (inputs, grad_out, write_proj, read_proj, log_decay)

    if fast:
        other = states(order[1][None], *data, head_size, False)
        got = swap(other[0], "seq", 1)
        mine = states(order[0][None], *data, head_size, True)
        outs = [shape_of((width + 8, lanes)), shape_of((width, lanes))]
        px, qx = call(chip_kernel, "chip", sel, (mine[0], got), outs)
        rx, sx = swap(px, "seq", 2), swap(qx, "seq", 2)
        early, gint, dots = scores(*data, head_size, (px,))
        near_own, send, pair = carry(0, sel, [rx, px], mine[0], got, (far_off(gint),))
        ry = swap(pair, "seq", 4)
        near_got = swap(send, "seq", 1)
        (acc,) = late(0, sel, mine, near_own, early, False, "late_near_mine")
        near_parts = late(0, sel, other, near_got, acc[None], True, "late_near_other")
        near_half = near_parts[0] + swap(near_parts[1], "head", 1)
        near_cross = swap(near_half, "head", 2)
        far_own, send = carry(1, sel, [rx, sx, ry], mine[0], got, (near_half,))
        far_got = swap(send, "seq", 1)
        (acc,) = late(1, sel, mine, far_own, early, False, "late_far_mine")
        far_parts = late(1, sel, other, far_got, acc[None], True, "late_far_other")
        far_arrived = swap(far_parts[1], "head", 1)
        near_sum = near_half + near_cross
        near_rest = swap(near_sum, "head", 1)
        held = grads(sel, 0, data, gint, dots, mine, (near_own, far_own), scale, head_size, (), (far_parts[1],))
        far_half = far_parts[0] + tied(far_arrived, *held)
        far_cross = swap(far_half, "head", 2)
        grad_inputs, grad_decay = grads(
            sel, 1, data, gint, dots, other, (near_got, far_got), scale, head_size, held, (far_half,)
        )
        far_sum = far_half + tied(far_cross, grad_decay)
        far_rest = swap(far_sum, "head", 1)
        held = join(sel, (near_sum, near_rest, far_sum), ((0, 0), (0, 1), (1, 0)), (rows, width))
        grad_read, grad_write = join(sel, (tied(far_rest, *held),), ((1, 1),), (rows, width), held)
        return grad_inputs, grad_write, grad_read, grad_decay

    local_states = [states(k[None], *data, head_size, False) for k in order]
    early, gint, dots = scores(*data, head_size, ())
    carried = [[scan_over(state[0], width, bool(way)) for state in local_states] for way in (0, 1)]
    totals = []
    for way in (0, 1):
        acc = early
        for k, state in enumerate(local_states):
            acc = late(way, sel, state, carried[way][k], acc, False, "late")[0][None]
        totals.append(acc[0])
    held = ()
    for k, state in enumerate(local_states):
        held = grads(sel, k, data, gint, dots, state, (carried[0][k], carried[1][k]), scale, head_size, tuple(held))
    grad_inputs, grad_decay = held
    grad_read, grad_write = lax.psum(tuple(totals), "head")
    return grad_inputs, grad_write, grad_read, grad_decay


def solution(mesh):
    in_specs = (
        P("seq", "head"),
        P("seq", "head"),
        P("seq", None),
        P("seq", None),
        P("head", "seq"),
    )
    out_specs = (P("seq", "head"), P("seq", None), P("seq", None), P("head", "seq"))
    return jax.shard_map(local, mesh=mesh, in_specs=in_specs, out_specs=out_specs, check_vma=False)
```

```python
import functools

import jax
import jax.numpy as jnp
from jax import lax
from jax.experimental import pallas as pl
from jax.experimental.pallas import tpu as pltpu
from jax.sharding import PartitionSpec as P

Q = 256
GROUP = 8
F32 = jnp.float32
BF16 = jnp.bfloat16
ANYWHERE = pl.BlockSpec(memory_space=pl.ANY)
FREE = pl.CostEstimate(flops=1000, bytes_accessed=1000, transcendentals=0)


def dot(a, b):
    return jnp.dot(a, b, preferred_element_type=F32)


def dot_t(a, b):
    return lax.dot_general(a, b, (((1,), (1,)), ((), ())), preferred_element_type=F32)


def iota(shape, dim):
    return lax.broadcasted_iota(jnp.int32, shape, dim)


def split_two(values):
    high = values.astype(BF16).astype(F32)
    return high, values - high


def split_three(values):
    high, rest = split_two(values)
    mid, low = split_two(rest)
    return high, mid, low


def times_ones(values, ones):
    high, mid, low = split_three(values)
    stacked = jnp.concatenate([high, mid, low, jnp.zeros_like(low)], axis=0).astype(BF16)
    out = dot(stacked, ones)
    return out[0:GROUP] + out[GROUP : 2 * GROUP] + out[2 * GROUP : 3 * GROUP]


def running_of(decay_blk):
    upto = (iota((Q, Q), 0) <= iota((Q, Q), 1)).astype(BF16)
    return times_ones(decay_blk, upto)


def spread_both(ld_ref, head_size):
    lanes = GROUP * head_size
    upto = (iota((Q, Q), 0) <= iota((Q, Q), 1)).astype(BF16)
    pieces = [split_three(ld_ref[:, b * Q : (b + 1) * Q]) for b in range(2)]
    summed = dot(jnp.concatenate([*pieces[0], *pieces[1], *([jnp.zeros((GROUP, Q), F32)] * 2)], axis=0).astype(BF16), upto)
    stacked = []
    for b in range(2):
        first, second, third = (summed[(3 * b + k) * GROUP : (3 * b + k + 1) * GROUP] for k in range(3))
        running = first + second + third
        stacked += split_two(jnp.exp(running)) + split_two(jnp.exp(running[:, Q - 1 : Q] - running))
    stacked = jnp.concatenate(stacked, axis=0).T.astype(BF16)
    row = iota((8 * GROUP, lanes), 0)
    owner = row % GROUP == iota((8 * GROUP, lanes), 1) // head_size
    masks = [(owner & (row // (2 * GROUP) == k)).astype(F32).astype(BF16) for k in range(4)]
    return [(dot(stacked, masks[2 * b]), dot(stacked, masks[2 * b + 1])) for b in range(2)]


def state_kernel(sel, x_hbm, g_hbm, w_hbm, r_hbm, ld_hbm, *rest):
    outs, (x_ref, g_ref, w_ref, r_ref, ld_ref, pay_ref, wg_ref, part_ref, tot_ref, sems) = rest[:4], rest[4:]
    state_body(sel, (x_hbm, g_hbm, w_hbm, r_hbm, ld_hbm), (x_ref, g_ref, w_ref, r_ref, ld_ref), outs, pay_ref, wg_ref, part_ref, tot_ref, sems)


def loaded_kernel(sel, *refs):
    state_body(sel, None, refs[:5], refs[5:9], *refs[9:])


def state_body(sel, sources, refs, outs, pay_ref, wg_ref, part_ref, tot_ref, sems):
    x_ref, g_ref, w_ref, r_ref, ld_ref = refs
    rows, lanes = x_ref.shape
    width = w_ref.shape[1]
    here = pl.ds(pl.multiple_of(sel[0] * lanes, lanes), lanes)
    group = pl.ds(pl.multiple_of(sel[0] * GROUP, GROUP), GROUP)
    moves = []
    if sources:
        x_hbm, g_hbm, w_hbm, r_hbm, ld_hbm = sources
        pairs = [(ld_hbm.at[group, :], ld_ref), (w_hbm, w_ref), (r_hbm, r_ref)]
        for src, dst in ((x_hbm, x_ref), (g_hbm, g_ref)):
            for b in range(2):
                at = pl.ds(b * Q, Q)
                pairs.append((src.at[at, here], dst.at[at, :]))
        moves = [pltpu.make_async_copy(src, dst, sems.at[k]) for k, (src, dst) in enumerate(pairs)]
    for move in moves:
        move.start()
    leaving = []

    def leave(src, dst):
        leaving.append(pltpu.make_async_copy(src, dst, sems.at[7 + len(leaving)]))
        leaving[-1].start()

    pay_out, wg_out, part_out, tot_out = outs
    for move in moves[:1]:
        move.wait()
    decays = spread_both(ld_ref, lanes // GROUP)
    ends = [decay_in[Q - 1 : Q, :] for decay_in, _ in decays]
    tot_ref[0:8, :] = jnp.broadcast_to(ends[0], (8, lanes))
    tot_ref[8:16, :] = jnp.broadcast_to(ends[1], (8, lanes))
    leave(tot_ref, tot_out)
    for move in moves[1:3]:
        move.wait()
    turned = [[ref[b * Q : (b + 1) * Q, :].astype(F32).T.astype(BF16) for b in range(2)] for ref in (w_ref, r_ref)]
    for way, src in ((1, x_ref), (0, g_ref)):
        parts = []
        for b in range(2):
            at = slice(b * Q, (b + 1) * Q)
            for move in moves[5 - 2 * way + b : 6 - 2 * way + b]:
                move.wait()
            scaled = (src[at, :].astype(F32) * decays[b][way]).astype(BF16)
            wg_ref[way, at, :] = scaled
            leave(wg_ref.at[way, pl.ds(b * Q, Q), :], wg_out.at[way, pl.ds(b * Q, Q), :])
            parts.append(dot(turned[1 - way][b], scaled))
        rows_of = pl.ds((1 - way) * width, width)
        if way:
            pay_ref[rows_of, :] = ends[1] * parts[0] + parts[1]
            leave(pay_ref.at[rows_of, :], pay_out.at[rows_of, :])
        else:
            pay_ref[rows_of, :] = ends[0] * parts[1] + parts[0]
            pay_ref[2 * width : 2 * width + 8, :] = jnp.broadcast_to(ends[0] * ends[1], (8, lanes))
            last = pl.ds(width, width + 8)
            leave(pay_ref.at[last, :], pay_out.at[last, :])
        part_ref[rows_of, :] = parts[1 - way]
        leave(part_ref.at[rows_of, :], part_out.at[rows_of, :])
    for move in leaving:
        move.wait()


def params(limit=32):
    return pltpu.CompilerParams(vmem_limit_bytes=limit * 1024 * 1024)


def shape_of(shape, dtype=F32):
    return jax.ShapeDtypeStruct(shape, dtype)


def stored(shape, dtype=F32):
    return pltpu.HBM(shape, dtype)


def far_off(values):
    return pltpu.with_memory_space_constraint(values, pltpu.HBM)


def states(which, inputs, grad_out, write_proj, read_proj, log_decay, head_size, loaded):
    rows, width = write_proj.shape
    lanes = GROUP * head_size
    shapes = [((2 * width + 8, lanes), F32), ((2, rows, lanes), BF16), ((2 * width, lanes), F32), ((16, lanes), F32)]
    args = (inputs, grad_out, write_proj, read_proj, log_decay)
    buffers = [((rows, lanes), BF16)] * 2 + [((rows, width), BF16)] * 2 + [((GROUP, rows), F32)]
    wide = pl.BlockSpec((rows, lanes), lambda i, s: (0, s[0]))
    return pl.pallas_call(
        loaded_kernel if loaded else state_kernel,
        grid_spec=pltpu.PrefetchScalarGridSpec(
            num_scalar_prefetch=1,
            grid=(1,),
            in_specs=[wide, wide, full(write_proj), full(read_proj), pl.BlockSpec((GROUP, rows), lambda i, s: (s[0], 0))]
            if loaded
            else [pl.BlockSpec(memory_space=pltpu.HBM)] * 5,
            out_specs=[ANYWHERE] * 4,
            scratch_shapes=[
                *[pltpu.VMEM(*a) for a in ([] if loaded else buffers) + shapes],
                pltpu.SemaphoreType.DMA((16,)),
            ],
        ),
        out_shape=[shape_of(*shapes[0]), *[stored(*a) for a in shapes[1:]]],
        compiler_params=params(),
        cost_estimate=FREE,
        name="states",
    )(which, *(args if loaded else map(far_off, args)))


def chip_kernel(sel, mine_ref, got_ref, first_ref, second_ref):
    width = (mine_ref.shape[0] - 8) // 2
    lead = sel[2] == 0
    f_rows, b_rows, d_rows = slice(0, width), slice(width, 2 * width), slice(2 * width, 2 * width + 8)
    dec_mine, dec_got = mine_ref[d_rows, :], got_ref[d_rows, :]
    dec_first = jnp.where(lead, dec_mine, dec_got)[0:1]
    dec_second = jnp.where(lead, dec_got, dec_mine)[0:1]
    f_mine, f_got = mine_ref[f_rows, :], got_ref[f_rows, :]
    b_mine, b_got = mine_ref[b_rows, :], got_ref[b_rows, :]
    forward = dec_second * jnp.where(lead, f_mine, f_got) + jnp.where(lead, f_got, f_mine)
    backward = jnp.where(lead, b_mine, b_got) + dec_first * jnp.where(lead, b_got, b_mine)
    low = sel[4] == 0
    first_ref[f_rows, :] = jnp.where(low, forward, backward)
    first_ref[width : width + 8, :] = dec_mine * dec_got
    second_ref[...] = jnp.where(low, backward, forward)


def full(ref_or_shape):
    shape = ref_or_shape.shape
    return pl.BlockSpec(shape, lambda i, s: (0,) * len(shape))


def call(kernel, name, sel, args, outs, in_specs=None, scratch=(), out_specs=None, after=()):
    skip, count = len(args), len(after)

    def body(s, *refs):
        kernel(s, *refs[:skip], *refs[skip + count :])

    return pl.pallas_call(
        body,
        grid_spec=pltpu.PrefetchScalarGridSpec(
            num_scalar_prefetch=1,
            grid=(1,),
            in_specs=(in_specs or [full(a) for a in args]) + [ANYWHERE] * count,
            out_specs=out_specs or [full(o) for o in outs],
            scratch_shapes=list(scratch),
        ),
        out_shape=list(outs),
        compiler_params=params(),
        cost_estimate=FREE,
        name=name,
    )(sel, *args, *after)


def leave_states(way, sel, entering, mine_ref, got_ref, mine_dec, got_dec, own_ref, send_ref):
    first = sel[way] == sel[2]
    own_ref[...] = jnp.where(first, entering, got_dec[0:1, :] * entering + got_ref[...])
    send_ref[...] = jnp.where(first, mine_dec[0:1, :] * entering + mine_ref[...], entering)


def near_kernel(sel, rx_ref, px_ref, *refs):
    width = rx_ref.shape[0] - 8
    head, tail = slice(0, width), slice(width, width + 1)
    same = sel[3] == sel[4]
    rx, px = rx_ref[head, :], px_ref[head, :]
    leave_states(0, sel, jnp.where(same, jnp.zeros_like(rx), rx), *refs[:-1])
    refs[-1][...] = jnp.where(same, rx_ref[tail, :] * px + rx, px_ref[tail, :] * rx + px)


def far_kernel(sel, rx_ref, sx_ref, ry_ref, *refs):
    width = sx_ref.shape[0]
    ry = ry_ref[...]
    leave_states(1, sel, jnp.where(sel[3] == sel[4], sx_ref[...] + rx_ref[width : width + 1, :] * ry, ry), *refs)


def carry(way, sel, arrived, mine, got, after=()):
    width, lanes = mine.shape[0] // 2 - 4, mine.shape[1]
    part = pl.BlockSpec((width, lanes), lambda i, s: (s[way], 0))
    dec = pl.BlockSpec((8, lanes), lambda i, s: (2 * width // 8, 0))
    return call(
        (near_kernel, far_kernel)[way],
        ("carry_near", "carry_far")[way],
        sel,
        [*arrived, mine, got, mine, got],
        [shape_of((width, lanes))] * (3 - way),
        in_specs=[full(a) for a in arrived] + [part, part, dec, dec],
        after=after,
    )


def late_kernel(way, sel, wg_ref, car_ref, part_ref, tot_ref, acc_ref, out_ref):
    car = car_ref[...]
    width = car_ref.shape[0]
    chosen = sel[way]
    part = part_ref[pl.ds(pl.multiple_of(chosen * width, width), width), :]
    onward = tot_ref[pl.ds(pl.multiple_of(chosen * 8, 8), 8), :][0:1] * car + part
    forward = chosen == 0
    of = chosen if acc_ref.shape[0] == 2 else 0
    for b in range(2):
        at = slice(b * Q, (b + 1) * Q)
        held = jnp.where(forward, onward if b else car, car if b else onward).astype(BF16)
        out_ref[at, :] = acc_ref[of, at, :] + dot_t(wg_ref[chosen, at, :], held)


def cut_kernel(way, sel, wg_ref, car_ref, part_ref, tot_ref, acc_ref, keep_ref, send_ref, total):
    late_kernel(way, sel, wg_ref, car_ref, part_ref, tot_ref, acc_ref, total)
    step = keep_ref.shape[0]
    odd = sel[5] % 2
    keep_ref[...] = total[pl.ds(pl.multiple_of(odd * step, step), step), :]
    send_ref[...] = total[pl.ds(pl.multiple_of((1 - odd) * step, step), step), :]


def late(way, sel, state, carried, acc, cut, name):
    _, wg, part, tot = state
    rows = wg.shape[1]
    width = carried.shape[0]
    outs = [shape_of((rows // 2, width))] * 2 if cut else [shape_of((rows, width))]
    here = pl.BlockSpec(memory_space=pltpu.VMEM)
    return pl.pallas_call(
        functools.partial(cut_kernel if cut else late_kernel, way),
        in_specs=[pl.BlockSpec(memory_space=pltpu.SMEM)] + [here] * 5,
        out_specs=[here] * len(outs),
        out_shape=outs,
        scratch_shapes=[pltpu.VMEM((rows, width), F32)] if cut else [],
        compiler_params=params(),
        cost_estimate=FREE,
        name=name,
    )(sel, wg, carried, part, tot, acc)


def both_kernel(way, sel, *refs):
    first, second, (acc_ref, keep_ref, send_ref, total) = refs[:4], refs[4:8], refs[8:]
    chosen = sel[way]
    forward = chosen == 0
    helds = []
    for wg_ref, car_ref, part_ref, tot_ref in (first, second):
        width = car_ref.shape[0]
        car = car_ref[...]
        part = part_ref[pl.ds(pl.multiple_of(chosen * width, width), width), :]
        onward = tot_ref[pl.ds(pl.multiple_of(chosen * 8, 8), 8), :][0:1] * car + part
        helds.append([jnp.where(forward, a, c).astype(BF16) for a, c in ((car, onward), (onward, car))])
    for b in range(2):
        at = slice(b * Q, (b + 1) * Q)
        sums = dot_t(first[0][chosen, at, :], helds[0][b]) + dot_t(second[0][chosen, at, :], helds[1][b])
        total[at, :] = acc_ref[chosen, at, :] + sums
    step = keep_ref.shape[0]
    odd = sel[5] % 2
    keep_ref[...] = total[pl.ds(pl.multiple_of(odd * step, step), step), :]
    send_ref[...] = total[pl.ds(pl.multiple_of((1 - odd) * step, step), step), :]


def late_both(way, sel, mine, own, other, got, acc, name):
    rows, width = acc.shape[1:]
    here = pl.BlockSpec(memory_space=pltpu.VMEM)
    return pl.pallas_call(
        functools.partial(both_kernel, way),
        in_specs=[pl.BlockSpec(memory_space=pltpu.SMEM)] + [here] * 9,
        out_specs=[here] * 2,
        out_shape=[shape_of((rows // 2, width))] * 2,
        scratch_shapes=[pltpu.VMEM((rows, width), F32)],
        compiler_params=params(),
        cost_estimate=FREE,
        name=name,
    )(sel, mine[1], own, *mine[2:], other[1], got, *other[2:], acc)


def decay_blocks(running):
    half = Q // 2
    columns = jnp.concatenate([running] * (128 // GROUP), axis=0).T
    keep_top = iota((half, Q), 0) <= iota((half, Q), 1)
    keep_low = iota((half, half), 0) <= iota((half, half), 1)

    def of(h):
        row, col = running[h : h + 1, :], columns[:, h : h + 1]
        top = jnp.exp(jnp.where(keep_top, row - col[0:half], -jnp.inf))
        low = jnp.exp(jnp.where(keep_low, row[:, half:] - col[half:], -jnp.inf))
        return top, low

    return of


def pair_products(x_pair, g_pair):
    half = Q // 2
    lane = iota(x_pair.shape, 1)
    none = jnp.zeros_like(x_pair)
    left = lane < x_pair.shape[1] // 2
    first, second = jnp.where(left, x_pair, none), jnp.where(left, none, x_pair)
    top = dot_t(jnp.concatenate([first[0:half], second[0:half]], axis=0), g_pair)
    low = dot_t(jnp.concatenate([first[half:], second[half:]], axis=0), g_pair[half:])
    return (top[0:half], low[0:half]), (top[half:], low[half:])


def scores_kernel(x_ref, g_ref, w_ref, r_ref, ld_ref, *rest):
    acc_ref, gint_ref, dot_ref, gs_ref = rest[-4:]
    group = pl.program_id(1)
    size = x_ref.shape[1] // GROUP
    half = Q // 2
    decays = decay_blocks(running_of(ld_ref[...]))
    products = dot_t(w_ref[...], r_ref[...])
    left = iota((Q, 2 * size), 1) < size
    gs_top = jnp.zeros((half, Q), F32)
    gs_low = jnp.zeros((half, half), F32)
    sums_top, sums_low = [], []
    for pair in range(GROUP // 2):
        at = slice(pair * 2 * size, (pair + 1) * 2 * size)
        g_pair = g_ref[:, at]
        none = jnp.zeros_like(g_pair)
        top = low = None
        for k, (pairs_top, pairs_low) in enumerate(pair_products(x_ref[:, at], g_pair)):
            decay_top, decay_low = decays(2 * pair + k)
            scaled_top, scaled_low = decay_top * pairs_top, decay_low * pairs_low
            gs_top = gs_top + scaled_top
            gs_low = gs_low + scaled_low
            sums_top.append(jnp.sum(products[0:half] * scaled_top, axis=0, keepdims=True))
            sums_low.append(jnp.sum(products[half:, half:] * scaled_low, axis=0, keepdims=True))
            g_own = jnp.where(left, g_pair, none) if k == 0 else jnp.where(left, none, g_pair)
            part_top = dot((products[0:half] * decay_top).astype(BF16), g_own)
            part_low = dot((products[half:, half:] * decay_low).astype(BF16), g_own[half:])
            top = part_top if top is None else top + part_top
            low = part_low if low is None else low + part_low
        gint_ref[0:half, at] = top
        gint_ref[half:, at] = low
    late_half = jnp.concatenate(sums_low, axis=0)
    dot_ref[...] = jnp.concatenate(sums_top, axis=0) + jnp.concatenate([jnp.zeros_like(late_half), late_half], axis=1)

    @pl.when(group == 0)
    def _():
        gs_ref[0:half, :] = gs_top
        gs_ref[half:, 0:half] = jnp.zeros_like(gs_low)
        gs_ref[half:, half:] = gs_low

    @pl.when(group > 0)
    def _():
        gs_ref[0:half, :] += gs_top
        gs_ref[half:, half:] += gs_low

    @pl.when(group == pl.num_programs(1) - 1)
    def _():
        grad_scores = gs_ref[...]
        acc_ref[0] = dot(grad_scores.T.astype(BF16), w_ref[...])
        acc_ref[1] = dot(grad_scores.astype(BF16), r_ref[...])


def scores(inputs, grad_out, write_proj, read_proj, log_decay, head_size, after):
    rows, width = write_proj.shape
    heads = log_decay.shape[0]
    lanes = GROUP * head_size
    wide = pl.BlockSpec((Q, lanes), lambda b, j: (b, j))
    narrow = pl.BlockSpec((Q, width), lambda b, j: (b, 0))
    return pl.pallas_call(
        scores_kernel,
        grid=(rows // Q, heads // GROUP),
        in_specs=[wide, wide, narrow, narrow, pl.BlockSpec((GROUP, Q), lambda b, j: (j, b))] + [ANYWHERE] * len(after),
        out_specs=[
            pl.BlockSpec((2, Q, width), lambda b, j: (0, b, 0)),
            wide,
            pl.BlockSpec((GROUP, Q), lambda b, j: (j, b)),
        ],
        out_shape=[shape_of((2, rows, width)), stored((rows, heads * head_size)), stored((heads, rows))],
        scratch_shapes=[pltpu.VMEM((Q, Q), F32)],
        compiler_params=params(),
        cost_estimate=FREE,
        name="scores",
    )(inputs, grad_out, write_proj, read_proj, log_decay, *after)


def grads_kernel(
    scale, sel, x_ref, gw_ref, w_ref, r_ref, ld_ref, gint_ref, dot_ref, part_ref, tot_ref, near_ref, far_ref, pay_ref, *rest
):
    gi_ref, gd_ref = rest[-2:]
    lanes = x_ref.shape[1]
    width = w_ref.shape[1]
    size = lanes // GROUP
    near_forward = sel[0] == 0
    f_car = jnp.where(near_forward, near_ref[...], far_ref[...])
    b_car = jnp.where(near_forward, far_ref[...], near_ref[...])
    f_next = tot_ref[0:1, :] * f_car + part_ref[0:width, :]
    b_next = tot_ref[8:9, :] * b_car + part_ref[width : 2 * width, :]
    state_in, grad_end = (f_car, f_next), (b_next, b_car)
    last = pay_ref[2 * width : 2 * width + 1, :] * f_car + pay_ref[0:width, :]
    after = (f_next, last)
    owner = iota((16, lanes), 0) == iota((16, lanes), 1) // size
    ones = owner.astype(F32).astype(BF16)
    onward = (iota((Q, Q), 0) >= iota((Q, Q), 1)).astype(F32).astype(BF16)
    decays = spread_both(ld_ref, size)
    for b in range(2):
        at = slice(b * Q, (b + 1) * Q)
        decay_out = decays[b][1]
        out_inter = dot(r_ref[at, :], state_in[b].astype(BF16))
        grad_full = gint_ref[at, :] + dot(w_ref[at, :], grad_end[b].astype(BF16)) * decay_out
        gi_ref[at, :] = grad_full.astype(BF16)
        high, low = split_two(gw_ref[0, at, :].astype(F32) * out_inter - x_ref[at, :].astype(F32) * grad_full)
        change = dot_t(ones, high.astype(BF16)) + dot_t(ones, low.astype(BF16))
        cross = jnp.sum(after[b] * grad_end[b], axis=0, keepdims=True)
        crossing = jnp.sum(jnp.where(owner[0:GROUP], cross, 0.0), axis=1, keepdims=True)
        gd_ref[:, at] = (times_ones(change[0:GROUP] + dot_ref[:, at], onward) + crossing) * scale


def grads(sel, k, data, gint, dots, state, carried, scale, head_size, held=(), after=()):
    inputs, _, write_proj, read_proj, log_decay = data
    pay, wg, part, tot = state
    rows, width = write_proj.shape
    heads = log_decay.shape[0]
    lanes = GROUP * head_size
    wide = pl.BlockSpec((rows, lanes), lambda i, s: (0, s[6 + k]))
    decays = pl.BlockSpec((GROUP, rows), lambda i, s: (s[6 + k], 0))
    args = [inputs, wg, write_proj, read_proj, log_decay, gint, dots, part, tot, *carried, pay]
    return pl.pallas_call(
        functools.partial(grads_kernel, scale),
        grid_spec=pltpu.PrefetchScalarGridSpec(
            num_scalar_prefetch=1,
            grid=(1,),
            in_specs=[
                wide,
                pl.BlockSpec((1, rows, lanes), lambda i, s: (0, 0, 0)),
                full(write_proj),
                full(read_proj),
                decays,
                wide,
                decays,
            ]
            + [full(a) for a in (part, tot, *carried, pay)]
            + [ANYWHERE] * (len(held) + len(after)),
            out_specs=[wide, decays],
        ),
        out_shape=[stored((rows, heads * head_size), BF16), stored((heads, rows))],
        input_output_aliases={1 + len(args): 0, 2 + len(args): 1} if held else {},
        compiler_params=params(),
        cost_estimate=FREE,
        name="grads",
    )(sel, *args, *held, *after)


def join_kernel(places, sel, *refs):
    count = len(places)
    parts, (read_ref, write_ref, sems) = refs[:count], refs[-3:]
    step = parts[0].shape[0]
    odd = sel[5] % 2

    def copies(*outs):
        moves = []
        for k, (part, (way, back)) in enumerate(zip(parts, places)):
            at = pl.multiple_of((1 - odd if back else odd) * step, step)
            moves.append(pltpu.make_async_copy(part, outs[way].at[pl.ds(at, step), :], sems.at[k]))
        for move in moves:
            move.start()
        for move in moves:
            move.wait()

    pl.when(sel[0] == 0)(lambda: copies(read_ref, write_ref))
    pl.when(sel[0] != 0)(lambda: copies(write_ref, read_ref))


def join(sel, parts, places, shape, held=()):
    count = len(parts)
    return pl.pallas_call(
        functools.partial(join_kernel, places),
        grid_spec=pltpu.PrefetchScalarGridSpec(
            num_scalar_prefetch=1,
            grid=(1,),
            in_specs=[ANYWHERE] * (count + len(held)),
            out_specs=[ANYWHERE] * 2,
            scratch_shapes=[pltpu.SemaphoreType.DMA((count,))],
        ),
        out_shape=[stored(shape)] * 2,
        input_output_aliases={1 + count: 0, 2 + count: 1} if held else {},
        compiler_params=params(),
        cost_estimate=FREE,
        name="join",
    )(sel, *parts, *held)


def swap(values, axis, mask):
    count = lax.axis_size(axis)
    return lax.ppermute(values, axis, [(i, i ^ mask) for i in range(count)])


def scan_over(pay, width, reverse):
    count = lax.axis_size("seq")
    place = lax.axis_index("seq")
    ahead = count - 1 - place if reverse else place
    part = pay[width : 2 * width] if reverse else pay[0:width]
    dec = pay[2 * width : 2 * width + 1]

    def shifted(values, hop):
        route = [(i, i - hop) if reverse else (i, i + hop) for i in range(count)]
        return lax.ppermute(values, "seq", [(a, b) for a, b in route if 0 <= b < count])

    hop = 1
    while hop < count:
        got_part, got_dec = shifted(part, hop), shifted(dec, hop)
        use = ahead >= hop
        part = jnp.where(use, part + dec * got_part, part)
        dec = jnp.where(use, dec * got_dec, dec)
        hop *= 2
    return shifted(part, 1)


def tied(value, *others):
    return lax.optimization_barrier((value, *others))[0]


def local(inputs, grad_out, write_proj, read_proj, log_decay):
    head_count, rows = log_decay.shape
    head_size = inputs.shape[1] // head_count
    width = write_proj.shape[1]
    lanes = GROUP * head_size
    groups = head_count // GROUP
    seq_count, head_parts = lax.axis_size("seq"), lax.axis_size("head")
    scale = (head_size * rows * seq_count) ** (-0.5)
    place = lax.axis_index("seq").astype(jnp.int32)
    core, x, y = place % 2, (place // 2) % 2, (place // 4) % 2
    fast = seq_count == 8 and groups == 2 and head_parts == 4
    order = [core, 1 - core] if fast else [jnp.int32(k) for k in range(groups)]
    ways = [y, 1 - y] if fast else [jnp.int32(0), jnp.int32(1)]
    sel = jnp.stack([*ways, core, x, y, lax.axis_index("head").astype(jnp.int32), *order])
    data = (inputs, grad_out, write_proj, read_proj, log_decay)

    if fast:
        other = states(order[1][None], *data, head_size, False)
        got = swap(other[0], "seq", 1)
        mine = states(order[0][None], *data, head_size, True)
        outs = [shape_of((width + 8, lanes)), shape_of((width, lanes))]
        px, qx = call(chip_kernel, "chip", sel, (mine[0], got), outs)
        rx, sx = swap(px, "seq", 2), swap(qx, "seq", 2)
        early, gint, dots = scores(*data, head_size, (px,))
        near_own, send, pair = carry(0, sel, [rx, px], mine[0], got, (far_off(gint),))
        ry = swap(pair, "seq", 4)
        near_got = swap(send, "seq", 1)
        near_parts = late_both(0, sel, mine, near_own, other, near_got, early, "late_near")
        near_half = near_parts[0] + swap(near_parts[1], "head", 1)
        near_cross = swap(near_half, "head", 2)
        far_own, send = carry(1, sel, [rx, sx, ry], mine[0], got, (near_half,))
        far_got = swap(send, "seq", 1)
        (acc,) = late(1, sel, mine, far_own, early, False, "late_far_mine")
        far_parts = late(1, sel, other, far_got, acc[None], True, "late_far_other")
        far_arrived = swap(far_parts[1], "head", 1)
        near_sum = near_half + near_cross
        near_rest = swap(near_sum, "head", 1)
        held = grads(sel, 0, data, gint, dots, mine, (near_own, far_own), scale, head_size, (), (far_parts[1],))
        far_half = far_parts[0] + tied(far_arrived, *held)
        far_cross = swap(far_half, "head", 2)
        grad_inputs, grad_decay = grads(
            sel, 1, data, gint, dots, other, (near_got, far_got), scale, head_size, held, (far_half,)
        )
        far_sum = far_half + tied(far_cross, grad_decay)
        far_rest = swap(far_sum, "head", 1)
        held = join(sel, (near_sum, near_rest, far_sum), ((0, 0), (0, 1), (1, 0)), (rows, width))
        grad_read, grad_write = join(sel, (tied(far_rest, *held),), ((1, 1),), (rows, width), held)
        return grad_inputs, grad_write, grad_read, grad_decay

    local_states = [states(k[None], *data, head_size, False) for k in order]
    early, gint, dots = scores(*data, head_size, ())
    carried = [[scan_over(state[0], width, bool(way)) for state in local_states] for way in (0, 1)]
    totals = []
    for way in (0, 1):
        acc = early
        for k, state in enumerate(local_states):
            acc = late(way, sel, state, carried[way][k], acc, False, "late")[0][None]
        totals.append(acc[0])
    held = ()
    for k, state in enumerate(local_states):
        held = grads(sel, k, data, gint, dots, state, (carried[0][k], carried[1][k]), scale, head_size, tuple(held))
    grad_inputs, grad_decay = held
    grad_read, grad_write = lax.psum(tuple(totals), "head")
    return grad_inputs, grad_write, grad_read, grad_decay


def solution(mesh):
    in_specs = (
        P("seq", "head"),
        P("seq", "head"),
        P("seq", None),
        P("seq", None),
        P("head", "seq"),
    )
    out_specs = (P("seq", "head"), P("seq", None), P("seq", None), P("head", "seq"))
    return jax.shard_map(local, mesh=mesh, in_specs=in_specs, out_specs=out_specs, check_vma=False)
```
